256 devices in a mesh: section: 8 (over z), expert: 32 (over x, y, core).
Axes of the slice: x: 4, y: 4, z: 8, core: 2. Of those that a mesh axis runs over, the one named last changes fastest.
Arguments:
- thinker_rows: bfloat16 [8192, 3, 2048], P(('expert', 'section')), may hold values from -6 to 6
- codec_prev: bfloat16 [8192, 3, 1024], P(('expert', 'section')), may hold values from -6 to 6
- w_text: bfloat16 [2048, 1024], replicated, may hold values from -0.125 to 0.125
- attn_gain: float32 [1024], replicated, may hold values from 0.25 to 2
- w_q: bfloat16 [1024, 1024], replicated, may hold values from -0.1875 to 0.1875
- key_value_weight: bfloat16 [1024, 512], replicated, may hold values from -0.1875 to 0.1875
- q_gain: float32 [128], replicated, may hold values from 0.25 to 2
- k_gain: float32 [128], replicated, may hold values from 0.25 to 2
- w_o: bfloat16 [1024, 1024], replicated, may hold values from -0.1875 to 0.1875
- cache_k: bfloat16 [8192, 32, 256], P(('expert', 'section')), may hold values from -800 to 800
- value_cache: bfloat16 [8192, 32, 256], P(('expert', 'section')), may hold values from -6 to 6
- lengths: int32 [8192], P(('expert', 'section')), may hold values from 1 to 32
- moe_gain: float32 [1024], replicated, may hold values from 0.25 to 2
- router: bfloat16 [1024, 32], replicated, may hold values from -30 to 30
- routes: int32 [8192, 3, 8], P(('expert', 'section')), may hold values from 0 to 31, all different within a row; in each aligned block of 96 rows (0 to 95, 96 to 191, ..., all dimensions but the last counted through in order) at most 64 rows name the same one
- w_gate_up: bfloat16 [32, 1024, 768], P('expert'), may hold values from -0.1875 to 0.1875
- w_down: bfloat16 [32, 384, 1024], P('expert'), may hold values from -0.3125 to 0.3125
- codes: int32 [8192, 14], P(('expert', 'section')), may hold values from 0 to 2047
- counts: int32 [8192], P(('expert', 'section')), may hold values from 1 to 8
- code_table: bfloat16 [2048, 1024], P(None, 'section'), may hold values from -6 to 6
- conv_weight: float32 [7, 1024], P(None, 'section'), may hold values from -2 to 2
- conv_bias: float32 [1024], P('section'), may hold values from -3 to 3
Outputs:
- talker_out: bfloat16 [8192, 3, 1024], P(('expert', 'section'))
- wave_feats: bfloat16 [8192, 8, 1024], P('expert', None, 'section')
The draws below stay inside these ranges and needn't reach their ends.
Inputs may be any that keep to these rules, and one draw needn't show every extreme that they name: `routes`: within the rows of one device (an aligned block of its 32 dialogues' 3 steps), no expert is named more than 64 times, a bound that some block reaches.
All inputs are finite; a program needn't handle non-finite values.
Results may differ from the reference program's by a relative error of at most 0.017.
Values may be sent and summed in bfloat16 or wider, within the bound.
No kernel may reach another device: no remote copies, remote signals or barrier semaphores. Data moves between devices by JAX's collectives and lax.ppermute only.
A program may use at most 128 MiB of HBM per device.

```python
import math
import jax
import jax.numpy as jnp
import numpy as np
from jax import lax

DT = 2048
TALKER_WIDTH = 1024
HEAD_DIMENSION = 128
HQ = 8
KEY_VALUE_HEADS = 2
FFE = 384
C = 1024
CODEBOOK = 2048
KW = 7
DECODE_STEPS = 3
B_DEV = 32
CACHE_POSITIONS = 32
FR = 8
EXPERTS = 32
TOP = 8
CAP = 64
DIALOGUE_TOTAL = 8192
N_SECTION = 8
N_EXPERT = 32


def draw_cache_k(key, part):
    key = jax.random.fold_in(key, 11)
    random_base_key, second_random_key = jax.random.split(key)
    halfway_count = CACHE_POSITIONS // 2
    leading_part = jnp.clip(jax.random.normal(random_base_key, (DIALOGUE_TOTAL, halfway_count, KEY_VALUE_HEADS, HEAD_DIMENSION), jnp.float32), -6.0, 6.0)
    trailing_part = jnp.clip(jax.random.normal(second_random_key, (DIALOGUE_TOTAL, halfway_count, KEY_VALUE_HEADS, HEAD_DIMENSION), jnp.float32), -6.0, 6.0)
    stacked_rows = jnp.stack([leading_part, trailing_part], axis=2)
    return stacked_rows.reshape(DIALOGUE_TOTAL, CACHE_POSITIONS, KEY_VALUE_HEADS * HEAD_DIMENSION).astype(jnp.bfloat16)


def draw_router(key, part):
    key = jax.random.fold_in(key, 23)
    first_key, second_key = jax.random.split(key)
    halfway_count = EXPERTS // 2
    leading_part = jnp.clip(jax.random.normal(first_key, (TALKER_WIDTH, halfway_count), jnp.float32), -6.0, 6.0) / math.sqrt(TALKER_WIDTH)
    trailing_part = jnp.clip(jax.random.normal(second_key, (TALKER_WIDTH, halfway_count), jnp.float32), -6.0, 6.0) / math.sqrt(TALKER_WIDTH)
    stacked_rows = jnp.stack([leading_part, trailing_part], axis=2)
    return stacked_rows.reshape(TALKER_WIDTH, EXPERTS).astype(jnp.bfloat16)


def touch_ends(result, rng, smallest, largest):
    longest = result.shape.index(max(result.shape))
    spots = []
    for shift in (0, 1):
        where = [jax.random.randint(jax.random.fold_in(rng, axis), (), 0, length) for axis, length in enumerate(result.shape)]
        where[longest] = (where[longest] + shift) % result.shape[longest]
        spots.append(tuple(where))
    return result.at[spots[0]].set(smallest).at[spots[1]].set(largest)


def block_levels(key, dims, shards, smallest, high):
    factor_of = 1.0
    for axis_at, shards_of in shards:
        steps = jax.random.uniform(jax.random.fold_in(jax.random.fold_in(key, 6), axis_at), (shards_of,), jnp.float32, smallest / len(shards), high / len(shards))
        factor_of = factor_of * jnp.repeat(jnp.exp(steps), dims[axis_at] // shards_of).reshape((-1,) + (1,) * (len(dims) - 1 - axis_at))
    return factor_of


def deal_out(stream_key, own, number, rows, number_of, top, most, skew):
    ranking = jax.random.permutation(stream_key, number_of)
    crowded, usual = load_shares(number_of, rows * top, most, skew, True), load_shares(number_of, rows * top, most, skew, False)
    places = jnp.arange(number_of)

    def named(sizes, rotation):
        used = int((sizes > 0).sum())
        fixed = max(1, used // 4)
        shifted = fixed + (places - fixed + rotation * (used - fixed)) % max(1, number_of - fixed)
        return jnp.zeros((number_of,), jnp.int32).at[ranking[jnp.where(places < fixed, places, shifted)]].set(jnp.asarray(sizes, jnp.int32))

    sizes = jnp.where(number % 4 == 0, named(crowded, number // 4), named(usual, number - number // 4 - 1))
    mixed = jax.random.permutation(jax.random.fold_in(own, 3), number_of)
    giver, taker = mixed[0:number_of // 2 * 2:2], mixed[1:number_of // 2 * 2:2]
    margin = jnp.minimum(sizes[giver] - 1, most - sizes[taker]) // 2
    margin = jnp.where((giver == ranking[0]) | (taker == ranking[0]) | (sizes[taker] == 0), 0, jnp.maximum(margin, 0))
    shifted = jax.random.randint(jax.random.fold_in(own, 4), (number_of // 2,), 0, 1 << 20) % (margin + 1)
    sizes = sizes.at[giver].add(-shifted).at[taker].add(shifted)
    items = jnp.searchsorted(jnp.cumsum(sizes), jnp.arange(rows * top), side="right").astype(jnp.int32)
    listing = items.reshape(top, rows).T
    listing = listing[jax.random.permutation(jax.random.fold_in(own, 1), rows)]
    rotation = jax.random.randint(jax.random.fold_in(own, 2), (rows, 1), 0, top)
    return jnp.take_along_axis(listing, (jnp.arange(top)[None, :] + rotation) % top, axis=1)


def load_shares(count, total, most, lean, full):
    portions = [(1 << 20) // math.isqrt(grade ** lean) + 1 for grade in range(1, count + 1)]
    largest = most if full else min(most, max(-(-total // count), total * portions[0] // sum(portions)))
    least = 1 if total - largest >= count - 1 else 0
    holding, surplus = [largest] + [least] * (count - 1), total - largest - least * (count - 1)
    while surplus > 0:
        free = [i for i in range(1, count) if holding[i] < largest] or [i for i in range(1, count) if holding[i] < most]
        pool, budget = sum([portions[i] for i in free]), surplus
        for i in free:
            addition = min(most - holding[i], max(1, budget * portions[i] // pool), surplus)
            holding[i] = holding[i] + addition
            surplus = surplus - addition
    return np.array(holding)


def scatter_about(own_key, extent, deviation, bound, cuts=(), kind=jnp.bfloat16):
    result = deviation * jax.random.normal(own_key, extent, jnp.float32)
    if cuts:
        result = result * block_levels(own_key, extent, cuts, -0.22, 0.18)
    return jnp.clip(result, -bound, bound).astype(kind)


def setup_inputs(seed: int = 0) -> dict:
    keys = jax.random.split(jax.random.key(seed), 23)
    thinker_rows = scatter_about(keys[0], (DIALOGUE_TOTAL, DECODE_STEPS, DT), 1.0, 6.0, ((0, 256),))
    codec_prev = scatter_about(keys[1], (DIALOGUE_TOTAL, DECODE_STEPS, TALKER_WIDTH), 1.0, 6.0, ((0, 256),))
    w_text = scatter_about(keys[2], (DT, TALKER_WIDTH), DT ** -0.5, 0.125)
    attn_gain = jnp.clip(jax.random.uniform(keys[3], (TALKER_WIDTH,), jnp.float32, 0.25, 2.0), 0.25, 2.0)
    w_q = scatter_about(keys[4], (TALKER_WIDTH, HQ * HEAD_DIMENSION), TALKER_WIDTH ** -0.5, 0.1875)
    key_value_weight = scatter_about(keys[5], (TALKER_WIDTH, 2 * KEY_VALUE_HEADS * HEAD_DIMENSION), TALKER_WIDTH ** -0.5, 0.1875)
    q_gain = jnp.clip(jax.random.uniform(keys[6], (HEAD_DIMENSION,), jnp.float32, 0.25, 2.0), 0.25, 2.0)
    k_gain = jnp.clip(jax.random.uniform(keys[7], (HEAD_DIMENSION,), jnp.float32, 0.25, 2.0), 0.25, 2.0)
    w_o = scatter_about(keys[8], (HQ * HEAD_DIMENSION, TALKER_WIDTH), (HQ * HEAD_DIMENSION) ** -0.5, 0.1875)
    cache_k = draw_cache_k(jax.random.fold_in(keys[22], 71), 0)
    value_cache = scatter_about(keys[10], (DIALOGUE_TOTAL, CACHE_POSITIONS, KEY_VALUE_HEADS * HEAD_DIMENSION), 1.0, 6.0, ((0, 256),))
    lengths = touch_ends(jax.random.randint(keys[11], (DIALOGUE_TOTAL,), 1, CACHE_POSITIONS + 1), jax.random.fold_in(keys[11], 1), 1, CACHE_POSITIONS).astype(jnp.int32)
    moe_gain = jnp.clip(jax.random.uniform(keys[12], (TALKER_WIDTH,), jnp.float32, 0.25, 2.0), 0.25, 2.0)
    router = draw_router(jax.random.fold_in(keys[22], 71), 0)
    routes_keys = jax.random.split(jax.random.fold_in(keys[14], 1), DIALOGUE_TOTAL * DECODE_STEPS // (B_DEV * DECODE_STEPS))
    routes_turns = jax.random.permutation(jax.random.fold_in(keys[14], 3), DIALOGUE_TOTAL * DECODE_STEPS // (B_DEV * DECODE_STEPS))
    routes = jax.vmap(lambda own, number: deal_out(jax.random.fold_in(keys[14], 2), own, number, B_DEV * DECODE_STEPS, EXPERTS, TOP, CAP, 2))(routes_keys, routes_turns).reshape((DIALOGUE_TOTAL, DECODE_STEPS, TOP))
    w_gate_up = scatter_about(keys[15], (EXPERTS, TALKER_WIDTH, 2 * FFE), TALKER_WIDTH ** -0.5, 0.1875, ((0, 32),))
    w_down = scatter_about(keys[16], (EXPERTS, FFE, TALKER_WIDTH), FFE ** -0.5, 0.3125, ((0, 32),))
    codes = touch_ends(jax.random.randint(keys[17], (DIALOGUE_TOTAL, FR + KW - 1), 0, CODEBOOK), jax.random.fold_in(keys[17], 1), 0, CODEBOOK - 1).astype(jnp.int32)
    counts = touch_ends(jax.random.randint(keys[18], (DIALOGUE_TOTAL,), 1, FR + 1), jax.random.fold_in(keys[18], 1), 1, FR).astype(jnp.int32)
    code_table = scatter_about(keys[19], (CODEBOOK, C), 1.0, 6.0, ((1, 8),))
    conv_weight = scatter_about(keys[20], (KW, C), KW ** -0.5, 2.0, ((1, 8),), jnp.float32)
    conv_bias = scatter_about(keys[21], (C,), 0.5, 3.0, ((0, 8),), jnp.float32)
    return {"thinker_rows": thinker_rows, "codec_prev": codec_prev, "w_text": w_text, "attn_gain": attn_gain, "w_q": w_q, "key_value_weight": key_value_weight, "q_gain": q_gain, "k_gain": k_gain, "w_o": w_o, "cache_k": cache_k, "value_cache": value_cache, "lengths": lengths, "moe_gain": moe_gain, "router": router, "routes": routes, "w_gate_up": w_gate_up, "w_down": w_down, "codes": codes, "counts": counts, "code_table": code_table, "conv_weight": conv_weight, "conv_bias": conv_bias}


epsilon = 1e-06
masked_score = -1e+30

def rms_norm(values, gain_vector):
    mean_square = lax.optimization_barrier(jnp.mean(values * values, axis=-1, keepdims=True))
    return values * lax.rsqrt(mean_square + epsilon) * gain_vector

def widen(values):
    return lax.optimization_barrier(values).astype(jnp.float32)

def attend(queries, new_keys, new_values, cache_k, value_cache, lengths):
    dialog_count, step_count, head_count, head_size = queries.shape
    kv_count = new_keys.shape[2]
    group_size = head_count // kv_count
    context = cache_k.shape[1]
    score_scale = 1.0 / math.sqrt(head_size)
    query_groups = widen(queries).reshape(dialog_count, step_count, kv_count, group_size, head_size)
    cached_keys = cache_k.astype(jnp.float32).reshape(dialog_count, context, kv_count, head_size)
    cached_values = value_cache.astype(jnp.float32).reshape(dialog_count, context, kv_count, head_size)
    fresh_keys = widen(new_keys)
    fresh_values = widen(new_values)
    earlier = jnp.einsum('btgjh,bcgh->btgjc', query_groups, cached_keys) * score_scale
    current = jnp.einsum('btgjh,bugh->btgju', query_groups, fresh_keys) * score_scale
    earlier_ok = (jnp.arange(context)[None, :] < lengths[:, None])[:, None, None, None, :]
    current_ok = (jnp.arange(step_count)[None, :] <= jnp.arange(step_count)[:, None])[None, :, None, None, :]
    earlier = jnp.where(earlier_ok, earlier, masked_score)
    current = jnp.where(current_ok, current, masked_score)
    highest = jnp.maximum(lax.optimization_barrier(jnp.max(earlier, axis=-1, keepdims=True)), lax.optimization_barrier(jnp.max(current, axis=-1, keepdims=True)))
    earlier_exp = jnp.where(earlier_ok, jnp.exp(earlier - highest), 0.0)
    current_exp = jnp.where(current_ok, jnp.exp(current - highest), 0.0)
    summed = lax.optimization_barrier(jnp.sum(earlier_exp, axis=-1, keepdims=True)) + lax.optimization_barrier(jnp.sum(current_exp, axis=-1, keepdims=True))
    earlier_weights = widen((earlier_exp / summed).astype(jnp.bfloat16))
    current_weights = widen((current_exp / summed).astype(jnp.bfloat16))
    attended = jnp.einsum('btgjc,bcgh->btgjh', earlier_weights, cached_values)
    attended = attended + jnp.einsum('btgju,bugh->btgjh', current_weights, fresh_values)
    return attended.reshape(dialog_count * step_count, head_count * head_size)

def reference(thinker_rows, codec_prev, w_text, attn_gain, w_q, key_value_weight, q_gain, k_gain, w_o, cache_k, value_cache, lengths, moe_gain, router, routes, w_gate_up, w_down, codes, counts, code_table, conv_weight, conv_bias):
    row_count = DIALOGUE_TOTAL * DECODE_STEPS
    moved = thinker_rows.reshape(N_EXPERT, N_SECTION, B_DEV, DECODE_STEPS, DT)
    moved = jnp.roll(moved, 1, axis=1).reshape(row_count, DT)
    inputs = jnp.dot(moved, w_text, preferred_element_type=jnp.float32)
    inputs = inputs + codec_prev.reshape(row_count, TALKER_WIDTH).astype(jnp.float32)
    normalized_rows = rms_norm(inputs, attn_gain).astype(jnp.bfloat16)
    queries = jnp.dot(normalized_rows, w_q, preferred_element_type=jnp.float32).reshape(DIALOGUE_TOTAL, DECODE_STEPS, HQ, HEAD_DIMENSION)
    queries = rms_norm(queries, q_gain).astype(jnp.bfloat16)
    key_value_pair = jnp.dot(normalized_rows, key_value_weight, preferred_element_type=jnp.float32).reshape(DIALOGUE_TOTAL, DECODE_STEPS, 2, KEY_VALUE_HEADS, HEAD_DIMENSION)
    new_keys = rms_norm(key_value_pair[:, :, 0], k_gain).astype(jnp.bfloat16)
    new_values = key_value_pair[:, :, 1].astype(jnp.bfloat16)
    attended = attend(queries, new_keys, new_values, cache_k, value_cache, lengths).astype(jnp.bfloat16)
    hidden = inputs + jnp.dot(attended, w_o, preferred_element_type=jnp.float32)
    routed = rms_norm(hidden, moe_gain).astype(jnp.bfloat16)
    logits = jnp.dot(routed, router, preferred_element_type=jnp.float32)
    expert_ids = routes.reshape(row_count, TOP)
    chosen = jnp.take_along_axis(logits, expert_ids, axis=1)
    gate_probs = jax.nn.softmax(chosen, axis=-1)

    def add_expert(carried, expert_slab):
        gate_up, down_proj, expert_index = expert_slab
        gate_up_out = jnp.dot(routed, gate_up, preferred_element_type=jnp.float32)
        activated = (jax.nn.silu(gate_up_out[:, :FFE]) * gate_up_out[:, FFE:]).astype(jnp.bfloat16)
        expert_out = jnp.dot(activated, down_proj, preferred_element_type=jnp.float32).astype(jnp.bfloat16)
        route_weight = lax.optimization_barrier(jnp.sum(jnp.where(expert_ids == expert_index, gate_probs, 0.0), axis=1))
        return (carried + route_weight[:, None] * widen(expert_out), None)
    start = jnp.zeros((row_count, TALKER_WIDTH), jnp.float32)
    expert_mix, _ = lax.scan(add_expert, start, (w_gate_up, w_down, jnp.arange(EXPERTS, dtype=jnp.int32)))
    talker_out = (hidden + expert_mix).astype(jnp.bfloat16).reshape(DIALOGUE_TOTAL, DECODE_STEPS, TALKER_WIDTH)
    frame_window = FR + KW - 1
    frames = jnp.take(code_table, codes, axis=0).astype(jnp.float32)
    live_frames = jnp.arange(frame_window)[None, :] < counts[:, None] + KW - 1
    frames = jnp.where(live_frames[:, :, None], frames, 0.0)
    summed = jnp.zeros((DIALOGUE_TOTAL, FR, C), jnp.float32)
    for offset in range(KW):
        summed = summed + conv_weight[offset] * frames[:, offset:offset + FR]
    finished = (jnp.arange(FR)[None, :] < counts[:, None])[:, :, None]
    wave_feats = jnp.where(finished, jax.nn.silu(summed + conv_bias), 0.0).astype(jnp.bfloat16)
    return (talker_out, wave_feats)
```

```python
import functools
import math

import jax
import jax.numpy as jnp
from jax import lax
from jax.experimental import pallas as pl
from jax.experimental.pallas import tpu as pltpu
from jax.sharding import PartitionSpec as P

epsilon = 1e-06
masked_score = -1e30
BF = jnp.bfloat16
F32 = jnp.float32
MIB = 1024 * 1024
GATE = 128


def vmem():
    return pl.BlockSpec(memory_space=pltpu.VMEM)


def smem():
    return pl.BlockSpec(memory_space=pltpu.SMEM)


def anywhere():
    return pl.BlockSpec(memory_space=pl.ANY)


def dot_t(a, b):
    return lax.dot_general(a, b, (((1,), (1,)), ((), ())), preferred_element_type=F32)


def dot_n(a, b):
    return jnp.dot(a, b, preferred_element_type=F32)


def rms_norm(values, gain):
    mean_square = jnp.mean(values * values, axis=-1, keepdims=True)
    return values * lax.rsqrt(mean_square + epsilon) * gain


def dense_kernel(
    handed,
    codec,
    attn_gain,
    q_gain,
    k_gain,
    moe_gain,
    router_t,
    picks,
    live,
    w_text,
    w_q,
    w_kv,
    w_o,
    cache_k,
    cache_v,
    hidden_out,
    first_out,
    second_out,
    text_buf,
    q_buf,
    kv_buf,
    o_buf,
    ck_buf,
    cv_buf,
    att,
    sems,
):
    steps, dialogs, wide = handed.shape
    rows = steps * dialogs
    width = text_buf.shape[1]
    head = q_gain.shape[1]
    heads = q_buf.shape[1] // head
    kv_heads = kv_buf.shape[1] // (2 * head)
    group = heads // kv_heads
    context = cache_k.shape[0] // dialogs
    parts = 4
    span = wide // parts

    def text_copy(i):
        place = pl.ds(i * span, span)
        return pltpu.make_async_copy(w_text.at[place], text_buf.at[place], sems.at[i])

    copies = [text_copy(i) for i in range(parts)]
    for i, (source, target) in enumerate(
        ((w_q, q_buf), (w_kv, kv_buf), (cache_k, ck_buf), (cache_v, cv_buf), (w_o, o_buf))
    ):
        copies.append(pltpu.make_async_copy(source, target, sems.at[parts + i]))
    for copy in copies:
        copy.start()

    inputs = codec[...].reshape(rows, width).astype(F32)
    for i in range(parts):
        copies[i].wait()
        block = handed[:, :, i * span : (i + 1) * span].reshape(rows, span)
        inputs = inputs + dot_n(block, text_buf[i * span : (i + 1) * span, :])
    normed = rms_norm(inputs, attn_gain[...]).astype(BF)
    copies[parts].wait()
    q_all = dot_n(normed, q_buf[...])
    copies[parts + 1].wait()
    kv = dot_n(normed, kv_buf[...])
    queries = [rms_norm(q_all[:, h * head : (h + 1) * head], q_gain[...]) for h in range(heads)]
    keys = [
        rms_norm(kv[:, n * head : (n + 1) * head], k_gain[...]).astype(BF) for n in range(kv_heads)
    ]
    values = [
        kv[:, (kv_heads + n) * head : (kv_heads + n + 1) * head].astype(BF)
        for n in range(kv_heads)
    ]
    copies[parts + 2].wait()
    copies[parts + 3].wait()

    bunch = 8
    q_rows = group * steps * bunch
    span_c = bunch * context
    row = lax.broadcasted_iota(jnp.int32, (q_rows, span_c), 0)
    col = lax.broadcasted_iota(jnp.int32, (q_rows, span_c), 1)
    same = (row % bunch) == (col // context)
    row_n = lax.broadcasted_iota(jnp.int32, (q_rows, rows), 0)
    col_n = lax.broadcasted_iota(jnp.int32, (q_rows, rows), 1)
    causal = (col_n // dialogs) <= ((row_n // bunch) % steps)
    scale = 1.0 / math.sqrt(head)
    for g in range(dialogs // bunch):
        ok_c = same & (live[:, g * span_c : (g + 1) * span_c] > 0)
        ok_n = causal & ((col_n % dialogs) == (row_n % bunch + g * bunch))
        for n in range(kv_heads):
            pieces = [
                queries[n * group + j][t * dialogs + g * bunch : t * dialogs + (g + 1) * bunch]
                for j in range(group)
                for t in range(steps)
            ]
            q = jnp.concatenate(pieces, axis=0).astype(BF)
            old_k = ck_buf[g * span_c : (g + 1) * span_c, n * head : (n + 1) * head]
            old_v = cv_buf[g * span_c : (g + 1) * span_c, n * head : (n + 1) * head]
            s_c = jnp.where(ok_c, dot_t(q, old_k) * scale, masked_score)
            s_n = jnp.where(ok_n, dot_t(q, keys[n]) * scale, masked_score)
            top = jnp.maximum(
                jnp.max(s_c, axis=-1, keepdims=True), jnp.max(s_n, axis=-1, keepdims=True)
            )
            e_c = jnp.where(ok_c, jnp.exp(s_c - top), 0.0)
            e_n = jnp.where(ok_n, jnp.exp(s_n - top), 0.0)
            total = jnp.sum(e_c, axis=-1, keepdims=True) + jnp.sum(e_n, axis=-1, keepdims=True)
            out = dot_n((e_c / total).astype(BF), old_v) + dot_n(
                (e_n / total).astype(BF), values[n]
            )
            for j in range(group):
                for t in range(steps):
                    at = (j * steps + t) * bunch
                    h = n * group + j
                    att[
                        t * dialogs + g * bunch : t * dialogs + (g + 1) * bunch,
                        h * head : (h + 1) * head,
                    ] = out[at : at + bunch]

    copies[parts + 4].wait()
    hidden = inputs + dot_n(att[...].astype(BF), o_buf[...])
    hidden_out[...] = hidden
    routed = rms_norm(hidden, moe_gain[...]).astype(BF)
    experts = router_t.shape[0]
    logits = dot_t(router_t[...], routed)
    expert_id = lax.broadcasted_iota(jnp.int32, (experts, rows), 0)
    chosen = expert_id == picks[0:1, :]
    for k in range(1, picks.shape[0]):
        chosen = chosen | (expert_id == picks[k : k + 1, :])
    logits = jnp.where(chosen, logits, masked_score)
    raised = jnp.where(chosen, jnp.exp(logits - jnp.max(logits, axis=0, keepdims=True)), 0.0)
    gate = raised / jnp.sum(raised, axis=0, keepdims=True)
    high = gate.astype(BF).astype(F32)
    low = gate - high
    flat = jnp.concatenate([high, low, jnp.zeros((GATE - 2 * experts, rows), F32)], axis=0)
    flat = jnp.concatenate([flat, jnp.zeros((GATE, GATE - rows), F32)], axis=1)
    columns = jnp.transpose(flat)[:rows].astype(BF)
    half = rows // 2
    first_out[:, :width] = routed[:half]
    second_out[:, :width] = routed[half:]
    first_out[:, width:] = columns[:half]
    second_out[:, width:] = columns[half:]


def dense(handed, codec, gains, router_t, picks, live, weights, caches):
    steps, dialogs, wide = handed.shape
    rows = steps * dialogs
    w_text, w_q, w_kv, w_o = weights
    width = w_text.shape[1]
    sent = jax.ShapeDtypeStruct((rows // 2, width + GATE), BF)
    scratch = [pltpu.VMEM(w.shape, w.dtype) for w in (w_text, w_q, w_kv, w_o) + tuple(caches)]
    return pl.pallas_call(
        dense_kernel,
        out_shape=(jax.ShapeDtypeStruct((rows, width), F32), sent, sent),
        in_specs=[vmem()] * 9 + [anywhere()] * 6,
        out_specs=(vmem(), vmem(), vmem()),
        scratch_shapes=scratch
        + [pltpu.VMEM((rows, w_o.shape[0]), F32), pltpu.SemaphoreType.DMA((9,))],
        compiler_params=pltpu.CompilerParams(vmem_limit_bytes=56 * MIB),
        cost_estimate=pl.CostEstimate(
            flops=10 * rows * width * width, bytes_accessed=11 * MIB, transcendentals=400000
        ),
        name="dense",
    )(handed, codec, *gains, router_t, picks, live, w_text, w_q, w_kv, w_o, *caches)


def expert_kernel(count, tiles, ids, *refs):
    ins = refs[:count]
    gu_a, down_a, gu_b, down_b = refs[count : count + 4]
    outs = refs[count + 4 : 2 * count + 4]
    gu_buf, down_buf, sems = refs[2 * count + 4 :]
    width = down_a.shape[1]
    inner = down_a.shape[0]
    copies = [
        pltpu.make_async_copy(source, target, sems.at[i])
        for i, (source, target) in enumerate(
            (
                (gu_a, gu_buf.at[0]),
                (down_a, down_buf.at[0]),
                (gu_b, gu_buf.at[1]),
                (down_b, down_buf.at[1]),
            )
        )
    ]
    for copy in copies:
        copy.start()
    for at, members in enumerate(tiles):
        x = jnp.concatenate([ins[m][:, :width] for m in members], axis=0)
        gates = jnp.concatenate([ins[m][:, width:] for m in members], axis=0).astype(F32)
        lane = lax.broadcasted_iota(jnp.int32, gates.shape, 1)
        total = None
        for e in range(2):
            mine = (lane == ids[e]) | (lane == ids[e] + ids[2])
            gate = jnp.sum(jnp.where(mine, gates, 0.0), axis=1, keepdims=True)
            if at == 0:
                copies[2 * e].wait()
            gu = dot_n(x, gu_buf[e])
            g = gu[:, :inner]
            act = ((g / (1.0 + jnp.exp(-g))) * gu[:, inner:]).astype(BF)
            if at == 0:
                copies[2 * e + 1].wait()
            out = dot_n(act, down_buf[e]) * gate
            total = out if total is None else total + out
        total = total.astype(BF)
        place = 0
        for m in members:
            size = ins[m].shape[0]
            outs[m][...] = total[place : place + size]
            place += size


def run_experts(arrays, tiles, ids, weights, name):
    count = len(arrays)
    width = weights[1].shape[1]
    inner = weights[1].shape[0]
    rows = sum(a.shape[0] for a in arrays)
    return pl.pallas_call(
        functools.partial(expert_kernel, count, tiles),
        out_shape=tuple(jax.ShapeDtypeStruct((a.shape[0], width), BF) for a in arrays),
        in_specs=[smem()] + [vmem()] * count + [anywhere()] * 4,
        out_specs=tuple(vmem() for _ in arrays),
        scratch_shapes=[
            pltpu.VMEM((2, width, 2 * inner), BF),
            pltpu.VMEM((2, inner, width), BF),
            pltpu.SemaphoreType.DMA((4,)),
        ],
        compiler_params=pltpu.CompilerParams(vmem_limit_bytes=30 * MIB),
        cost_estimate=pl.CostEstimate(
            flops=2 * rows * 6 * inner * width,
            bytes_accessed=4 * rows * width + 12 * inner * width,
            transcendentals=rows * 2 * inner,
        ),
        name=name,
    )(ids, *arrays, *weights)


def add_kernel(near_a, far_a, near_b, far_b, near_c, far_c, near_d, far_d, *outs):
    groups = ((near_a, far_a, 0), (near_b, far_b, 1), (near_c, far_c, 0), (near_d, far_d, 1))
    for (near, far, upper), out in zip(groups, outs):
        half = far.shape[0]
        added, kept = pl.ds(upper * half, half), pl.ds((1 - upper) * half, half)
        out[kept, :] = near[kept, :]
        out[added, :] = (near[added, :].astype(F32) + far[...].astype(F32)).astype(BF)


def add_far(pairs):
    args = [a for pair in pairs for a in pair]
    shape = jax.ShapeDtypeStruct(pairs[0][0].shape, BF)
    return pl.pallas_call(
        add_kernel,
        out_shape=(shape,) * 4,
        in_specs=[vmem()] * 8,
        out_specs=(vmem(),) * 4,
        compiler_params=pltpu.CompilerParams(vmem_limit_bytes=16 * MIB),
        cost_estimate=pl.CostEstimate(flops=2**18, bytes_accessed=4 * MIB, transcendentals=0),
        name="add_far",
    )(*args)


def merge_kernel(hidden, own_a, a1, a2, own_b, b1, b2, kept, *outs):
    size = outs[0].shape[0]
    for side, (own, one, two) in enumerate(((own_a, a1, a2), (own_b, b1, b2))):
        for k in range(4):
            place = slice(k * size, (k + 1) * size)
            total = (
                own[place, :].astype(F32) + one[place, :].astype(F32) + two[place, :].astype(F32)
            )
            if k == 0:
                half = slice(side * size, (side + 1) * size)
                kept[half, :] = hidden[half, :] + total
            else:
                outs[side * 3 + k - 1][...] = total.astype(BF)


def merge(hidden, side_a, side_b):
    width = hidden.shape[1]
    size = side_a[0].shape[0] // 4
    return pl.pallas_call(
        merge_kernel,
        out_shape=(jax.ShapeDtypeStruct(hidden.shape, F32),)
        + (jax.ShapeDtypeStruct((size, width), BF),) * 6,
        in_specs=[vmem()] * 7,
        out_specs=(vmem(),) * 7,
        compiler_params=pltpu.CompilerParams(vmem_limit_bytes=16 * MIB),
        cost_estimate=pl.CostEstimate(flops=2**20, bytes_accessed=4 * MIB, transcendentals=0),
        name="merge",
    )(hidden, *side_a, *side_b)


def finish_kernel(kept, a1, a2, a3, b1, b2, b3, out):
    size = a1.shape[0]
    for side, parts in enumerate(((a1, a2, a3), (b1, b2, b3))):
        half = slice(side * size, (side + 1) * size)
        total = kept[half, :]
        for part in parts:
            total = total + part[...].astype(F32)
        out[half, :] = total.astype(BF)


def finish(kept, parts):
    return pl.pallas_call(
        finish_kernel,
        out_shape=jax.ShapeDtypeStruct(kept.shape, BF),
        in_specs=[vmem()] * 7,
        out_specs=vmem(),
        compiler_params=pltpu.CompilerParams(vmem_limit_bytes=16 * MIB),
        cost_estimate=pl.CostEstimate(flops=2**19, bytes_accessed=2 * MIB, transcendentals=0),
        name="finish",
    )(kept, *parts)


def wave_kernel(window, section, codes, table, taps, bias, out, laid):
    blocks, dialogs, _ = codes.shape
    entries, channels = table.shape
    tap_count = taps.shape[0]
    frames_out = window - tap_count + 1

    def one_block(k, carry):
        block = codes[k]
        count = block[:, window : window + 1]
        entry = lax.broadcasted_iota(jnp.int32, (dialogs, entries), 1)
        hot = []
        for p in range(window):
            code = jnp.where(p < count + tap_count - 1, block[:, p : p + 1], -1)
            hot.append((entry == code).astype(F32).astype(BF))
        frames = dot_n(jnp.concatenate(hot, axis=0), table[...])
        for t in range(frames_out):
            total = jnp.zeros((dialogs, channels), F32)
            for j in range(tap_count):
                at = (t + j) * dialogs
                total = total + taps[j : j + 1, :] * frames[at : at + dialogs]
            total = total + bias[...]
            feats = total / (1.0 + jnp.exp(-total))
            laid[pl.ds(t, dialogs, stride=frames_out), :] = jnp.where(t < count, feats, 0.0)
        owner = lax.rem(section[0] - k + blocks, blocks)
        result = laid[...].astype(BF).reshape(dialogs, frames_out, channels)
        out[pl.ds(owner * dialogs, dialogs)] = result
        return carry

    lax.fori_loop(0, blocks, one_block, 0)


def wave(section, codes, table, taps, bias, window):
    blocks, dialogs, _ = codes.shape
    channels = table.shape[1]
    frames_out = window - taps.shape[0] + 1
    rows = blocks * dialogs
    return pl.pallas_call(
        functools.partial(wave_kernel, window),
        out_shape=jax.ShapeDtypeStruct((rows, frames_out, channels), BF),
        in_specs=[smem()] + [vmem()] * 4,
        out_specs=vmem(),
        scratch_shapes=[pltpu.VMEM((dialogs * frames_out, channels), F32)],
        compiler_params=pltpu.CompilerParams(vmem_limit_bytes=16 * MIB),
        cost_estimate=pl.CostEstimate(
            flops=2 * rows * window * table.shape[0] * channels,
            bytes_accessed=2 * MIB,
            transcendentals=rows * frames_out * channels,
        ),
        name="wave",
    )(section, codes, table, taps, bias)


def chip_sides(total):
    chips = total // 2
    side = math.isqrt(chips)
    return side, chips // side


def hop(array, dx, dy, dc=0):
    total = lax.axis_size("expert")
    nx, ny = chip_sides(total)
    route = []
    for x in range(nx):
        for y in range(ny):
            for c in range(2):
                target = ((x + dx) % nx * ny + (y + dy) % ny) * 2 + (c + dc) % 2
                route.append(((x * ny + y) * 2 + c, target))
    return lax.ppermute(array, "expert", route)


def along(array, distance):
    size = lax.axis_size("section")
    return lax.ppermute(array, "section", [(i, (i + distance) % size) for i in range(size)])


def talker(thinker, codec, weights, gains, router, caches, lengths, routes, w_gate_up, w_down):
    dialogs, steps, _ = thinker.shape
    context = caches[0].shape[1]
    rows = dialogs * steps
    width = codec.shape[2]
    handed = along(jnp.transpose(thinker, (1, 0, 2)), 1)
    gu_a, down_a = w_gate_up[0], w_down[0]
    gu_b, down_b = hop(gu_a, 0, 0, 1), hop(down_a, 0, 0, 1)
    mine = lax.axis_index("expert").astype(jnp.int32)
    ids = jnp.stack([mine, mine + 1 - 2 * (mine % 2), jnp.int32(router.shape[1]), jnp.int32(0)])
    picks = jnp.transpose(routes, (2, 1, 0)).reshape(routes.shape[2], rows)
    live = (jnp.arange(context)[None, :] < lengths[:, None]).astype(F32)
    hidden, first, second = dense(
        handed,
        jnp.transpose(codec, (1, 0, 2)),
        gains,
        jnp.transpose(router),
        picks,
        live.reshape(1, dialogs * context),
        weights,
        [c.reshape(dialogs * context, c.shape[2]) for c in caches],
    )
    expert_weights = (gu_a, down_a, gu_b, down_b)
    a = jnp.concatenate([first, hop(first, 1, 0), hop(first, -1, 0), hop(first, 2, 0)], axis=0)
    b = jnp.concatenate([second, hop(second, 0, 1), hop(second, 0, -1), hop(second, 0, 2)], axis=0)
    a_m, a_p = hop(a, 0, 1), hop(a, 0, -1)
    b_m, b_p = hop(b, 1, 0), hop(b, -1, 0)
    own_a, own_b = run_experts((a, b), ((0, 1),), ids, expert_weights, "experts_own")
    half = a.shape[0] // 2
    a_ft, a_fb = hop(a_m[:half], 0, 1), hop(a_p[half:], 0, -1)
    b_ft, b_fb = hop(b_m[:half], 1, 0), hop(b_p[half:], -1, 0)
    near = run_experts(
        (a_m, a_p, b_m, b_p), ((0, 1), (2, 3)), ids, expert_weights, "experts_near"
    )
    far = run_experts(
        (a_ft, a_fb, b_ft, b_fb), ((0, 1, 2, 3),), ids, expert_weights, "experts_far"
    )
    back = (
        hop(far[0], 0, -1),
        hop(far[1], 0, 1),
        hop(far[2], -1, 0),
        hop(far[3], 1, 0),
    )
    near = add_far(list(zip(near, back)))
    side_a = (own_a, hop(near[0], 0, -1), hop(near[1], 0, 1))
    side_b = (own_b, hop(near[2], -1, 0), hop(near[3], 1, 0))
    kept, *sends = merge(hidden, side_a, side_b)
    received = (
        hop(sends[0], -1, 0),
        hop(sends[1], 1, 0),
        hop(sends[2], 2, 0),
        hop(sends[3], 0, -1),
        hop(sends[4], 0, 1),
        hop(sends[5], 0, 2),
    )
    out = finish(kept, received)
    return jnp.transpose(out.reshape(steps, dialogs, width), (1, 0, 2))


def vocoder(codes, counts, code_table, conv_weight, conv_bias):
    dialogs, window = codes.shape
    held = jnp.concatenate(
        [codes, counts[:, None], jnp.zeros((dialogs, 15 - window), jnp.int32)], axis=1
    )
    held = jnp.transpose(held)[None]
    distance = 1
    while distance < lax.axis_size("section"):
        held = jnp.concatenate([held, along(held, distance)], axis=0)
        distance *= 2
    section = lax.axis_index("section").astype(jnp.int32).reshape(1)
    return wave(
        section,
        jnp.transpose(held, (0, 2, 1)),
        code_table,
        conv_weight,
        conv_bias[None],
        window,
    )


def shards(
    thinker_rows,
    codec_prev,
    w_text,
    attn_gain,
    w_q,
    key_value_weight,
    q_gain,
    k_gain,
    w_o,
    cache_k,
    value_cache,
    lengths,
    moe_gain,
    router,
    routes,
    w_gate_up,
    w_down,
    codes,
    counts,
    code_table,
    conv_weight,
    conv_bias,
):
    talker_out = talker(
        thinker_rows,
        codec_prev,
        (w_text, w_q, key_value_weight, w_o),
        (attn_gain[None], q_gain[None], k_gain[None], moe_gain[None]),
        router,
        (cache_k, value_cache),
        lengths,
        routes,
        w_gate_up,
        w_down,
    )
    wave_feats = vocoder(codes, counts, code_table, conv_weight, conv_bias)
    return (talker_out, wave_feats)


def solution(mesh):
    each = P(("expert", "section"), None, None)
    return jax.shard_map(
        shards,
        mesh=mesh,
        in_specs=(
            each,
            each,
            P(),
            P(),
            P(),
            P(),
            P(),
            P(),
            P(),
            each,
            each,
            P(("expert", "section")),
            P(),
            P(),
            each,
            P("expert", None, None),
            P("expert", None, None),
            P(("expert", "section"), None),
            P(("expert", "section")),
            P(None, "section"),
            P(None, "section"),
            P("section"),
        ),
        out_specs=(each, P("expert", None, "section")),
        check_vma=False,
    )
```

```python
import functools
import math

import jax
import jax.numpy as jnp
from jax import lax
from jax.experimental import pallas as pl
from jax.experimental.pallas import tpu as pltpu
from jax.sharding import PartitionSpec as P

epsilon = 1e-06
masked_score = -1e30
BF = jnp.bfloat16
F32 = jnp.float32
MIB = 1024 * 1024
GATE = 128


def vmem():
    return pl.BlockSpec(memory_space=pltpu.VMEM)


def smem():
    return pl.BlockSpec(memory_space=pltpu.SMEM)


def anywhere():
    return pl.BlockSpec(memory_space=pl.ANY)


def dot_t(a, b):
    return lax.dot_general(a, b, (((1,), (1,)), ((), ())), preferred_element_type=F32)


def dot_n(a, b):
    return jnp.dot(a, b, preferred_element_type=F32)


def rms_norm(values, gain):
    mean_square = jnp.mean(values * values, axis=-1, keepdims=True)
    return values * lax.rsqrt(mean_square + epsilon) * gain


def dense_kernel(
    handed,
    codec,
    attn_gain,
    q_gain,
    k_gain,
    moe_gain,
    router_t,
    picks,
    live,
    w_text,
    w_q,
    w_kv,
    w_o,
    cache_k,
    cache_v,
    _after,
    hidden_out,
    sent_out,
    text_buf,
    q_buf,
    kv_buf,
    o_buf,
    ck_buf,
    cv_buf,
    att,
    sems,
):
    steps, dialogs, wide = handed.shape
    rows = steps * dialogs
    width = text_buf.shape[1]
    head = q_gain.shape[1]
    heads = q_buf.shape[1] // head
    kv_heads = kv_buf.shape[1] // (2 * head)
    group = heads // kv_heads
    context = cache_k.shape[0] // dialogs
    parts = 4
    span = wide // parts

    def text_copy(i):
        place = pl.ds(i * span, span)
        return pltpu.make_async_copy(w_text.at[place], text_buf.at[place], sems.at[i])

    copies = [text_copy(i) for i in range(parts)]
    for i, (source, target) in enumerate(
        ((w_q, q_buf), (w_kv, kv_buf), (cache_k, ck_buf), (cache_v, cv_buf), (w_o, o_buf))
    ):
        copies.append(pltpu.make_async_copy(source, target, sems.at[parts + i]))
    for copy in copies:
        copy.start()

    inputs = codec[...].reshape(rows, width).astype(F32)
    for i in range(parts):
        copies[i].wait()
        block = handed[:, :, i * span : (i + 1) * span].reshape(rows, span)
        inputs = inputs + dot_n(block, text_buf[i * span : (i + 1) * span, :])
    normed = rms_norm(inputs, attn_gain[...]).astype(BF)
    copies[parts].wait()
    q_all = dot_n(normed, q_buf[...])
    copies[parts + 1].wait()
    kv = dot_n(normed, kv_buf[...])
    queries = [rms_norm(q_all[:, h * head : (h + 1) * head], q_gain[...]) for h in range(heads)]
    keys = [
        rms_norm(kv[:, n * head : (n + 1) * head], k_gain[...]).astype(BF) for n in range(kv_heads)
    ]
    values = [
        kv[:, (kv_heads + n) * head : (kv_heads + n + 1) * head].astype(BF)
        for n in range(kv_heads)
    ]
    copies[parts + 2].wait()
    copies[parts + 3].wait()

    bunch = 8
    q_rows = group * steps * bunch
    span_c = bunch * context
    row = lax.broadcasted_iota(jnp.int32, (q_rows, span_c), 0)
    col = lax.broadcasted_iota(jnp.int32, (q_rows, span_c), 1)
    same = (row % bunch) == (col // context)
    row_n = lax.broadcasted_iota(jnp.int32, (q_rows, rows), 0)
    col_n = lax.broadcasted_iota(jnp.int32, (q_rows, rows), 1)
    causal = (col_n // dialogs) <= ((row_n // bunch) % steps)
    scale = 1.0 / math.sqrt(head)
    pairs = [(g, n) for g in range(dialogs // bunch) for n in range(kv_heads)]
    scored = []
    for g, n in pairs:
        pieces = [
            queries[n * group + j][t * dialogs + g * bunch : t * dialogs + (g + 1) * bunch]
            for j in range(group)
            for t in range(steps)
        ]
        q = jnp.concatenate(pieces, axis=0).astype(BF)
        old_k = ck_buf[g * span_c : (g + 1) * span_c, n * head : (n + 1) * head]
        scored.append((dot_t(q, old_k) * scale, dot_t(q, keys[n]) * scale))
    weighted = []
    for (g, n), (s_c, s_n) in zip(pairs, scored):
        ok_c = same & (live[:, g * span_c : (g + 1) * span_c] > 0)
        ok_n = causal & ((col_n % dialogs) == (row_n % bunch + g * bunch))
        s_c = jnp.where(ok_c, s_c, masked_score)
        s_n = jnp.where(ok_n, s_n, masked_score)
        top = jnp.maximum(
            jnp.max(s_c, axis=-1, keepdims=True), jnp.max(s_n, axis=-1, keepdims=True)
        )
        e_c = jnp.where(ok_c, jnp.exp(s_c - top), 0.0)
        e_n = jnp.where(ok_n, jnp.exp(s_n - top), 0.0)
        total = jnp.sum(e_c, axis=-1, keepdims=True) + jnp.sum(e_n, axis=-1, keepdims=True)
        weighted.append(((e_c / total).astype(BF), (e_n / total).astype(BF)))
    for (g, n), (w_c, w_n) in zip(pairs, weighted):
        old_v = cv_buf[g * span_c : (g + 1) * span_c, n * head : (n + 1) * head]
        out = dot_n(w_c, old_v) + dot_n(w_n, values[n])
        for j in range(group):
            for t in range(steps):
                at = (j * steps + t) * bunch
                h = n * group + j
                att[
                    t * dialogs + g * bunch : t * dialogs + (g + 1) * bunch,
                    h * head : (h + 1) * head,
                ] = out[at : at + bunch]

    copies[parts + 4].wait()
    hidden = inputs + dot_n(att[...].astype(BF), o_buf[...])
    hidden_out[...] = hidden
    routed = rms_norm(hidden, moe_gain[...]).astype(BF)
    experts = router_t.shape[0]
    logits = dot_t(router_t[...], routed)
    expert_id = lax.broadcasted_iota(jnp.int32, (experts, rows), 0)
    chosen = expert_id == picks[0:1, :]
    for k in range(1, picks.shape[0]):
        chosen = chosen | (expert_id == picks[k : k + 1, :])
    logits = jnp.where(chosen, logits, masked_score)
    raised = jnp.where(chosen, jnp.exp(logits - jnp.max(logits, axis=0, keepdims=True)), 0.0)
    gate = raised / jnp.sum(raised, axis=0, keepdims=True)
    high = gate.astype(BF).astype(F32)
    low = gate - high
    flat = jnp.concatenate([high, low, jnp.zeros((GATE - 2 * experts, rows), F32)], axis=0)
    flat = jnp.concatenate([flat, jnp.zeros((GATE, GATE - rows), F32)], axis=1)
    columns = jnp.transpose(flat)[:rows].astype(BF)
    sent_out[:, :width] = routed
    sent_out[:, width:] = columns


def dense(handed, codec, gains, router_t, picks, live, weights, caches, after):
    steps, dialogs, wide = handed.shape
    rows = steps * dialogs
    w_text, w_q, w_kv, w_o = weights
    width = w_text.shape[1]
    sent = jax.ShapeDtypeStruct((rows, width + GATE), BF)
    scratch = [pltpu.VMEM(w.shape, w.dtype) for w in (w_text, w_q, w_kv, w_o) + tuple(caches)]
    return pl.pallas_call(
        dense_kernel,
        out_shape=(jax.ShapeDtypeStruct((rows, width), F32), sent),
        in_specs=[vmem()] * 9 + [anywhere()] * 7,
        out_specs=(vmem(), vmem()),
        scratch_shapes=scratch
        + [pltpu.VMEM((rows, w_o.shape[0]), F32), pltpu.SemaphoreType.DMA((9,))],
        compiler_params=pltpu.CompilerParams(vmem_limit_bytes=56 * MIB),
        cost_estimate=pl.CostEstimate(
            flops=10 * rows * width * width, bytes_accessed=11 * MIB, transcendentals=400000
        ),
        name="dense",
    )(handed, codec, *gains, router_t, picks, live, w_text, w_q, w_kv, w_o, *caches, after)


def expert_kernel(count, tiles, ids, *refs):
    ins = refs[:count]
    gu_a, down_a, gu_b, down_b = refs[count : count + 4]
    outs = refs[count + 5 : 2 * count + 5]
    gu_buf, down_buf, sems = refs[2 * count + 5 :]
    width = down_a.shape[1]
    inner = down_a.shape[0]
    copies = [
        pltpu.make_async_copy(source, target, sems.at[i])
        for i, (source, target) in enumerate(
            (
                (gu_a, gu_buf.at[0]),
                (down_a, down_buf.at[0]),
                (gu_b, gu_buf.at[1]),
                (down_b, down_buf.at[1]),
            )
        )
    ]
    for copy in copies:
        copy.start()
    for at, members in enumerate(tiles):
        x = jnp.concatenate([ins[m][:, :width] for m in members], axis=0)
        gates = jnp.concatenate([ins[m][:, width:] for m in members], axis=0).astype(F32)
        lane = lax.broadcasted_iota(jnp.int32, gates.shape, 1)
        total = None
        for e in range(2):
            mine = (lane == ids[e]) | (lane == ids[e] + ids[2])
            gate = jnp.sum(jnp.where(mine, gates, 0.0), axis=1, keepdims=True)
            if at == 0:
                copies[2 * e].wait()
            gu = dot_n(x, gu_buf[e])
            g = gu[:, :inner]
            act = ((g / (1.0 + jnp.exp(-g))) * gu[:, inner:]).astype(BF)
            if at == 0:
                copies[2 * e + 1].wait()
            out = dot_n(act, down_buf[e]) * gate
            total = out if total is None else total + out
        total = total.astype(BF)
        place = 0
        for m in members:
            size = ins[m].shape[0]
            outs[m][...] = total[place : place + size]
            place += size


def run_experts(arrays, tiles, ids, weights, after, name):
    count = len(arrays)
    width = weights[1].shape[1]
    inner = weights[1].shape[0]
    rows = sum(a.shape[0] for a in arrays)
    return pl.pallas_call(
        functools.partial(expert_kernel, count, tiles),
        out_shape=tuple(jax.ShapeDtypeStruct((a.shape[0], width), BF) for a in arrays),
        in_specs=[smem()] + [vmem()] * count + [anywhere()] * 5,
        out_specs=tuple(vmem() for _ in arrays),
        scratch_shapes=[
            pltpu.VMEM((2, width, 2 * inner), BF),
            pltpu.VMEM((2, inner, width), BF),
            pltpu.SemaphoreType.DMA((4,)),
        ],
        compiler_params=pltpu.CompilerParams(vmem_limit_bytes=30 * MIB),
        cost_estimate=pl.CostEstimate(
            flops=2 * rows * 6 * inner * width,
            bytes_accessed=4 * rows * width + 12 * inner * width,
            transcendentals=rows * 2 * inner,
        ),
        name=name,
    )(ids, *arrays, *weights, after)


def join_kernel(*refs):
    *ins, _after, out = refs
    place = 0
    for part in ins:
        out[place : place + part.shape[0], :] = part[...]
        place += part.shape[0]


def join(arrays, after):
    rows = sum(a.shape[0] for a in arrays)
    return pl.pallas_call(
        join_kernel,
        out_shape=jax.ShapeDtypeStruct((rows, arrays[0].shape[1]), arrays[0].dtype),
        in_specs=[vmem()] * len(arrays) + [anywhere()],
        out_specs=vmem(),
        compiler_params=pltpu.CompilerParams(vmem_limit_bytes=16 * MIB),
        cost_estimate=pl.CostEstimate(flops=0, bytes_accessed=2 * MIB, transcendentals=0),
        name="join",
    )(*arrays, after)


def cut_kernel(near_m, near_p, _after, upper, lower):
    half = upper.shape[0]
    upper[...] = near_m[:half, :]
    lower[...] = near_p[half:, :]


def cut(near_m, near_p, after):
    shape = jax.ShapeDtypeStruct((near_m.shape[0] // 2, near_m.shape[1]), near_m.dtype)
    return pl.pallas_call(
        cut_kernel,
        out_shape=(shape,) * 2,
        in_specs=[vmem()] * 2 + [anywhere()],
        out_specs=(vmem(),) * 2,
        compiler_params=pltpu.CompilerParams(vmem_limit_bytes=16 * MIB),
        cost_estimate=pl.CostEstimate(flops=0, bytes_accessed=2 * MIB, transcendentals=0),
        name="cut",
    )(near_m, near_p, after)


def add_kernel(near_m, far_t, near_p, far_b, *outs):
    for near, far, upper, out in ((near_m, far_t, 0, outs[0]), (near_p, far_b, 1, outs[1])):
        half = far.shape[0]
        added, kept = pl.ds(upper * half, half), pl.ds((1 - upper) * half, half)
        out[kept, :] = near[kept, :]
        out[added, :] = (near[added, :].astype(F32) + far[...].astype(F32)).astype(BF)


def add_far(near_m, far_t, near_p, far_b):
    shape = jax.ShapeDtypeStruct(near_m.shape, BF)
    return pl.pallas_call(
        add_kernel,
        out_shape=(shape,) * 2,
        in_specs=[vmem()] * 4,
        out_specs=(vmem(),) * 2,
        compiler_params=pltpu.CompilerParams(vmem_limit_bytes=16 * MIB),
        cost_estimate=pl.CostEstimate(flops=2**18, bytes_accessed=4 * MIB, transcendentals=0),
        name="add_far",
    )(near_m, far_t, near_p, far_b)


def merge_kernel(hidden, own, one, two, _after, kept, *outs):
    size = hidden.shape[0]
    for k in range(1 + len(outs)):
        place = slice(k * size, (k + 1) * size)
        total = own[place, :].astype(F32) + one[place, :].astype(F32) + two[place, :].astype(F32)
        if k == 0:
            kept[...] = hidden[...] + total
        else:
            outs[k - 1][...] = total.astype(BF)


def merge(hidden, own, one, two, after):
    size, width = hidden.shape
    count = own.shape[0] // size
    return pl.pallas_call(
        merge_kernel,
        out_shape=(jax.ShapeDtypeStruct(hidden.shape, F32),)
        + (jax.ShapeDtypeStruct((size, width), BF),) * (count - 1),
        in_specs=[vmem()] * 4 + [anywhere()],
        out_specs=(vmem(),) * count,
        compiler_params=pltpu.CompilerParams(vmem_limit_bytes=16 * MIB),
        cost_estimate=pl.CostEstimate(flops=2**20, bytes_accessed=4 * MIB, transcendentals=0),
        name="merge",
    )(hidden, own, one, two, after)


def finish_kernel(kept, *refs):
    *parts, out = refs
    total = kept[...]
    for part in parts:
        total = total + part[...].astype(F32)
    out[...] = total.astype(BF)


def finish(kept, parts):
    return pl.pallas_call(
        finish_kernel,
        out_shape=jax.ShapeDtypeStruct(kept.shape, BF),
        in_specs=[vmem()] * (1 + len(parts)),
        out_specs=vmem(),
        compiler_params=pltpu.CompilerParams(vmem_limit_bytes=16 * MIB),
        cost_estimate=pl.CostEstimate(flops=2**19, bytes_accessed=2 * MIB, transcendentals=0),
        name="finish",
    )(kept, *parts)


def wave_kernel(window, section, codes, table, taps, bias, _after, out, done, laid):
    blocks, dialogs, _ = codes.shape
    entries, channels = table.shape
    tap_count = taps.shape[0]
    frames_out = window - tap_count + 1

    def one_block(k, carry):
        block = codes[k]
        count = block[:, window : window + 1]
        entry = lax.broadcasted_iota(jnp.int32, (dialogs, entries), 1)
        hot = []
        for p in range(window):
            code = jnp.where(p < count + tap_count - 1, block[:, p : p + 1], -1)
            hot.append((entry == code).astype(F32).astype(BF))
        frames = dot_n(jnp.concatenate(hot, axis=0), table[...])
        for t in range(frames_out):
            total = jnp.zeros((dialogs, channels), F32)
            for j in range(tap_count):
                at = (t + j) * dialogs
                total = total + taps[j : j + 1, :] * frames[at : at + dialogs]
            total = total + bias[...]
            feats = total / (1.0 + jnp.exp(-total))
            laid[pl.ds(t, dialogs, stride=frames_out), :] = jnp.where(t < count, feats, 0.0)
        owner = lax.rem(section[0] - k + blocks, blocks)
        result = laid[...].astype(BF).reshape(dialogs, frames_out, channels)
        out[pl.ds(owner * dialogs, dialogs)] = result
        return carry

    lax.fori_loop(0, blocks, one_block, 0)
    done[...] = jnp.zeros_like(done)


def wave(section, codes, table, taps, bias, after, window):
    blocks, dialogs, _ = codes.shape
    channels = table.shape[1]
    frames_out = window - taps.shape[0] + 1
    rows = blocks * dialogs
    return pl.pallas_call(
        functools.partial(wave_kernel, window),
        out_shape=(
            jax.ShapeDtypeStruct((rows, frames_out, channels), BF),
            jax.ShapeDtypeStruct((8, 128), F32),
        ),
        in_specs=[smem()] + [vmem()] * 4 + [anywhere()],
        out_specs=(vmem(), vmem()),
        scratch_shapes=[pltpu.VMEM((dialogs * frames_out, channels), F32)],
        compiler_params=pltpu.CompilerParams(vmem_limit_bytes=16 * MIB),
        cost_estimate=pl.CostEstimate(
            flops=2 * rows * window * table.shape[0] * channels,
            bytes_accessed=2 * MIB,
            transcendentals=rows * frames_out * channels,
        ),
        name="wave",
    )(section, codes, table, taps, bias, after)


def expert_grid():
    chips = lax.axis_size("expert") // 2
    side = math.isqrt(chips)
    return side, chips // side


def swap_cores(array):
    return lax.ppermute(array, "expert", [(i, i ^ 1) for i in range(lax.axis_size("expert"))])


def move(array, stage, distance):
    nx, ny = expert_grid()
    route = []
    for x in range(nx):
        for y in range(ny):
            for core in range(2):
                if core == stage:
                    target = (x + distance) % nx * ny + y
                else:
                    target = x * ny + (y + distance) % ny
                route.append(((x * ny + y) * 2 + core, target * 2 + core))
    return lax.ppermute(array, "expert", route)


def along(array, distance):
    size = lax.axis_size("section")
    return lax.ppermute(array, "section", [(i, (i + distance) % size) for i in range(size)])


def gather_codes(codes, counts):
    dialogs, window = codes.shape
    held = jnp.concatenate(
        [codes, counts[:, None], jnp.zeros((dialogs, 15 - window), jnp.int32)], axis=1
    )
    held = [jnp.transpose(held)[None]]
    distance = 1
    while distance < lax.axis_size("section"):
        held.append(jnp.concatenate([held[-1], along(held[-1], distance)], axis=0))
        distance *= 2
    return held


def shards(
    thinker_rows,
    codec_prev,
    w_text,
    attn_gain,
    w_q,
    key_value_weight,
    q_gain,
    k_gain,
    w_o,
    cache_k,
    value_cache,
    lengths,
    moe_gain,
    router,
    routes,
    w_gate_up,
    w_down,
    codes,
    counts,
    code_table,
    conv_weight,
    conv_bias,
):
    dialogs, steps, _ = thinker_rows.shape
    context = cache_k.shape[1]
    rows = dialogs * steps
    width = codec_prev.shape[2]
    handed = along(jnp.transpose(thinker_rows, (1, 0, 2)), 1)
    gu_a, down_a = w_gate_up[0], w_down[0]
    gu_b, down_b = swap_cores(gu_a), swap_cores(down_a)
    held = gather_codes(codes, counts)
    mine = lax.axis_index("expert").astype(jnp.int32)
    ids = jnp.stack([mine, mine + 1 - 2 * (mine % 2), jnp.int32(router.shape[1])])
    picks = jnp.transpose(routes, (2, 1, 0)).reshape(routes.shape[2], rows)
    live = (jnp.arange(context)[None, :] < lengths[:, None]).astype(F32)
    hidden, sent = dense(
        handed,
        jnp.transpose(codec_prev, (1, 0, 2)),
        (attn_gain[None], q_gain[None], k_gain[None], moe_gain[None]),
        jnp.transpose(router),
        picks,
        live.reshape(1, dialogs * context),
        (w_text, w_q, key_value_weight, w_o),
        [c.reshape(dialogs * context, c.shape[2]) for c in (cache_k, value_cache)],
        held[min(1, len(held) - 1)],
    )
    expert_weights = (gu_a, down_a, gu_b, down_b)
    line = join(
        (sent, move(sent, 0, 1), move(sent, 0, -1), move(sent, 0, 2)), held[min(2, len(held) - 1)]
    )
    half = line.shape[0] // 2
    near_m, near_p = move(line, 1, 1), move(line, 1, -1)
    (own,) = run_experts((line,), ((0,),), ids, expert_weights, line, "experts_own")
    far_t, far_b = cut(near_m, near_p, own)
    far_t, far_b = move(far_t, 1, 1), move(far_b, 1, -1)
    near = run_experts((near_m, near_p), ((0,), (1,)), ids, expert_weights, own, "experts_near")
    far = run_experts((far_t, far_b), ((0, 1),), ids, expert_weights, near[0], "experts_far")
    back_t, back_b = move(far[0], 1, -1), move(far[1], 1, 1)
    near = add_far(near[0], back_t, near[1], back_b)
    sum_m, sum_p = move(near[0], 1, -1), move(near[1], 1, 1)
    wave_feats, wave_done = wave(
        lax.axis_index("section").astype(jnp.int32).reshape(1),
        jnp.transpose(held[-1], (0, 2, 1)),
        code_table,
        conv_weight,
        conv_bias[None],
        near[0],
        codes.shape[1],
    )
    kept, *sums = merge(hidden, own, sum_m, sum_p, wave_done)
    out = finish(kept, (move(sums[0], 0, -1), move(sums[1], 0, 1), move(sums[2], 0, 2)))
    return (jnp.transpose(out.reshape(steps, dialogs, width), (1, 0, 2)), wave_feats)


def solution(mesh):
    each = P(("expert", "section"), None, None)
    return jax.shard_map(
        shards,
        mesh=mesh,
        in_specs=(
            each,
            each,
            P(),
            P(),
            P(),
            P(),
            P(),
            P(),
            P(),
            each,
            each,
            P(("expert", "section")),
            P(),
            P(),
            each,
            P("expert", None, None),
            P("expert", None, None),
            P(("expert", "section"), None),
            P(("expert", "section")),
            P(None, "section"),
            P(None, "section"),
            P("section"),
        ),
        out_specs=(each, P("expert", None, "section")),
        check_vma=False,
    )
```

```python
import functools
import math

import jax
import jax.numpy as jnp
from jax import lax
from jax.experimental import pallas as pl
from jax.experimental.pallas import tpu as pltpu
from jax.sharding import PartitionSpec as P

epsilon = 1e-06
masked_score = -1e30
BF = jnp.bfloat16
F32 = jnp.float32
MIB = 1024 * 1024
CODES_BLOCK = (256, 128)
GATE = 128


def vmem():
    return pl.BlockSpec(memory_space=pltpu.VMEM)


def smem():
    return pl.BlockSpec(memory_space=pltpu.SMEM)


def anywhere():
    return pl.BlockSpec(memory_space=pl.ANY)


def stay(array):
    return pltpu.with_memory_space_constraint(array, pltpu.HBM)


def dot_t(a, b):
    return lax.dot_general(a, b, (((1,), (1,)), ((), ())), preferred_element_type=F32)


def dot_n(a, b):
    return jnp.dot(a, b, preferred_element_type=F32)


def rms_norm(values, gain):
    mean_square = jnp.mean(values * values, axis=-1, keepdims=True)
    return values * lax.rsqrt(mean_square + epsilon) * gain


def dense_kernel(
    handed,
    picks,
    live,
    codes,
    attn_gain_hbm,
    q_gain_hbm,
    k_gain_hbm,
    moe_gain_hbm,
    router_hbm,
    codec_hbm,
    w_text,
    w_q,
    w_kv,
    w_o,
    cache_k,
    cache_v,
    hidden_out,
    sent_out,
    codes_out,
    attn_gain,
    q_gain,
    k_gain,
    moe_gain,
    router_t,
    codec,
    text_buf,
    q_buf,
    kv_buf,
    o_buf,
    ck_buf,
    cv_buf,
    att,
    sems,
):
    steps, dialogs, wide = handed.shape
    rows = steps * dialogs
    width = text_buf.shape[1]
    head = q_gain.shape[1]
    heads = q_buf.shape[1] // head
    kv_heads = kv_buf.shape[1] // (2 * head)
    group = heads // kv_heads
    context = cache_k.shape[0] // dialogs
    parts = 4
    span = wide // parts

    def text_copy(i):
        place = pl.ds(i * span, span)
        return pltpu.make_async_copy(w_text.at[place], text_buf.at[place], sems.at[i])

    def whole_copies(pairs, first):
        return [
            pltpu.make_async_copy(source, target, sems.at[first + i])
            for i, (source, target) in enumerate(pairs)
        ]

    copies = [text_copy(i) for i in range(parts)]
    copies += whole_copies(
        ((w_q, q_buf), (w_kv, kv_buf), (cache_k, ck_buf), (cache_v, cv_buf), (w_o, o_buf)), parts
    )
    small = whole_copies(
        (
            (codec_hbm, codec),
            (attn_gain_hbm, attn_gain),
            (q_gain_hbm, q_gain),
            (k_gain_hbm, k_gain),
            (moe_gain_hbm, moe_gain),
            (router_hbm, router_t),
        ),
        parts + 5,
    )
    copies[0].start()
    for copy in small:
        copy.start()
    for copy in copies[1:]:
        copy.start()
    codes_out[...] = jnp.zeros_like(codes_out)
    codes_out[: codes.shape[0], : codes.shape[1]] = codes[...]
    for copy in small:
        copy.wait()
    inputs = codec[...].reshape(rows, width).astype(F32)
    for i in range(parts):
        copies[i].wait()
        block = handed[:, :, i * span : (i + 1) * span].reshape(rows, span)
        inputs = inputs + dot_n(block, text_buf[i * span : (i + 1) * span, :])
    normed = rms_norm(inputs, attn_gain[...]).astype(BF)
    copies[parts].wait()
    q_all = dot_n(normed, q_buf[...])
    copies[parts + 1].wait()
    kv = dot_n(normed, kv_buf[...])
    queries = [rms_norm(q_all[:, h * head : (h + 1) * head], q_gain[...]) for h in range(heads)]
    keys = [
        rms_norm(kv[:, n * head : (n + 1) * head], k_gain[...]).astype(BF) for n in range(kv_heads)
    ]
    values = [
        kv[:, (kv_heads + n) * head : (kv_heads + n + 1) * head].astype(BF)
        for n in range(kv_heads)
    ]
    copies[parts + 2].wait()
    copies[parts + 3].wait()

    bunch = 8
    q_rows = group * steps * bunch
    span_c = bunch * context
    row = lax.broadcasted_iota(jnp.int32, (q_rows, span_c), 0)
    col = lax.broadcasted_iota(jnp.int32, (q_rows, span_c), 1)
    same = (row % bunch) == (col // context)
    row_n = lax.broadcasted_iota(jnp.int32, (q_rows, rows), 0)
    col_n = lax.broadcasted_iota(jnp.int32, (q_rows, rows), 1)
    causal = (col_n // dialogs) <= ((row_n // bunch) % steps)
    scale = 1.0 / math.sqrt(head)
    pairs = [(g, n) for g in range(dialogs // bunch) for n in range(kv_heads)]
    scored = []
    for g, n in pairs:
        pieces = [
            queries[n * group + j][t * dialogs + g * bunch : t * dialogs + (g + 1) * bunch]
            for j in range(group)
            for t in range(steps)
        ]
        q = jnp.concatenate(pieces, axis=0).astype(BF)
        old_k = ck_buf[g * span_c : (g + 1) * span_c, n * head : (n + 1) * head]
        scored.append((dot_t(q, old_k) * scale, dot_t(q, keys[n]) * scale))
    weighted = []
    for (g, n), (s_c, s_n) in zip(pairs, scored):
        ok_c = same & (live[:, g * span_c : (g + 1) * span_c] > 0)
        ok_n = causal & ((col_n % dialogs) == (row_n % bunch + g * bunch))
        s_c = jnp.where(ok_c, s_c, masked_score)
        s_n = jnp.where(ok_n, s_n, masked_score)
        top = jnp.maximum(
            jnp.max(s_c, axis=-1, keepdims=True), jnp.max(s_n, axis=-1, keepdims=True)
        )
        e_c = jnp.where(ok_c, jnp.exp(s_c - top), 0.0)
        e_n = jnp.where(ok_n, jnp.exp(s_n - top), 0.0)
        total = jnp.sum(e_c, axis=-1, keepdims=True) + jnp.sum(e_n, axis=-1, keepdims=True)
        weighted.append(((e_c / total).astype(BF), (e_n / total).astype(BF)))
    for (g, n), (w_c, w_n) in zip(pairs, weighted):
        old_v = cv_buf[g * span_c : (g + 1) * span_c, n * head : (n + 1) * head]
        out = dot_n(w_c, old_v) + dot_n(w_n, values[n])
        for j in range(group):
            for t in range(steps):
                at = (j * steps + t) * bunch
                h = n * group + j
                att[
                    t * dialogs + g * bunch : t * dialogs + (g + 1) * bunch,
                    h * head : (h + 1) * head,
                ] = out[at : at + bunch]

    copies[parts + 4].wait()
    hidden = inputs + dot_n(att[...].astype(BF), o_buf[...])
    hidden_out[...] = hidden
    routed = rms_norm(hidden, moe_gain[...]).astype(BF)
    experts = router_t.shape[0]
    logits = dot_t(router_t[...], routed)
    expert_id = lax.broadcasted_iota(jnp.int32, (experts, rows), 0)
    chosen = expert_id == picks[0:1, :]
    for k in range(1, picks.shape[0]):
        chosen = chosen | (expert_id == picks[k : k + 1, :])
    logits = jnp.where(chosen, logits, masked_score)
    raised = jnp.where(chosen, jnp.exp(logits - jnp.max(logits, axis=0, keepdims=True)), 0.0)
    gate = raised / jnp.sum(raised, axis=0, keepdims=True)
    high = gate.astype(BF).astype(F32)
    low = gate - high
    flat = jnp.concatenate([high, low, jnp.zeros((GATE - 2 * experts, rows), F32)], axis=0)
    flat = jnp.concatenate([flat, jnp.zeros((GATE, GATE - rows), F32)], axis=1)
    columns = jnp.transpose(flat)[:rows].astype(BF)
    sent_out[:, :width] = routed
    sent_out[:, width:] = columns


def dense(handed, picks, live, codes, small, weights, caches):
    steps, dialogs, _ = handed.shape
    rows = steps * dialogs
    w_text, _, _, w_o = weights
    width = w_text.shape[1]
    copied = [*small, *weights, *caches]
    return pl.pallas_call(
        dense_kernel,
        out_shape=(
            jax.ShapeDtypeStruct((rows, width), F32),
            jax.ShapeDtypeStruct((rows, width + GATE), BF),
            jax.ShapeDtypeStruct(CODES_BLOCK, jnp.int32),
        ),
        in_specs=[vmem()] * 4 + [anywhere()] * len(copied),
        out_specs=(vmem(),) * 3,
        scratch_shapes=[pltpu.VMEM(c.shape, c.dtype) for c in copied]
        + [pltpu.VMEM((rows, w_o.shape[0]), F32), pltpu.SemaphoreType.DMA((15,))],
        compiler_params=pltpu.CompilerParams(vmem_limit_bytes=24 * MIB),
        cost_estimate=pl.CostEstimate(
            flops=10 * rows * width * width, bytes_accessed=11 * MIB, transcendentals=400000
        ),
        name="dense",
    )(handed, picks, live, codes, *(stay(c) for c in copied))


def expert_kernel(count, ids, *refs):
    ins = refs[:count]
    weights = refs[count : count + 4]
    outs = refs[count + 5 :]
    inner, width = weights[1].shape
    x = jnp.concatenate([part[:, :width] for part in ins], axis=0)
    gates = jnp.concatenate([part[:, width:] for part in ins], axis=0).astype(F32)
    lane = lax.broadcasted_iota(jnp.int32, gates.shape, 1)
    total = None
    for e in range(2):
        gate_up, down = weights[2 * e], weights[2 * e + 1]
        mine = (lane == ids[e]) | (lane == ids[e] + ids[2])
        gate = jnp.sum(jnp.where(mine, gates, 0.0), axis=1, keepdims=True)
        gu = dot_n(x, gate_up[...])
        g = gu[:, :inner]
        act = ((g / (1.0 + jnp.exp(-g))) * gu[:, inner:]).astype(BF)
        out = dot_n(act, down[...]) * gate
        total = out if total is None else total + out
    total = total.astype(BF)
    place = 0
    for out in outs:
        out[...] = total[place : place + out.shape[0]]
        place += out.shape[0]


def run_experts(arrays, ids, weights, after, name):
    count = len(arrays)
    inner, width = weights[1].shape
    rows = sum(a.shape[0] for a in arrays)
    return pl.pallas_call(
        functools.partial(expert_kernel, count),
        out_shape=tuple(jax.ShapeDtypeStruct((a.shape[0], width), BF) for a in arrays),
        in_specs=[smem()] + [vmem()] * (count + 4) + [anywhere()],
        out_specs=tuple(vmem() for _ in arrays),
        compiler_params=pltpu.CompilerParams(vmem_limit_bytes=24 * MIB),
        cost_estimate=pl.CostEstimate(
            flops=2 * rows * 6 * inner * width,
            bytes_accessed=4 * rows * width + 12 * inner * width,
            transcendentals=rows * 2 * inner,
        ),
        name=name,
    )(ids, *arrays, *weights, after)


def join_kernel(*refs):
    *ins, out = refs
    place = 0
    for part in ins:
        out[place : place + part.shape[0], :] = part[...]
        place += part.shape[0]


def join(arrays):
    rows = sum(a.shape[0] for a in arrays)
    return pl.pallas_call(
        join_kernel,
        out_shape=jax.ShapeDtypeStruct((rows, arrays[0].shape[1]), arrays[0].dtype),
        in_specs=[vmem()] * len(arrays),
        out_specs=vmem(),
        compiler_params=pltpu.CompilerParams(vmem_limit_bytes=16 * MIB),
        cost_estimate=pl.CostEstimate(flops=0, bytes_accessed=2 * MIB, transcendentals=0),
        name="join",
    )(*arrays)


def add_kernel(a, b, c, d, _after, first, second):
    first[...] = (a[...].astype(F32) + b[...].astype(F32)).astype(BF)
    second[...] = (c[...].astype(F32) + d[...].astype(F32)).astype(BF)


def add_two(a, b, c, d, after):
    shape = jax.ShapeDtypeStruct(a.shape, BF)
    return pl.pallas_call(
        add_kernel,
        out_shape=(shape,) * 2,
        in_specs=[vmem()] * 4 + [anywhere()],
        out_specs=(vmem(),) * 2,
        compiler_params=pltpu.CompilerParams(vmem_limit_bytes=16 * MIB),
        cost_estimate=pl.CostEstimate(flops=2**18, bytes_accessed=2 * MIB, transcendentals=0),
        name="add_far",
    )(a, b, c, d, after)


def merge_kernel(hidden, own_t, t1, t2, own_b, b1, b2, _after, kept, *outs):
    size = hidden.shape[0]
    for k in range(1 + len(outs)):
        group = (own_t, t1, t2) if k < 2 else (own_b, b1, b2)
        place = slice(k % 2 * size, (k % 2 + 1) * size)
        total = sum(part[place, :].astype(F32) for part in group)
        if k == 0:
            kept[...] = hidden[...] + total
        else:
            outs[k - 1][...] = total.astype(BF)


def merge(hidden, upper, lower, after):
    size, width = hidden.shape
    return pl.pallas_call(
        merge_kernel,
        out_shape=(jax.ShapeDtypeStruct(hidden.shape, F32),)
        + (jax.ShapeDtypeStruct((size, width), BF),) * 3,
        in_specs=[vmem()] * 7 + [anywhere()],
        out_specs=(vmem(),) * 4,
        compiler_params=pltpu.CompilerParams(vmem_limit_bytes=16 * MIB),
        cost_estimate=pl.CostEstimate(flops=2**20, bytes_accessed=4 * MIB, transcendentals=0),
        name="merge",
    )(hidden, *upper, *lower, after)


def finish_kernel(kept, *refs):
    *parts, out = refs
    total = kept[...]
    for part in parts:
        total = total + part[...].astype(F32)
    out[...] = total.astype(BF)


def finish(kept, parts):
    return pl.pallas_call(
        finish_kernel,
        out_shape=jax.ShapeDtypeStruct(kept.shape, BF),
        in_specs=[vmem()] * (1 + len(parts)),
        out_specs=vmem(),
        compiler_params=pltpu.CompilerParams(vmem_limit_bytes=16 * MIB),
        cost_estimate=pl.CostEstimate(flops=2**19, bytes_accessed=2 * MIB, transcendentals=0),
        name="finish",
    )(kept, *parts)


def wave_kernel(window, dialogs, first, blocks, codes, table, taps, bias, *refs):
    _before, out, done, held, laid, sem = refs
    entries, channels = table.shape
    tap_count = taps.shape[0]
    frames_out = window - tap_count + 1
    copy = pltpu.make_async_copy(
        codes.at[pl.ds(first, blocks), pl.ds(0, dialogs), :], held, sem.at[0]
    )
    copy.start()
    copy.wait()

    def one_block(k, carry):
        block = held[k]
        count = block[:, window : window + 1]
        entry = lax.broadcasted_iota(jnp.int32, (dialogs, entries), 1)
        hot = []
        for p in range(window):
            code = jnp.where(p < count + tap_count - 1, block[:, p : p + 1], -1)
            hot.append((entry == code).astype(F32).astype(BF))
        frames = dot_n(jnp.concatenate(hot, axis=0), table[...])
        for t in range(frames_out):
            total = jnp.zeros((dialogs, channels), F32)
            for j in range(tap_count):
                at = (t + j) * dialogs
                total = total + taps[j : j + 1, :] * frames[at : at + dialogs]
            total = total + bias[...]
            feats = total / (1.0 + jnp.exp(-total))
            laid[pl.ds(t, dialogs, stride=frames_out), :] = jnp.where(t < count, feats, 0.0)
        result = laid[...].astype(BF).reshape(dialogs, frames_out, channels)
        out[pl.ds(k * dialogs, dialogs)] = result
        return carry

    lax.fori_loop(0, blocks, one_block, 0)
    done[...] = jnp.zeros_like(done)


def wave(codes, table, taps, bias, before, window, dialogs, part, parts):
    blocks = codes.shape[0] // parts
    channels = table.shape[1]
    frames_out = window - taps.shape[0] + 1
    rows = blocks * dialogs
    return pl.pallas_call(
        functools.partial(wave_kernel, window, dialogs, part * blocks, blocks),
        grid=(1,),
        out_shape=(
            jax.ShapeDtypeStruct((parts * rows, frames_out, channels), BF),
            jax.ShapeDtypeStruct((8, 128), F32),
        ),
        in_specs=[anywhere()]
        + [pl.BlockSpec(a.shape, lambda i: (0, 0)) for a in (table, taps, bias)]
        + [anywhere()],
        out_specs=(
            pl.BlockSpec((rows, frames_out, channels), lambda i: (part, 0, 0)),
            pl.BlockSpec((8, 128), lambda i: (0, 0)),
        ),
        scratch_shapes=[
            pltpu.VMEM((blocks, dialogs, codes.shape[2]), jnp.int32),
            pltpu.VMEM((dialogs * frames_out, channels), F32),
            pltpu.SemaphoreType.DMA((1,)),
        ],
        input_output_aliases={4: 0} if part else {},
        compiler_params=pltpu.CompilerParams(vmem_limit_bytes=16 * MIB),
        cost_estimate=pl.CostEstimate(
            flops=2 * rows * window * table.shape[0] * channels,
            bytes_accessed=2 * MIB,
            transcendentals=rows * frames_out * channels,
        ),
        name="wave",
    )(stay(codes), table, taps, bias, before)


def expert_grid():
    chips = lax.axis_size("expert") // 2
    side = math.isqrt(chips)
    return side, chips // side


def swap_cores(array):
    return lax.ppermute(array, "expert", [(i, i ^ 1) for i in range(lax.axis_size("expert"))])


def move(array, stage, distance):
    nx, ny = expert_grid()
    route = []
    for x in range(nx):
        for y in range(ny):
            for core in range(2):
                if core == stage:
                    target = (x + distance) % nx * ny + y
                else:
                    target = x * ny + (y + distance) % ny
                route.append(((x * ny + y) * 2 + core, target * 2 + core))
    return lax.ppermute(array, "expert", route)


def along(array, distance):
    size = lax.axis_size("section")
    return lax.ppermute(array, "section", [(i, (i + distance) % size) for i in range(size)])


def shards(
    thinker_rows,
    codec_prev,
    w_text,
    attn_gain,
    w_q,
    key_value_weight,
    q_gain,
    k_gain,
    w_o,
    cache_k,
    value_cache,
    lengths,
    moe_gain,
    router,
    routes,
    w_gate_up,
    w_down,
    codes,
    counts,
    code_table,
    conv_weight,
    conv_bias,
):
    dialogs, steps, _ = thinker_rows.shape
    context = cache_k.shape[1]
    rows = dialogs * steps
    width = codec_prev.shape[2]
    handed = along(jnp.transpose(thinker_rows, (1, 0, 2)), 1)
    gu_a, down_a = w_gate_up[0], w_down[0]
    expert_weights = (gu_a, down_a, swap_cores(gu_a), swap_cores(down_a))
    mine = lax.axis_index("expert").astype(jnp.int32)
    ids = jnp.stack([mine, mine + 1 - 2 * (mine % 2), jnp.int32(router.shape[1])])
    picks = jnp.transpose(routes, (2, 1, 0)).reshape(routes.shape[2], rows)
    live = (jnp.arange(context)[None, :] < lengths[:, None]).astype(F32)
    live = live.reshape(1, dialogs * context)
    codes = jnp.concatenate([codes, counts[:, None]], axis=1)
    hidden, sent, codes_block = dense(
        handed,
        picks,
        live,
        codes,
        (
            attn_gain[None],
            q_gain[None],
            k_gain[None],
            moe_gain[None],
            jnp.transpose(router),
            jnp.transpose(codec_prev, (1, 0, 2)),
        ),
        (w_text, w_q, key_value_weight, w_o),
        [c.reshape(dialogs * context, c.shape[2]) for c in (cache_k, value_cache)],
    )
    all_codes = lax.all_gather(codes_block, "section", axis=0)
    sent_m, sent_p, sent_x = move(sent, 0, 1), move(sent, 0, -1), move(sent, 0, 2)
    upper = join((sent, sent_m))
    upper_m, upper_p = move(upper, 1, 1), move(upper, 1, -1)
    lower = join((sent_p, sent_x))
    lower_m, lower_p = move(lower, 1, 1), move(lower, 1, -1)
    experts = functools.partial(run_experts, ids=ids, weights=expert_weights)
    own_u, own_l = experts((upper, lower), after=lower, name="experts_own")
    upper_m, lower_p, own_u = lax.optimization_barrier((upper_m, lower_p, own_u))
    far_u, far_l = move(upper_m, 1, 1), move(lower_p, 1, -1)
    from_um, from_up = experts((upper_m, upper_p), after=own_u, name="experts_upper")
    from_lm, from_lp = experts((lower_m, lower_p), after=from_um, name="experts_lower")
    from_fu, from_fl = experts((far_u, far_l), after=from_lm, name="experts_far")
    back_up, back_lm = move(from_up, 1, 1), move(from_lm, 1, -1)
    back_fu, back_fl = move(from_fu, 1, -1), move(from_fl, 1, 1)
    wave_part = functools.partial(
        wave,
        all_codes,
        code_table,
        conv_weight,
        conv_bias[None],
        window=codes.shape[1] - 1,
        dialogs=dialogs,
        parts=2,
    )
    from_fu, back_up, back_lm = lax.optimization_barrier((from_fu, back_up, back_lm))
    wave_half, wave_done = wave_part(before=from_fu, part=0)
    from_um, from_lp = add_two(from_um, back_fu, from_lp, back_fl, wave_done)
    back_um, back_lp = move(from_um, 1, -1), move(from_lp, 1, 1)
    wave_feats, wave_done = wave_part(before=wave_half, part=1)
    kept, *sums = merge(
        hidden, (own_u, back_um, back_up), (own_l, back_lm, back_lp), wave_done
    )
    out = finish(kept, (move(sums[0], 0, -1), move(sums[1], 0, 1), move(sums[2], 0, 2)))
    return (jnp.transpose(out.reshape(steps, dialogs, width), (1, 0, 2)), wave_feats)


def solution(mesh):
    each = P(("expert", "section"), None, None)
    return jax.shard_map(
        shards,
        mesh=mesh,
        in_specs=(
            each,
            each,
            P(),
            P(),
            P(),
            P(),
            P(),
            P(),
            P(),
            each,
            each,
            P(("expert", "section")),
            P(),
            P(),
            each,
            P("expert", None, None),
            P("expert", None, None),
            P(("expert", "section"), None),
            P(("expert", "section")),
            P(None, "section"),
            P(None, "section"),
            P("section"),
        ),
        out_specs=(each, P("expert", None, "section")),
        check_vma=False,
    )
```

```python
import functools
import math

import jax
import jax.numpy as jnp
from jax import lax
from jax.experimental import pallas as pl
from jax.experimental.pallas import tpu as pltpu
from jax.sharding import PartitionSpec as P

epsilon = 1e-06
masked_score = -1e30
BF = jnp.bfloat16
F32 = jnp.float32
MIB = 1024 * 1024
GATE = 128


def vmem():
    return pl.BlockSpec(memory_space=pltpu.VMEM)


def smem():
    return pl.BlockSpec(memory_space=pltpu.SMEM)


def anywhere():
    return pl.BlockSpec(memory_space=pl.ANY)


def stay(array):
    return pltpu.with_memory_space_constraint(array, pltpu.HBM)


def dot_t(a, b):
    return lax.dot_general(a, b, (((1,), (1,)), ((), ())), preferred_element_type=F32)


def dot_n(a, b):
    return jnp.dot(a, b, preferred_element_type=F32)


def rms_norm(values, gain):
    mean_square = jnp.mean(values * values, axis=-1, keepdims=True)
    return values * lax.rsqrt(mean_square + epsilon) * gain


def dense_kernel(
    handed,
    picks,
    live,
    attn_gain_hbm,
    q_gain_hbm,
    k_gain_hbm,
    moe_gain_hbm,
    router_hbm,
    codec_hbm,
    w_text,
    w_q,
    w_kv,
    w_o,
    cache_k,
    cache_v,
    _after,
    hidden_out,
    sent_out,
    attn_gain,
    q_gain,
    k_gain,
    moe_gain,
    router_t,
    codec,
    text_buf,
    q_buf,
    kv_buf,
    o_buf,
    ck_buf,
    cv_buf,
    att,
    sems,
):
    steps, dialogs, wide = handed.shape
    rows = steps * dialogs
    width = text_buf.shape[1]
    head = q_gain.shape[1]
    heads = q_buf.shape[1] // head
    kv_heads = kv_buf.shape[1] // (2 * head)
    group = heads // kv_heads
    context = cache_k.shape[0] // dialogs
    parts = 4
    span = wide // parts

    def text_copy(i):
        place = pl.ds(i * span, span)
        return pltpu.make_async_copy(w_text.at[place], text_buf.at[place], sems.at[i])

    def whole_copies(pairs, first):
        return [
            pltpu.make_async_copy(source, target, sems.at[first + i])
            for i, (source, target) in enumerate(pairs)
        ]

    copies = [text_copy(i) for i in range(parts)]
    copies += whole_copies(
        ((w_q, q_buf), (w_kv, kv_buf), (cache_k, ck_buf), (cache_v, cv_buf), (w_o, o_buf)), parts
    )
    small = whole_copies(
        (
            (codec_hbm, codec),
            (attn_gain_hbm, attn_gain),
            (q_gain_hbm, q_gain),
            (k_gain_hbm, k_gain),
            (moe_gain_hbm, moe_gain),
            (router_hbm, router_t),
        ),
        parts + 5,
    )
    copies[0].start()
    for copy in small:
        copy.start()
    for copy in copies[1:]:
        copy.start()
    for copy in small:
        copy.wait()
    inputs = codec[...].reshape(rows, width).astype(F32)
    for i in range(parts):
        copies[i].wait()
        block = handed[:, :, i * span : (i + 1) * span].reshape(rows, span)
        inputs = inputs + dot_n(block, text_buf[i * span : (i + 1) * span, :])
    normed = rms_norm(inputs, attn_gain[...]).astype(BF)
    copies[parts].wait()
    q_all = dot_n(normed, q_buf[...])
    copies[parts + 1].wait()
    kv = dot_n(normed, kv_buf[...])
    queries = [rms_norm(q_all[:, h * head : (h + 1) * head], q_gain[...]) for h in range(heads)]
    keys = [
        rms_norm(kv[:, n * head : (n + 1) * head], k_gain[...]).astype(BF) for n in range(kv_heads)
    ]
    values = [
        kv[:, (kv_heads + n) * head : (kv_heads + n + 1) * head].astype(BF)
        for n in range(kv_heads)
    ]
    copies[parts + 2].wait()
    copies[parts + 3].wait()

    bunch = 8
    q_rows = group * steps * bunch
    span_c = bunch * context
    row = lax.broadcasted_iota(jnp.int32, (q_rows, span_c), 0)
    col = lax.broadcasted_iota(jnp.int32, (q_rows, span_c), 1)
    same = (row % bunch) == (col // context)
    row_n = lax.broadcasted_iota(jnp.int32, (q_rows, rows), 0)
    col_n = lax.broadcasted_iota(jnp.int32, (q_rows, rows), 1)
    causal = (col_n // dialogs) <= ((row_n // bunch) % steps)
    scale = 1.0 / math.sqrt(head)
    pairs = [(g, n) for g in range(dialogs // bunch) for n in range(kv_heads)]
    scored = []
    for g, n in pairs:
        pieces = [
            queries[n * group + j][t * dialogs + g * bunch : t * dialogs + (g + 1) * bunch]
            for j in range(group)
            for t in range(steps)
        ]
        q = jnp.concatenate(pieces, axis=0).astype(BF)
        old_k = ck_buf[g * span_c : (g + 1) * span_c, n * head : (n + 1) * head]
        scored.append((dot_t(q, old_k) * scale, dot_t(q, keys[n]) * scale))
    weighted = []
    for (g, n), (s_c, s_n) in zip(pairs, scored):
        ok_c = same & (live[:, g * span_c : (g + 1) * span_c] > 0)
        ok_n = causal & ((col_n % dialogs) == (row_n % bunch + g * bunch))
        s_c = jnp.where(ok_c, s_c, masked_score)
        s_n = jnp.where(ok_n, s_n, masked_score)
        top = jnp.maximum(
            jnp.max(s_c, axis=-1, keepdims=True), jnp.max(s_n, axis=-1, keepdims=True)
        )
        e_c = jnp.where(ok_c, jnp.exp(s_c - top), 0.0)
        e_n = jnp.where(ok_n, jnp.exp(s_n - top), 0.0)
        total = jnp.sum(e_c, axis=-1, keepdims=True) + jnp.sum(e_n, axis=-1, keepdims=True)
        weighted.append(((e_c / total).astype(BF), (e_n / total).astype(BF)))
    for (g, n), (w_c, w_n) in zip(pairs, weighted):
        old_v = cv_buf[g * span_c : (g + 1) * span_c, n * head : (n + 1) * head]
        out = dot_n(w_c, old_v) + dot_n(w_n, values[n])
        for j in range(group):
            for t in range(steps):
                at = (j * steps + t) * bunch
                h = n * group + j
                att[
                    t * dialogs + g * bunch : t * dialogs + (g + 1) * bunch,
                    h * head : (h + 1) * head,
                ] = out[at : at + bunch]

    copies[parts + 4].wait()
    hidden = inputs + dot_n(att[...].astype(BF), o_buf[...])
    hidden_out[...] = hidden
    routed = rms_norm(hidden, moe_gain[...]).astype(BF)
    experts = router_t.shape[0]
    logits = dot_t(router_t[...], routed)
    expert_id = lax.broadcasted_iota(jnp.int32, (experts, rows), 0)
    chosen = expert_id == picks[0:1, :]
    for k in range(1, picks.shape[0]):
        chosen = chosen | (expert_id == picks[k : k + 1, :])
    logits = jnp.where(chosen, logits, masked_score)
    raised = jnp.where(chosen, jnp.exp(logits - jnp.max(logits, axis=0, keepdims=True)), 0.0)
    gate = raised / jnp.sum(raised, axis=0, keepdims=True)
    high = gate.astype(BF).astype(F32)
    low = gate - high
    flat = jnp.concatenate([high, low, jnp.zeros((GATE - 2 * experts, rows), F32)], axis=0)
    flat = jnp.concatenate([flat, jnp.zeros((GATE, GATE - rows), F32)], axis=1)
    columns = jnp.transpose(flat)[:rows].astype(BF)
    sent_out[:, :width] = routed
    sent_out[:, width:] = columns


def dense(handed, picks, live, small, weights, caches, after):
    steps, dialogs, _ = handed.shape
    rows = steps * dialogs
    w_text, _, _, w_o = weights
    width = w_text.shape[1]
    copied = [*small, *weights, *caches]
    return pl.pallas_call(
        dense_kernel,
        out_shape=(
            jax.ShapeDtypeStruct((rows, width), F32),
            jax.ShapeDtypeStruct((rows, width + GATE), BF),
        ),
        in_specs=[vmem()] * 3 + [anywhere()] * (len(copied) + 1),
        out_specs=(vmem(),) * 2,
        scratch_shapes=[pltpu.VMEM(c.shape, c.dtype) for c in copied]
        + [pltpu.VMEM((rows, w_o.shape[0]), F32), pltpu.SemaphoreType.DMA((15,))],
        compiler_params=pltpu.CompilerParams(vmem_limit_bytes=24 * MIB),
        cost_estimate=pl.CostEstimate(
            flops=10 * rows * width * width, bytes_accessed=11 * MIB, transcendentals=400000
        ),
        name="dense",
    )(handed, picks, live, *(stay(c) for c in copied), after)


def silu(v):
    half = 0.5 * v
    return half + half * jnp.tanh(half)


def expert_kernel(count, ids, *refs):
    ins = refs[:count]
    sources = refs[count : count + 4]
    outs = refs[count + 5 : 2 * count + 5]
    gate_up, down, sems = refs[2 * count + 5 :]
    inner, width = sources[1].shape
    targets = (gate_up.at[0], down.at[0], gate_up.at[1], down.at[1])
    copies = [
        pltpu.make_async_copy(sources[i], targets[i], sems.at[i]) for i in range(len(sources))
    ]
    for i in (0, 2, 1, 3):
        copies[i].start()
    x = jnp.concatenate([part[:, :width] for part in ins], axis=0)
    gates = jnp.concatenate([part[:, width:] for part in ins], axis=0).astype(F32)
    lane = lax.broadcasted_iota(jnp.int32, gates.shape, 1)
    acts = []
    for e in range(2):
        copies[2 * e].wait()
        gu = dot_n(x, gate_up[e])
        acts.append((silu(gu[:, :inner]) * gu[:, inner:]).astype(BF))
    total = None
    for e in range(2):
        mine = (lane == ids[e]) | (lane == ids[e] + ids[2])
        gate = jnp.sum(jnp.where(mine, gates, 0.0), axis=1, keepdims=True)
        copies[2 * e + 1].wait()
        out = dot_n(acts[e], down[e]) * gate
        total = out if total is None else total + out
    total = total.astype(BF)
    place = 0
    for out in outs:
        out[...] = total[place : place + out.shape[0]]
        place += out.shape[0]


def run_experts(arrays, ids, weights, after, name):
    count = len(arrays)
    inner, width = weights[1].shape
    rows = sum(a.shape[0] for a in arrays)
    return pl.pallas_call(
        functools.partial(expert_kernel, count),
        out_shape=tuple(jax.ShapeDtypeStruct((a.shape[0], width), BF) for a in arrays),
        in_specs=[smem()] + [vmem()] * count + [anywhere()] * 5,
        out_specs=tuple(vmem() for _ in arrays),
        scratch_shapes=[
            pltpu.VMEM((2, width, 2 * inner), BF),
            pltpu.VMEM((2, inner, width), BF),
            pltpu.SemaphoreType.DMA((4,)),
        ],
        compiler_params=pltpu.CompilerParams(vmem_limit_bytes=30 * MIB),
        cost_estimate=pl.CostEstimate(
            flops=2 * rows * 6 * inner * width,
            bytes_accessed=4 * rows * width + 12 * inner * width,
            transcendentals=rows * 2 * inner,
        ),
        name=name,
    )(ids, *arrays, stay(weights[0]), stay(weights[1]), weights[2], weights[3], after)


def join_kernel(*refs):
    *ins, _after, out = refs
    place = 0
    for part in ins:
        out[place : place + part.shape[0], :] = part[...]
        place += part.shape[0]


def join(arrays, after):
    rows = sum(a.shape[0] for a in arrays)
    return pl.pallas_call(
        join_kernel,
        out_shape=jax.ShapeDtypeStruct((rows, arrays[0].shape[1]), arrays[0].dtype),
        in_specs=[vmem()] * len(arrays) + [anywhere()],
        out_specs=vmem(),
        compiler_params=pltpu.CompilerParams(vmem_limit_bytes=16 * MIB),
        cost_estimate=pl.CostEstimate(flops=0, bytes_accessed=2 * MIB, transcendentals=0),
        name="join",
    )(*arrays, after)


def add_kernel(a, b, c, d, first, second):
    first[...] = (a[...].astype(F32) + b[...].astype(F32)).astype(BF)
    second[...] = (c[...].astype(F32) + d[...].astype(F32)).astype(BF)


def add_two(a, b, c, d):
    shape = jax.ShapeDtypeStruct(a.shape, BF)
    return pl.pallas_call(
        add_kernel,
        out_shape=(shape,) * 2,
        in_specs=[vmem()] * 4,
        out_specs=(vmem(),) * 2,
        compiler_params=pltpu.CompilerParams(vmem_limit_bytes=16 * MIB),
        cost_estimate=pl.CostEstimate(flops=2**18, bytes_accessed=2 * MIB, transcendentals=0),
        name="add_far",
    )(a, b, c, d)


def merge_kernel(hidden, own_t, t1, t2, own_b, b1, b2, _after, kept, *outs):
    size = hidden.shape[0]
    for k in range(1 + len(outs)):
        group = (own_t, t1, t2) if k < 2 else (own_b, b1, b2)
        place = slice(k % 2 * size, (k % 2 + 1) * size)
        total = sum(part[place, :].astype(F32) for part in group)
        if k == 0:
            kept[...] = hidden[...] + total
        else:
            outs[k - 1][...] = total.astype(BF)


def merge(hidden, upper, lower, after):
    size, width = hidden.shape
    return pl.pallas_call(
        merge_kernel,
        out_shape=(jax.ShapeDtypeStruct(hidden.shape, F32),)
        + (jax.ShapeDtypeStruct((size, width), BF),) * 3,
        in_specs=[vmem()] * 7 + [anywhere()],
        out_specs=(vmem(),) * 4,
        compiler_params=pltpu.CompilerParams(vmem_limit_bytes=16 * MIB),
        cost_estimate=pl.CostEstimate(flops=2**20, bytes_accessed=4 * MIB, transcendentals=0),
        name="merge",
    )(hidden, *upper, *lower, after)


def finish_kernel(kept, *refs):
    *parts, out = refs
    total = kept[...]
    for part in parts:
        total = total + part[...].astype(F32)
    out[...] = total.astype(BF)


def finish(kept, parts):
    return pl.pallas_call(
        finish_kernel,
        out_shape=jax.ShapeDtypeStruct(kept.shape, BF),
        in_specs=[vmem()] * (1 + len(parts)),
        out_specs=vmem(),
        compiler_params=pltpu.CompilerParams(vmem_limit_bytes=16 * MIB),
        cost_estimate=pl.CostEstimate(flops=2**19, bytes_accessed=2 * MIB, transcendentals=0),
        name="finish",
    )(kept, *parts)


def wave_kernel(
    window, section, near, far, table_hbm, taps_hbm, bias_hbm, _after, out, done, table, taps, bias, laid, sems
):
    blocks, dialogs, _ = near.shape
    part, channels = table.shape[0], bias.shape[1]
    tap_count = taps.shape[0]
    frames_out = window - tap_count + 1
    copies = [
        pltpu.make_async_copy(taps_hbm, taps, sems.at[0]),
        pltpu.make_async_copy(bias_hbm, bias, sems.at[1]),
    ]
    for q in range(2):
        copies.append(
            pltpu.make_async_copy(
                table_hbm.at[pl.ds(q * part, part)],
                table.at[:, pl.ds(q * channels, channels)],
                sems.at[2 + q],
            )
        )
    for copy in copies:
        copy.start()
    for copy in copies:
        copy.wait()
    entry = lax.broadcasted_iota(jnp.int32, (dialogs, part), 1)
    for first, codes in ((0, near), (blocks, far)):

        def one_block(k, carry, first=first, codes=codes):
            block = codes[k]
            count = block[:, window : window + 1]
            hot, upper = [], []
            for p in range(window):
                code = block[:, p : p + 1]
                upper.append(code >= part)
                code = jnp.where(code >= part, code - part, code)
                code = jnp.where(p < count + tap_count - 1, code, -1)
                hot.append((entry == code).astype(F32).astype(BF))
            found = dot_n(jnp.concatenate(hot, axis=0), table[...])
            frames = []
            for p in range(window):
                rows = found[p * dialogs : (p + 1) * dialogs]
                frames.append(jnp.where(upper[p], rows[:, channels:], rows[:, :channels]))
            for t in range(frames_out):
                total = jnp.zeros((dialogs, channels), F32) + bias[...]
                for j in range(tap_count):
                    total = total + taps[j : j + 1, :] * frames[t + j]
                laid[pl.ds(t, dialogs, stride=frames_out), :] = jnp.where(
                    t < count, silu(total), 0.0
                )
            owner = lax.rem(section[0] - (first + k) + 2 * blocks, 2 * blocks)
            result = laid[...].astype(BF).reshape(dialogs, frames_out, channels)
            out[pl.ds(owner * dialogs, dialogs)] = result
            return carry

        lax.fori_loop(0, blocks, one_block, 0)
    done[...] = jnp.zeros_like(done)


def wave(section, near, far, table, taps, bias, after, window):
    blocks, dialogs, _ = near.shape
    entries, channels = table.shape
    frames_out = window - taps.shape[0] + 1
    rows = 2 * blocks * dialogs
    return pl.pallas_call(
        functools.partial(wave_kernel, window),
        out_shape=(
            jax.ShapeDtypeStruct((rows, frames_out, channels), BF),
            jax.ShapeDtypeStruct((8, 128), F32),
        ),
        in_specs=[smem()] + [vmem()] * 2 + [anywhere()] * 4,
        out_specs=(vmem(), vmem()),
        scratch_shapes=[
            pltpu.VMEM((entries // 2, 2 * channels), BF),
            pltpu.VMEM(taps.shape, F32),
            pltpu.VMEM(bias.shape, F32),
            pltpu.VMEM((dialogs * frames_out, channels), F32),
            pltpu.SemaphoreType.DMA((4,)),
        ],
        compiler_params=pltpu.CompilerParams(vmem_limit_bytes=16 * MIB),
        cost_estimate=pl.CostEstimate(
            flops=2 * rows * window * entries * channels,
            bytes_accessed=2 * MIB,
            transcendentals=rows * frames_out * channels,
        ),
        name="wave",
    )(section, near, far, stay(table), stay(taps), stay(bias), after)


def expert_grid():
    chips = lax.axis_size("expert") // 2
    side = math.isqrt(chips)
    return side, chips // side


def swap_cores(array):
    return lax.ppermute(array, "expert", [(i, i ^ 1) for i in range(lax.axis_size("expert"))])


def move(array, stage, distance):
    nx, ny = expert_grid()
    route = []
    for x in range(nx):
        for y in range(ny):
            for core in range(2):
                if core == stage:
                    target = (x + distance) % nx * ny + y
                else:
                    target = x * ny + (y + distance) % ny
                route.append(((x * ny + y) * 2 + core, target * 2 + core))
    return lax.ppermute(array, "expert", route)


def along(array, distance):
    size = lax.axis_size("section")
    return lax.ppermute(array, "section", [(i, (i + distance) % size) for i in range(size)])


def shards(
    thinker_rows,
    codec_prev,
    w_text,
    attn_gain,
    w_q,
    key_value_weight,
    q_gain,
    k_gain,
    w_o,
    cache_k,
    value_cache,
    lengths,
    moe_gain,
    router,
    routes,
    w_gate_up,
    w_down,
    codes,
    counts,
    code_table,
    conv_weight,
    conv_bias,
):
    dialogs, steps, _ = thinker_rows.shape
    context = cache_k.shape[1]
    rows = dialogs * steps
    width = codec_prev.shape[2]
    handed = along(jnp.transpose(thinker_rows, (1, 0, 2)), 1)
    gu_a, down_a = w_gate_up[0], w_down[0]
    expert_weights = (gu_a, down_a, swap_cores(gu_a), swap_cores(down_a))
    mine = lax.axis_index("expert").astype(jnp.int32)
    ids = jnp.stack([mine, mine + 1 - 2 * (mine % 2), jnp.int32(router.shape[1])])
    picks = jnp.transpose(routes, (2, 1, 0)).reshape(routes.shape[2], rows)
    live = (jnp.arange(context)[None, :] < lengths[:, None]).astype(F32)
    window = codes.shape[1]
    held = jnp.concatenate(
        [codes, counts[:, None], jnp.zeros((dialogs, 15 - window), jnp.int32)], axis=1
    )[None]
    came = [along(held, 1)]
    while 2 * held.shape[0] < lax.axis_size("section"):
        held = jnp.concatenate([held, came[-1]], axis=0)
        came.append(along(held, held.shape[0]))
    hidden, sent = dense(
        handed,
        picks,
        live.reshape(1, dialogs * context),
        (
            attn_gain[None],
            q_gain[None],
            k_gain[None],
            moe_gain[None],
            jnp.transpose(router),
            jnp.transpose(codec_prev, (1, 0, 2)),
        ),
        (w_text, w_q, key_value_weight, w_o),
        [c.reshape(dialogs * context, c.shape[2]) for c in (cache_k, value_cache)],
        came[0],
    )
    sent_m, sent_p, sent_x = move(sent, 0, 1), move(sent, 0, -1), move(sent, 0, 2)
    upper = join((sent, sent_m), came[0])
    upper_m, upper_p = move(upper, 1, 1), move(upper, 1, -1)
    lower = join((sent_p, sent_x), came[len(came) // 2])
    lower_m, lower_p = move(lower, 1, 1), move(lower, 1, -1)
    experts = functools.partial(run_experts, ids=ids, weights=expert_weights)
    own_u, own_l = experts((upper, lower), after=came[0], name="experts_own")
    upper_m, lower_p, own_u = lax.optimization_barrier((upper_m, lower_p, own_u))
    far_u, far_l = move(upper_m, 1, 1), move(lower_p, 1, -1)
    from_um, from_up, from_lm, from_lp = experts(
        (upper_m, upper_p, lower_m, lower_p), after=own_u, name="experts_near"
    )
    from_fu, from_fl = experts((far_u, far_l), after=came[-1], name="experts_far")
    back_up, back_lm = move(from_up, 1, 1), move(from_lm, 1, -1)
    back_fu, back_fl = move(from_fu, 1, -1), move(from_fl, 1, 1)
    from_um, from_lp = add_two(from_um, back_fu, from_lp, back_fl)
    back_um, back_lp = move(from_um, 1, -1), move(from_lp, 1, 1)
    wave_feats, wave_done = wave(
        lax.axis_index("section").astype(jnp.int32).reshape(1),
        held,
        came[-1],
        code_table,
        conv_weight,
        conv_bias[None],
        from_um,
        window,
    )
    kept, *sums = merge(
        hidden, (own_u, back_um, back_up), (own_l, back_lm, back_lp), wave_done
    )
    out = finish(kept, (move(sums[0], 0, -1), move(sums[1], 0, 1), move(sums[2], 0, 2)))
    return (jnp.transpose(out.reshape(steps, dialogs, width), (1, 0, 2)), wave_feats)


def solution(mesh):
    each = P(("expert", "section"), None, None)
    return jax.shard_map(
        shards,
        mesh=mesh,
        in_specs=(
            each,
            each,
            P(),
            P(),
            P(),
            P(),
            P(),
            P(),
            P(),
            each,
            each,
            P(("expert", "section")),
            P(),
            P(),
            each,
            P("expert", None, None),
            P("expert", None, None),
            P(("expert", "section"), None),
            P(("expert", "section")),
            P(None, "section"),
            P(None, "section"),
            P("section"),
        ),
        out_specs=(each, P("expert", None, "section")),
        check_vma=False,
    )
```

```python
import functools
import math

import jax
import jax.numpy as jnp
from jax import lax
from jax.experimental import pallas as pl
from jax.experimental.pallas import tpu as pltpu
from jax.sharding import PartitionSpec as P

epsilon = 1e-06
masked_score = -1e30
BF = jnp.bfloat16
F32 = jnp.float32
MIB = 1024 * 1024
GATE = 128


def vmem():
    return pl.BlockSpec(memory_space=pltpu.VMEM)


def smem():
    return pl.BlockSpec(memory_space=pltpu.SMEM)


def anywhere():
    return pl.BlockSpec(memory_space=pl.ANY)


def stay(array):
    return pltpu.with_memory_space_constraint(array, pltpu.HBM)


def dot_t(a, b):
    return lax.dot_general(a, b, (((1,), (1,)), ((), ())), preferred_element_type=F32)


def dot_n(a, b):
    return jnp.dot(a, b, preferred_element_type=F32)


def rms_norm(values, gain):
    mean_square = jnp.mean(values * values, axis=-1, keepdims=True)
    return values * lax.rsqrt(mean_square + epsilon) * gain


def dense_kernel(
    handed,
    picks,
    live,
    attn_gain_hbm,
    q_gain_hbm,
    k_gain_hbm,
    moe_gain_hbm,
    router_hbm,
    codec_hbm,
    w_text,
    w_q,
    w_kv,
    w_o,
    cache_k,
    cache_v,
    _after,
    hidden_out,
    sent_out,
    attn_gain,
    q_gain,
    k_gain,
    moe_gain,
    router_t,
    codec,
    text_buf,
    q_buf,
    kv_buf,
    o_buf,
    ck_buf,
    cv_buf,
    att,
    sems,
):
    steps, dialogs, wide = handed.shape
    rows = steps * dialogs
    width = text_buf.shape[1]
    head = q_gain.shape[1]
    heads = q_buf.shape[1] // head
    kv_heads = kv_buf.shape[1] // (2 * head)
    group = heads // kv_heads
    context = cache_k.shape[0] // dialogs
    parts = 4
    span = wide // parts

    def text_copy(i):
        place = pl.ds(i * span, span)
        return pltpu.make_async_copy(w_text.at[place], text_buf.at[place], sems.at[i])

    def whole_copies(pairs, first):
        return [
            pltpu.make_async_copy(source, target, sems.at[first + i])
            for i, (source, target) in enumerate(pairs)
        ]

    copies = [text_copy(i) for i in range(parts)]
    copies += whole_copies(
        ((w_q, q_buf), (w_kv, kv_buf), (cache_k, ck_buf), (cache_v, cv_buf), (w_o, o_buf)), parts
    )
    small = whole_copies(
        (
            (codec_hbm, codec),
            (attn_gain_hbm, attn_gain),
            (q_gain_hbm, q_gain),
            (k_gain_hbm, k_gain),
            (moe_gain_hbm, moe_gain),
            (router_hbm, router_t),
        ),
        parts + 5,
    )
    copies[0].start()
    for copy in small:
        copy.start()
    for copy in copies[1:]:
        copy.start()
    for copy in small:
        copy.wait()
    inputs = codec[...].reshape(rows, width).astype(F32)
    for i in range(parts):
        copies[i].wait()
        block = handed[:, :, i * span : (i + 1) * span].reshape(rows, span)
        inputs = inputs + dot_n(block, text_buf[i * span : (i + 1) * span, :])
    normed = rms_norm(inputs, attn_gain[...]).astype(BF)
    copies[parts].wait()
    q_all = dot_n(normed, q_buf[...])
    copies[parts + 1].wait()
    kv = dot_n(normed, kv_buf[...])
    queries = [rms_norm(q_all[:, h * head : (h + 1) * head], q_gain[...]) for h in range(heads)]
    keys = [
        rms_norm(kv[:, n * head : (n + 1) * head], k_gain[...]).astype(BF) for n in range(kv_heads)
    ]
    values = [
        kv[:, (kv_heads + n) * head : (kv_heads + n + 1) * head].astype(BF)
        for n in range(kv_heads)
    ]
    copies[parts + 2].wait()
    copies[parts + 3].wait()

    bunch = 8
    q_rows = group * steps * bunch
    span_c = bunch * context
    row = lax.broadcasted_iota(jnp.int32, (q_rows, span_c), 0)
    col = lax.broadcasted_iota(jnp.int32, (q_rows, span_c), 1)
    same = (row % bunch) == (col // context)
    row_n = lax.broadcasted_iota(jnp.int32, (q_rows, rows), 0)
    col_n = lax.broadcasted_iota(jnp.int32, (q_rows, rows), 1)
    causal = (col_n // dialogs) <= ((row_n // bunch) % steps)
    scale = 1.0 / math.sqrt(head)
    pairs = [(g, n) for g in range(dialogs // bunch) for n in range(kv_heads)]
    scored = []
    for g, n in pairs:
        pieces = [
            queries[n * group + j][t * dialogs + g * bunch : t * dialogs + (g + 1) * bunch]
            for j in range(group)
            for t in range(steps)
        ]
        q = jnp.concatenate(pieces, axis=0).astype(BF)
        old_k = ck_buf[g * span_c : (g + 1) * span_c, n * head : (n + 1) * head]
        scored.append((dot_t(q, old_k) * scale, dot_t(q, keys[n]) * scale))
    weighted = []
    for (g, n), (s_c, s_n) in zip(pairs, scored):
        ok_c = same & (live[:, g * span_c : (g + 1) * span_c] > 0)
        ok_n = causal & ((col_n % dialogs) == (row_n % bunch + g * bunch))
        s_c = jnp.where(ok_c, s_c, masked_score)
        s_n = jnp.where(ok_n, s_n, masked_score)
        top = jnp.maximum(
            jnp.max(s_c, axis=-1, keepdims=True), jnp.max(s_n, axis=-1, keepdims=True)
        )
        e_c = jnp.where(ok_c, jnp.exp(s_c - top), 0.0)
        e_n = jnp.where(ok_n, jnp.exp(s_n - top), 0.0)
        total = jnp.sum(e_c, axis=-1, keepdims=True) + jnp.sum(e_n, axis=-1, keepdims=True)
        weighted.append(((e_c / total).astype(BF), (e_n / total).astype(BF)))
    for (g, n), (w_c, w_n) in zip(pairs, weighted):
        old_v = cv_buf[g * span_c : (g + 1) * span_c, n * head : (n + 1) * head]
        out = dot_n(w_c, old_v) + dot_n(w_n, values[n])
        for j in range(group):
            for t in range(steps):
                at = (j * steps + t) * bunch
                h = n * group + j
                att[
                    t * dialogs + g * bunch : t * dialogs + (g + 1) * bunch,
                    h * head : (h + 1) * head,
                ] = out[at : at + bunch]

    copies[parts + 4].wait()
    hidden = inputs + dot_n(att[...].astype(BF), o_buf[...])
    hidden_out[...] = hidden
    routed = rms_norm(hidden, moe_gain[...]).astype(BF)
    experts = router_t.shape[0]
    logits = dot_t(router_t[...], routed)
    expert_id = lax.broadcasted_iota(jnp.int32, (experts, rows), 0)
    chosen = expert_id == picks[0:1, :]
    for k in range(1, picks.shape[0]):
        chosen = chosen | (expert_id == picks[k : k + 1, :])
    logits = jnp.where(chosen, logits, masked_score)
    raised = jnp.where(chosen, jnp.exp(logits - jnp.max(logits, axis=0, keepdims=True)), 0.0)
    gate = raised / jnp.sum(raised, axis=0, keepdims=True)
    high = gate.astype(BF).astype(F32)
    low = gate - high
    flat = jnp.concatenate([high, low, jnp.zeros((GATE - 2 * experts, rows), F32)], axis=0)
    flat = jnp.concatenate([flat, jnp.zeros((GATE, GATE - rows), F32)], axis=1)
    columns = jnp.transpose(flat)[:rows].astype(BF)
    sent_out[:, :width] = routed
    sent_out[:, width:] = columns


def dense(handed, picks, live, small, weights, caches, after):
    steps, dialogs, _ = handed.shape
    rows = steps * dialogs
    w_text, _, _, w_o = weights
    width = w_text.shape[1]
    copied = [*small, *weights, *caches]
    return pl.pallas_call(
        dense_kernel,
        out_shape=(
            jax.ShapeDtypeStruct((rows, width), F32),
            jax.ShapeDtypeStruct((rows, width + GATE), BF),
        ),
        in_specs=[vmem()] * 3 + [anywhere()] * (len(copied) + 1),
        out_specs=(vmem(),) * 2,
        scratch_shapes=[pltpu.VMEM(c.shape, c.dtype) for c in copied]
        + [pltpu.VMEM((rows, w_o.shape[0]), F32), pltpu.SemaphoreType.DMA((15,))],
        compiler_params=pltpu.CompilerParams(vmem_limit_bytes=24 * MIB),
        cost_estimate=pl.CostEstimate(
            flops=10 * rows * width * width, bytes_accessed=11 * MIB, transcendentals=400000
        ),
        name="dense",
    )(handed, picks, live, *(stay(c) for c in copied), after)


def silu(v):
    half = 0.5 * v
    return half + half * jnp.tanh(half)


def expert_kernel(count, ids, *refs):
    ins = refs[:count]
    sources = refs[count : count + 4]
    outs = refs[count + 5 : 2 * count + 5]
    gate_up, down, sems = refs[2 * count + 5 :]
    inner, width = sources[1].shape
    targets = (gate_up.at[0], down.at[0], gate_up.at[1], down.at[1])
    piece = width // 4
    first = [
        pltpu.make_async_copy(
            sources[0].at[pl.ds(i * piece, piece)],
            gate_up.at[0, pl.ds(i * piece, piece)],
            sems.at[4 + i],
        )
        for i in range(4)
    ]
    copies = [
        pltpu.make_async_copy(sources[i], targets[i], sems.at[i]) for i in range(len(sources))
    ]
    for copy in (*first, copies[2], copies[1], copies[3]):
        copy.start()
    x = jnp.concatenate([part[:, :width] for part in ins], axis=0)
    gates = jnp.concatenate([part[:, width:] for part in ins], axis=0).astype(F32)
    lane = lax.broadcasted_iota(jnp.int32, gates.shape, 1)
    acts = []
    for e in range(2):
        if e == 0:
            gu = 0.0
            for i in range(4):
                first[i].wait()
                place = slice(i * piece, (i + 1) * piece)
                gu = gu + dot_n(x[:, place], gate_up[0, place, :])
        else:
            copies[2].wait()
            gu = dot_n(x, gate_up[1])
        acts.append((silu(gu[:, :inner]) * gu[:, inner:]).astype(BF))
    total = None
    for e in range(2):
        mine = (lane == ids[e]) | (lane == ids[e] + ids[2])
        gate = jnp.sum(jnp.where(mine, gates, 0.0), axis=1, keepdims=True)
        copies[2 * e + 1].wait()
        out = dot_n(acts[e], down[e]) * gate
        total = out if total is None else total + out
    total = total.astype(BF)
    place = 0
    for out in outs:
        out[...] = total[place : place + out.shape[0]]
        place += out.shape[0]


def run_experts(arrays, ids, weights, after, name):
    count = len(arrays)
    inner, width = weights[1].shape
    rows = sum(a.shape[0] for a in arrays)
    return pl.pallas_call(
        functools.partial(expert_kernel, count),
        out_shape=tuple(jax.ShapeDtypeStruct((a.shape[0], width), BF) for a in arrays),
        in_specs=[smem()] + [vmem()] * count + [anywhere()] * 5,
        out_specs=tuple(vmem() for _ in arrays),
        scratch_shapes=[
            pltpu.VMEM((2, width, 2 * inner), BF),
            pltpu.VMEM((2, inner, width), BF),
            pltpu.SemaphoreType.DMA((8,)),
        ],
        compiler_params=pltpu.CompilerParams(vmem_limit_bytes=30 * MIB),
        cost_estimate=pl.CostEstimate(
            flops=2 * rows * 6 * inner * width,
            bytes_accessed=4 * rows * width + 12 * inner * width,
            transcendentals=rows * 2 * inner,
        ),
        name=name,
    )(ids, *arrays, stay(weights[0]), stay(weights[1]), weights[2], weights[3], after)


def join_kernel(*refs):
    *ins, _after, out = refs
    place = 0
    for part in ins:
        out[place : place + part.shape[0], :] = part[...]
        place += part.shape[0]


def join(arrays, after):
    rows = sum(a.shape[0] for a in arrays)
    return pl.pallas_call(
        join_kernel,
        out_shape=jax.ShapeDtypeStruct((rows, arrays[0].shape[1]), arrays[0].dtype),
        in_specs=[vmem()] * len(arrays) + [anywhere()],
        out_specs=vmem(),
        compiler_params=pltpu.CompilerParams(vmem_limit_bytes=16 * MIB),
        cost_estimate=pl.CostEstimate(flops=0, bytes_accessed=2 * MIB, transcendentals=0),
        name="join",
    )(*arrays, after)


def add_kernel(a, b, c, d, first, second):
    first[...] = (a[...].astype(F32) + b[...].astype(F32)).astype(BF)
    second[...] = (c[...].astype(F32) + d[...].astype(F32)).astype(BF)


def add_two(a, b, c, d):
    shape = jax.ShapeDtypeStruct(a.shape, BF)
    return pl.pallas_call(
        add_kernel,
        out_shape=(shape,) * 2,
        in_specs=[vmem()] * 4,
        out_specs=(vmem(),) * 2,
        compiler_params=pltpu.CompilerParams(vmem_limit_bytes=16 * MIB),
        cost_estimate=pl.CostEstimate(flops=2**18, bytes_accessed=2 * MIB, transcendentals=0),
        name="add_far",
    )(a, b, c, d)


def merge_kernel(hidden, own_t, t1, t2, own_b, b1, b2, _after, kept, *outs):
    size = hidden.shape[0]
    for k in range(1 + len(outs)):
        group = (own_t, t1, t2) if k < 2 else (own_b, b1, b2)
        place = slice(k % 2 * size, (k % 2 + 1) * size)
        total = sum(part[place, :].astype(F32) for part in group)
        if k == 0:
            kept[...] = hidden[...] + total
        else:
            outs[k - 1][...] = total.astype(BF)


def merge(hidden, upper, lower, after):
    size, width = hidden.shape
    return pl.pallas_call(
        merge_kernel,
        out_shape=(jax.ShapeDtypeStruct(hidden.shape, F32),)
        + (jax.ShapeDtypeStruct((size, width), BF),) * 3,
        in_specs=[vmem()] * 7 + [anywhere()],
        out_specs=(vmem(),) * 4,
        compiler_params=pltpu.CompilerParams(vmem_limit_bytes=16 * MIB),
        cost_estimate=pl.CostEstimate(flops=2**20, bytes_accessed=4 * MIB, transcendentals=0),
        name="merge",
    )(hidden, *upper, *lower, after)


def finish_kernel(kept, *refs):
    *parts, out = refs
    total = kept[...]
    for part in parts:
        total = total + part[...].astype(F32)
    out[...] = total.astype(BF)


def finish(kept, parts):
    return pl.pallas_call(
        finish_kernel,
        out_shape=jax.ShapeDtypeStruct(kept.shape, BF),
        in_specs=[vmem()] * (1 + len(parts)),
        out_specs=vmem(),
        compiler_params=pltpu.CompilerParams(vmem_limit_bytes=16 * MIB),
        cost_estimate=pl.CostEstimate(flops=2**19, bytes_accessed=2 * MIB, transcendentals=0),
        name="finish",
    )(kept, *parts)


def wave_kernel(
    window, owners, codes, table_hbm, taps_hbm, bias_hbm, _before, out, done, table, taps, bias, laid, result, sems
):
    blocks, dialogs, _ = codes.shape
    part, channels = table.shape[0], bias.shape[1]
    tap_count = taps.shape[0]
    frames_out = window - tap_count + 1
    copies = [
        pltpu.make_async_copy(taps_hbm, taps, sems.at[0]),
        pltpu.make_async_copy(bias_hbm, bias, sems.at[1]),
    ]
    for q in range(2):
        copies.append(
            pltpu.make_async_copy(
                table_hbm.at[pl.ds(q * part, part)],
                table.at[:, pl.ds(q * channels, channels)],
                sems.at[2 + q],
            )
        )
    for copy in copies:
        copy.start()
    for copy in copies:
        copy.wait()
    entry = lax.broadcasted_iota(jnp.int32, (dialogs, part), 1)

    def one_block(k, carry):
        block = codes[k]
        count = block[:, window : window + 1]
        hot, upper = [], []
        for p in range(window):
            code = block[:, p : p + 1]
            upper.append(code >= part)
            code = jnp.where(code >= part, code - part, code)
            code = jnp.where(p < count + tap_count - 1, code, -1)
            hot.append((entry == code).astype(F32).astype(BF))
        found = dot_n(jnp.concatenate(hot, axis=0), table[...])
        frames = []
        for p in range(window):
            rows = found[p * dialogs : (p + 1) * dialogs]
            frames.append(jnp.where(upper[p], rows[:, channels:], rows[:, :channels]))
        for t in range(frames_out):
            total = jnp.zeros((dialogs, channels), F32) + bias[...]
            for j in range(tap_count):
                total = total + taps[j : j + 1, :] * frames[t + j]
            laid[pl.ds(t, dialogs, stride=frames_out), :] = jnp.where(t < count, silu(total), 0.0)
        result[k] = laid[...].astype(BF).reshape(dialogs, frames_out, channels)
        return carry

    lax.fori_loop(0, blocks, one_block, 0)
    copies = [
        pltpu.make_async_copy(
            result.at[k], out.at[pl.ds(owners[k] * dialogs, dialogs)], sems.at[4 + k]
        )
        for k in range(blocks)
    ]
    for copy in copies:
        copy.start()
    for copy in copies:
        copy.wait()
    done[...] = jnp.zeros_like(done)


def wave(owners, codes, table, taps, bias, before, total, window):
    blocks, dialogs, _ = codes.shape
    entries, channels = table.shape
    frames_out = window - taps.shape[0] + 1
    rows = blocks * dialogs
    aliases = {}
    if before is None:
        before = codes
    else:
        aliases = {5: 0}
    return pl.pallas_call(
        functools.partial(wave_kernel, window),
        out_shape=(
            pltpu.HBM((total * dialogs, frames_out, channels), BF),
            jax.ShapeDtypeStruct((8, 128), F32),
        ),
        in_specs=[smem(), vmem()] + [anywhere()] * 4,
        out_specs=(anywhere(), vmem()),
        scratch_shapes=[
            pltpu.VMEM((entries // 2, 2 * channels), BF),
            pltpu.VMEM(taps.shape, F32),
            pltpu.VMEM(bias.shape, F32),
            pltpu.VMEM((dialogs * frames_out, channels), F32),
            pltpu.VMEM((blocks, dialogs, frames_out, channels), BF),
            pltpu.SemaphoreType.DMA((4 + blocks,)),
        ],
        input_output_aliases=aliases,
        compiler_params=pltpu.CompilerParams(vmem_limit_bytes=16 * MIB),
        cost_estimate=pl.CostEstimate(
            flops=2 * rows * window * entries * channels,
            bytes_accessed=2 * MIB,
            transcendentals=rows * frames_out * channels,
        ),
        name="wave",
    )(owners, codes, stay(table), stay(taps), stay(bias), before)


def expert_grid():
    chips = lax.axis_size("expert") // 2
    side = math.isqrt(chips)
    return side, chips // side


def swap_cores(array):
    return lax.ppermute(array, "expert", [(i, i ^ 1) for i in range(lax.axis_size("expert"))])


def move(array, stage, distance):
    nx, ny = expert_grid()
    route = []
    for x in range(nx):
        for y in range(ny):
            for core in range(2):
                if core == stage:
                    target = (x + distance) % nx * ny + y
                else:
                    target = x * ny + (y + distance) % ny
                route.append(((x * ny + y) * 2 + core, target * 2 + core))
    return lax.ppermute(array, "expert", route)


def along(array, distance):
    size = lax.axis_size("section")
    return lax.ppermute(array, "section", [(i, (i + distance) % size) for i in range(size)])


def shards(
    thinker_rows,
    codec_prev,
    w_text,
    attn_gain,
    w_q,
    key_value_weight,
    q_gain,
    k_gain,
    w_o,
    cache_k,
    value_cache,
    lengths,
    moe_gain,
    router,
    routes,
    w_gate_up,
    w_down,
    codes,
    counts,
    code_table,
    conv_weight,
    conv_bias,
):
    dialogs, steps, _ = thinker_rows.shape
    context = cache_k.shape[1]
    rows = dialogs * steps
    width = codec_prev.shape[2]
    handed = along(jnp.transpose(thinker_rows, (1, 0, 2)), 1)
    gu_a, down_a = w_gate_up[0], w_down[0]
    expert_weights = (gu_a, down_a, swap_cores(gu_a), swap_cores(down_a))
    mine = lax.axis_index("expert").astype(jnp.int32)
    ids = jnp.stack([mine, mine + 1 - 2 * (mine % 2), jnp.int32(router.shape[1])])
    picks = jnp.transpose(routes, (2, 1, 0)).reshape(routes.shape[2], rows)
    live = (jnp.arange(context)[None, :] < lengths[:, None]).astype(F32)
    window = codes.shape[1]
    held = jnp.concatenate(
        [codes, counts[:, None], jnp.zeros((dialogs, 15 - window), jnp.int32)], axis=1
    )[None]
    held = jnp.concatenate([held, along(held, 1), along(held, -1), along(held, -2)], axis=0)
    held_far = along(held, 4)
    sections = lax.axis_size("section")
    place = lax.axis_index("section").astype(jnp.int32)
    wave_part = functools.partial(
        wave,
        table=code_table,
        taps=conv_weight,
        bias=conv_bias[None],
        total=sections,
        window=window,
    )

    def owners(shifts):
        return jnp.stack([(place + shift) % sections for shift in shifts])

    hidden, sent = dense(
        handed,
        picks,
        live.reshape(1, dialogs * context),
        (
            attn_gain[None],
            q_gain[None],
            k_gain[None],
            moe_gain[None],
            jnp.transpose(router),
            jnp.transpose(codec_prev, (1, 0, 2)),
        ),
        (w_text, w_q, key_value_weight, w_o),
        [c.reshape(dialogs * context, c.shape[2]) for c in (cache_k, value_cache)],
        held,
    )
    wave_feats, wave_done = wave_part(owners((0, 7, 1, 2)), held, before=None)
    sent_m, sent_p, sent_x = move(sent, 0, 1), move(sent, 0, -1), move(sent, 0, 2)
    upper = join((sent, sent_m), sent)
    upper_m, upper_p = move(upper, 1, 1), move(upper, 1, -1)
    lower = join((sent_p, sent_x), wave_done)
    lower_m, lower_p = move(lower, 1, 1), move(lower, 1, -1)
    experts = functools.partial(run_experts, ids=ids, weights=expert_weights)
    own_u, own_l = experts((upper, lower), after=lower, name="experts_own")
    upper_m, lower_p, own_u = lax.optimization_barrier((upper_m, lower_p, own_u))
    far_u, far_l = move(upper_m, 1, 1), move(lower_p, 1, -1)
    from_um, from_up, from_lm, from_lp = experts(
        (upper_m, upper_p, lower_m, lower_p), after=own_u, name="experts_near"
    )
    from_fu, from_fl = experts((far_u, far_l), after=own_u, name="experts_far")
    back_up, back_lm = move(from_up, 1, 1), move(from_lm, 1, -1)
    back_fu, back_fl = move(from_fu, 1, -1), move(from_fl, 1, 1)
    from_um, from_lp = add_two(from_um, back_fu, from_lp, back_fl)
    back_um, back_lp = move(from_um, 1, -1), move(from_lp, 1, 1)
    wave_feats, wave_done = wave_part(owners((4, 3, 5, 6)), held_far, before=wave_feats)
    kept, *sums = merge(
        hidden, (own_u, back_um, back_up), (own_l, back_lm, back_lp), wave_done
    )
    out = finish(kept, (move(sums[0], 0, -1), move(sums[1], 0, 1), move(sums[2], 0, 2)))
    return (jnp.transpose(out.reshape(steps, dialogs, width), (1, 0, 2)), wave_feats)


def solution(mesh):
    each = P(("expert", "section"), None, None)
    return jax.shard_map(
        shards,
        mesh=mesh,
        in_specs=(
            each,
            each,
            P(),
            P(),
            P(),
            P(),
            P(),
            P(),
            P(),
            each,
            each,
            P(("expert", "section")),
            P(),
            P(),
            each,
            P("expert", None, None),
            P("expert", None, None),
            P(("expert", "section"), None),
            P(("expert", "section")),
            P(None, "section"),
            P(None, "section"),
            P("section"),
        ),
        out_specs=(each, P("expert", None, "section")),
        check_vma=False,
    )
```

```python
import functools
import math

import jax
import jax.numpy as jnp
from jax import lax
from jax.experimental import pallas as pl
from jax.experimental.pallas import tpu as pltpu
from jax.sharding import PartitionSpec as P

epsilon = 1e-06
masked_score = -1e30
BF = jnp.bfloat16
F32 = jnp.float32
MIB = 1024 * 1024
GATE = 128


def vmem():
    return pl.BlockSpec(memory_space=pltpu.VMEM)


def smem():
    return pl.BlockSpec(memory_space=pltpu.SMEM)


def anywhere():
    return pl.BlockSpec(memory_space=pl.ANY)


def stay(array):
    return pltpu.with_memory_space_constraint(array, pltpu.HBM)


def pin(array):
    return pltpu.with_memory_space_constraint(array, pltpu.VMEM)


def dot_t(a, b):
    return lax.dot_general(a, b, (((1,), (1,)), ((), ())), preferred_element_type=F32)


def dot_n(a, b):
    return jnp.dot(a, b, preferred_element_type=F32)


def rms_norm(values, gain):
    mean_square = jnp.mean(values * values, axis=-1, keepdims=True)
    return values * lax.rsqrt(mean_square + epsilon) * gain


def dense_kernel(
    handed,
    picks,
    live,
    attn_gain_hbm,
    q_gain_hbm,
    k_gain_hbm,
    moe_gain_hbm,
    router_hbm,
    codec_hbm,
    w_text,
    w_q,
    w_kv,
    w_o,
    cache_k,
    cache_v,
    _after_codes,
    _after_numbers,
    hidden_out,
    sent_out,
    attn_gain,
    q_gain,
    k_gain,
    moe_gain,
    router_t,
    codec,
    text_buf,
    q_buf,
    kv_buf,
    o_buf,
    ck_buf,
    cv_buf,
    att,
    sems,
):
    steps, dialogs, wide = handed.shape
    rows = steps * dialogs
    width = text_buf.shape[1]
    head = q_gain.shape[1]
    heads = q_buf.shape[1] // head
    kv_heads = kv_buf.shape[1] // (2 * head)
    group = heads // kv_heads
    context = cache_k.shape[0] // dialogs
    parts = 4
    span = wide // parts

    def text_copy(i):
        place = pl.ds(i * span, span)
        return pltpu.make_async_copy(w_text.at[place], text_buf.at[place], sems.at[i])

    def whole_copies(pairs, first):
        return [
            pltpu.make_async_copy(source, target, sems.at[first + i])
            for i, (source, target) in enumerate(pairs)
        ]

    copies = [text_copy(i) for i in range(parts)]
    copies += whole_copies(
        ((w_q, q_buf), (w_kv, kv_buf), (cache_k, ck_buf), (cache_v, cv_buf), (w_o, o_buf)), parts
    )
    small = whole_copies(
        (
            (codec_hbm, codec),
            (attn_gain_hbm, attn_gain),
            (q_gain_hbm, q_gain),
            (k_gain_hbm, k_gain),
            (moe_gain_hbm, moe_gain),
            (router_hbm, router_t),
        ),
        parts + 5,
    )
    copies[0].start()
    for copy in small:
        copy.start()
    for copy in copies[1:]:
        copy.start()
    for copy in small:
        copy.wait()
    inputs = codec[...].reshape(rows, width).astype(F32)
    for i in range(parts):
        copies[i].wait()
        block = handed[:, :, i * span : (i + 1) * span].reshape(rows, span)
        inputs = inputs + dot_n(block, text_buf[i * span : (i + 1) * span, :])
    normed = rms_norm(inputs, attn_gain[...]).astype(BF)
    copies[parts].wait()
    q_all = dot_n(normed, q_buf[...])
    copies[parts + 1].wait()
    kv = dot_n(normed, kv_buf[...])
    queries = [rms_norm(q_all[:, h * head : (h + 1) * head], q_gain[...]) for h in range(heads)]
    keys = [
        rms_norm(kv[:, n * head : (n + 1) * head], k_gain[...]).astype(BF) for n in range(kv_heads)
    ]
    values = [
        kv[:, (kv_heads + n) * head : (kv_heads + n + 1) * head].astype(BF)
        for n in range(kv_heads)
    ]
    copies[parts + 2].wait()
    copies[parts + 3].wait()

    bunch = 8
    q_rows = group * steps * bunch
    span_c = bunch * context
    row = lax.broadcasted_iota(jnp.int32, (q_rows, span_c), 0)
    col = lax.broadcasted_iota(jnp.int32, (q_rows, span_c), 1)
    same = (row % bunch) == (col // context)
    row_n = lax.broadcasted_iota(jnp.int32, (q_rows, rows), 0)
    col_n = lax.broadcasted_iota(jnp.int32, (q_rows, rows), 1)
    causal = (col_n // dialogs) <= ((row_n // bunch) % steps)
    scale = 1.0 / math.sqrt(head)
    pairs = [(g, n) for g in range(dialogs // bunch) for n in range(kv_heads)]
    scored = []
    for g, n in pairs:
        pieces = [
            queries[n * group + j][t * dialogs + g * bunch : t * dialogs + (g + 1) * bunch]
            for j in range(group)
            for t in range(steps)
        ]
        q = jnp.concatenate(pieces, axis=0).astype(BF)
        old_k = ck_buf[g * span_c : (g + 1) * span_c, n * head : (n + 1) * head]
        scored.append((dot_t(q, old_k) * scale, dot_t(q, keys[n]) * scale))
    weighted = []
    for (g, n), (s_c, s_n) in zip(pairs, scored):
        ok_c = same & (live[:, g * span_c : (g + 1) * span_c] > 0)
        ok_n = causal & ((col_n % dialogs) == (row_n % bunch + g * bunch))
        s_c = jnp.where(ok_c, s_c, masked_score)
        s_n = jnp.where(ok_n, s_n, masked_score)
        top = jnp.maximum(
            jnp.max(s_c, axis=-1, keepdims=True), jnp.max(s_n, axis=-1, keepdims=True)
        )
        e_c = jnp.where(ok_c, jnp.exp(s_c - top), 0.0)
        e_n = jnp.where(ok_n, jnp.exp(s_n - top), 0.0)
        total = jnp.sum(e_c, axis=-1, keepdims=True) + jnp.sum(e_n, axis=-1, keepdims=True)
        weighted.append(((e_c / total).astype(BF), (e_n / total).astype(BF)))
    for (g, n), (w_c, w_n) in zip(pairs, weighted):
        old_v = cv_buf[g * span_c : (g + 1) * span_c, n * head : (n + 1) * head]
        out = dot_n(w_c, old_v) + dot_n(w_n, values[n])
        for j in range(group):
            for t in range(steps):
                at = (j * steps + t) * bunch
                h = n * group + j
                att[
                    t * dialogs + g * bunch : t * dialogs + (g + 1) * bunch,
                    h * head : (h + 1) * head,
                ] = out[at : at + bunch]

    copies[parts + 4].wait()
    hidden = inputs + dot_n(att[...].astype(BF), o_buf[...])
    hidden_out[...] = hidden
    routed = rms_norm(hidden, moe_gain[...]).astype(BF)
    experts = router_t.shape[0]
    logits = dot_t(router_t[...], routed)
    expert_id = lax.broadcasted_iota(jnp.int32, (experts, rows), 0)
    chosen = expert_id == picks[0:1, :]
    for k in range(1, picks.shape[0]):
        chosen = chosen | (expert_id == picks[k : k + 1, :])
    logits = jnp.where(chosen, logits, masked_score)
    raised = jnp.where(chosen, jnp.exp(logits - jnp.max(logits, axis=0, keepdims=True)), 0.0)
    gate = raised / jnp.sum(raised, axis=0, keepdims=True)
    high = gate.astype(BF).astype(F32)
    low = gate - high
    flat = jnp.concatenate([high, low, jnp.zeros((GATE - 2 * experts, rows), F32)], axis=0)
    flat = jnp.concatenate([flat, jnp.zeros((GATE, GATE - rows), F32)], axis=1)
    columns = jnp.transpose(flat)[:rows].astype(BF)
    sent_out[:, :width] = routed
    sent_out[:, width:] = columns


def dense(handed, picks, live, small, weights, caches, after):
    steps, dialogs, _ = handed.shape
    rows = steps * dialogs
    w_text, _, _, w_o = weights
    width = w_text.shape[1]
    copied = [*small, *weights, *caches]
    return pl.pallas_call(
        dense_kernel,
        out_shape=(
            jax.ShapeDtypeStruct((rows, width), F32),
            jax.ShapeDtypeStruct((rows, width + GATE), BF),
        ),
        in_specs=[vmem()] * 3 + [anywhere()] * (len(copied) + len(after)),
        out_specs=(vmem(),) * 2,
        scratch_shapes=[pltpu.VMEM(c.shape, c.dtype) for c in copied]
        + [pltpu.VMEM((rows, w_o.shape[0]), F32), pltpu.SemaphoreType.DMA((15,))],
        compiler_params=pltpu.CompilerParams(vmem_limit_bytes=24 * MIB),
        cost_estimate=pl.CostEstimate(
            flops=10 * rows * width * width, bytes_accessed=11 * MIB, transcendentals=400000
        ),
        name="dense",
    )(handed, picks, live, *(stay(c) for c in copied), *after)


def silu(v):
    half = 0.5 * v
    return half + half * jnp.tanh(half)


def stage_kernel(count, *refs):
    sources, targets, sems = refs[:count], refs[count + 1 : 2 * count + 1], refs[-1]
    copies = [pltpu.make_async_copy(sources[i], targets[i], sems.at[i]) for i in range(count)]
    for copy in copies:
        copy.start()
    for copy in copies:
        copy.wait()


def stage(weights, after):
    count = len(weights)
    return pl.pallas_call(
        functools.partial(stage_kernel, count),
        out_shape=tuple(pltpu.VMEM(w.shape, w.dtype) for w in weights),
        in_specs=[anywhere()] * (count + 1),
        out_specs=(vmem(),) * count,
        scratch_shapes=[pltpu.SemaphoreType.DMA((count,))],
        compiler_params=pltpu.CompilerParams(vmem_limit_bytes=8 * MIB),
        cost_estimate=pl.CostEstimate(flops=0, bytes_accessed=10 * MIB, transcendentals=0),
        name="stage",
    )(*weights, after)


def expert_kernel(count, ids, *refs):
    ins = refs[:count]
    weights = refs[count : count + 4]
    outs = refs[count + 5 :]
    inner, width = weights[1].shape
    x = jnp.concatenate([part[:, :width] for part in ins], axis=0)
    gates = jnp.concatenate([part[:, width:] for part in ins], axis=0).astype(F32)
    lane = lax.broadcasted_iota(jnp.int32, gates.shape, 1)
    acts = []
    for e in range(2):
        gu = dot_n(x, weights[2 * e][...])
        acts.append((silu(gu[:, :inner]) * gu[:, inner:]).astype(BF))
    total = None
    for e in range(2):
        mine = (lane == ids[e]) | (lane == ids[e] + ids[2])
        gate = jnp.sum(jnp.where(mine, gates, 0.0), axis=1, keepdims=True)
        out = dot_n(acts[e], weights[2 * e + 1][...]) * gate
        total = out if total is None else total + out
    total = total.astype(BF)
    place = 0
    for out in outs:
        out[...] = total[place : place + out.shape[0]]
        place += out.shape[0]


def run_experts(arrays, ids, weights, after, name):
    count = len(arrays)
    inner, width = weights[1].shape
    rows = sum(a.shape[0] for a in arrays)
    return pl.pallas_call(
        functools.partial(expert_kernel, count),
        out_shape=tuple(pltpu.VMEM((a.shape[0], width), BF) for a in arrays),
        in_specs=[smem()] + [vmem()] * (count + 4) + [anywhere()],
        out_specs=tuple(vmem() for _ in arrays),
        compiler_params=pltpu.CompilerParams(vmem_limit_bytes=24 * MIB),
        cost_estimate=pl.CostEstimate(
            flops=2 * rows * 6 * inner * width,
            bytes_accessed=4 * rows * width + 12 * inner * width,
            transcendentals=rows * 2 * inner,
        ),
        name=name,
    )(ids, *arrays, *(pin(w) for w in weights), after)


def join_kernel(*refs):
    *ins, _after, out = refs
    place = 0
    for part in ins:
        out[place : place + part.shape[0], :] = part[...]
        place += part.shape[0]


def join(arrays, after):
    rows = sum(a.shape[0] for a in arrays)
    return pl.pallas_call(
        join_kernel,
        out_shape=jax.ShapeDtypeStruct((rows, arrays[0].shape[1]), arrays[0].dtype),
        in_specs=[vmem()] * len(arrays) + [anywhere()],
        out_specs=vmem(),
        compiler_params=pltpu.CompilerParams(vmem_limit_bytes=16 * MIB),
        cost_estimate=pl.CostEstimate(flops=0, bytes_accessed=2 * MIB, transcendentals=0),
        name="join",
    )(*arrays, after)


def add_kernel(a, b, c, d, first, second):
    first[...] = (a[...].astype(F32) + b[...].astype(F32)).astype(BF)
    second[...] = (c[...].astype(F32) + d[...].astype(F32)).astype(BF)


def add_two(a, b, c, d):
    shape = jax.ShapeDtypeStruct(a.shape, BF)
    return pl.pallas_call(
        add_kernel,
        out_shape=(shape,) * 2,
        in_specs=[vmem()] * 4,
        out_specs=(vmem(),) * 2,
        compiler_params=pltpu.CompilerParams(vmem_limit_bytes=16 * MIB),
        cost_estimate=pl.CostEstimate(flops=2**18, bytes_accessed=2 * MIB, transcendentals=0),
        name="add_far",
    )(a, b, c, d)


def merge_kernel(hidden, own_t, t1, t2, own_b, b1, b2, _after, kept, *outs):
    size = hidden.shape[0]
    for k in range(1 + len(outs)):
        group = (own_t, t1, t2) if k < 2 else (own_b, b1, b2)
        place = slice(k % 2 * size, (k % 2 + 1) * size)
        total = sum(part[place, :].astype(F32) for part in group)
        if k == 0:
            kept[...] = hidden[...] + total
        else:
            outs[k - 1][...] = total.astype(BF)


def merge(hidden, upper, lower, after):
    size, width = hidden.shape
    return pl.pallas_call(
        merge_kernel,
        out_shape=(jax.ShapeDtypeStruct(hidden.shape, F32),)
        + (jax.ShapeDtypeStruct((size, width), BF),) * 3,
        in_specs=[vmem()] * 7 + [anywhere()],
        out_specs=(vmem(),) * 4,
        compiler_params=pltpu.CompilerParams(vmem_limit_bytes=16 * MIB),
        cost_estimate=pl.CostEstimate(flops=2**20, bytes_accessed=4 * MIB, transcendentals=0),
        name="merge",
    )(hidden, *upper, *lower, after)


def finish_kernel(kept, *refs):
    *parts, out = refs
    total = kept[...]
    for part in parts:
        total = total + part[...].astype(F32)
    out[...] = total.astype(BF)


def finish(kept, parts):
    return pl.pallas_call(
        finish_kernel,
        out_shape=jax.ShapeDtypeStruct(kept.shape, BF),
        in_specs=[vmem()] * (1 + len(parts)),
        out_specs=vmem(),
        compiler_params=pltpu.CompilerParams(vmem_limit_bytes=16 * MIB),
        cost_estimate=pl.CostEstimate(flops=2**19, bytes_accessed=2 * MIB, transcendentals=0),
        name="finish",
    )(kept, *parts)


def wave_kernel(
    window, first, owners, codes, table_hbm, taps_hbm, bias_hbm, _before, out, done, table, taps, bias, rows_of, laid, result, sems
):
    dialogs = laid.shape[0] // (window - taps.shape[0] + 1)
    blocks = codes.shape[1] // dialogs
    part, channels = table.shape[0], bias.shape[1]
    tap_count = taps.shape[0]
    frames_out = window - tap_count + 1
    copies = [
        pltpu.make_async_copy(taps_hbm, taps, sems.at[0]),
        pltpu.make_async_copy(bias_hbm, bias, sems.at[1]),
    ]
    for q in range(2):
        copies.append(
            pltpu.make_async_copy(
                table_hbm.at[pl.ds(q * part, part)],
                table.at[:, pl.ds(q * channels, channels)],
                sems.at[2 + q],
            )
        )
    for copy in copies:
        copy.start()
    for copy in copies:
        copy.wait()
    entry = lax.broadcasted_iota(jnp.int32, (dialogs, part), 1)
    lanes = codes.shape[1]
    square = jnp.concatenate(
        [codes[...].astype(F32), jnp.zeros((lanes - codes.shape[0], lanes), F32)], axis=0
    )
    rows_of[...] = jnp.transpose(square).astype(jnp.int32)

    def one_block(k, carry):
        block = rows_of[pl.ds(pl.multiple_of(k * dialogs, dialogs), dialogs), :]
        count = block[:, window : window + 1]
        hot, upper = [], []
        for p in range(window):
            code = block[:, p : p + 1]
            upper.append(code >= part)
            code = jnp.where(code >= part, code - part, code)
            code = jnp.where(p < count + tap_count - 1, code, -1)
            hot.append((entry == code).astype(F32).astype(BF))
        found = dot_n(jnp.concatenate(hot, axis=0), table[...])
        frames = []
        for p in range(window):
            rows = found[p * dialogs : (p + 1) * dialogs]
            frames.append(jnp.where(upper[p], rows[:, channels:], rows[:, :channels]))
        for t in range(frames_out):
            total = jnp.zeros((dialogs, channels), F32) + bias[...]
            for j in range(tap_count):
                total = total + taps[j : j + 1, :] * frames[t + j]
            laid[pl.ds(t, dialogs, stride=frames_out), :] = jnp.where(t < count, silu(total), 0.0)
        result[k] = laid[...].astype(BF).reshape(dialogs, frames_out, channels)
        return carry

    lax.fori_loop(0, blocks, one_block, 0)
    copies = [
        pltpu.make_async_copy(
            result.at[k], out.at[pl.ds(owners[first + k] * dialogs, dialogs)], sems.at[4 + k]
        )
        for k in range(blocks)
    ]
    for copy in copies:
        copy.start()
    for copy in copies:
        copy.wait()
    done[...] = jnp.zeros_like(done)


def wave(numbers, codes, table, taps, bias, before, total, window, dialogs, first):
    lanes = codes.shape[1]
    blocks = lanes // dialogs
    entries, channels = table.shape
    frames_out = window - taps.shape[0] + 1
    rows = blocks * dialogs
    aliases = {}
    if before is None:
        before = codes
    else:
        aliases = {5: 0}
    return pl.pallas_call(
        functools.partial(wave_kernel, window, first),
        out_shape=(
            pltpu.HBM((total * dialogs, frames_out, channels), BF),
            jax.ShapeDtypeStruct((8, 128), F32),
        ),
        in_specs=[smem(), vmem()] + [anywhere()] * 4,
        out_specs=(anywhere(), vmem()),
        scratch_shapes=[
            pltpu.VMEM((entries // 2, 2 * channels), BF),
            pltpu.VMEM(taps.shape, F32),
            pltpu.VMEM(bias.shape, F32),
            pltpu.VMEM((lanes, lanes), jnp.int32),
            pltpu.VMEM((dialogs * frames_out, channels), F32),
            pltpu.VMEM((blocks, dialogs, frames_out, channels), BF),
            pltpu.SemaphoreType.DMA((4 + blocks,)),
        ],
        input_output_aliases=aliases,
        compiler_params=pltpu.CompilerParams(vmem_limit_bytes=16 * MIB),
        cost_estimate=pl.CostEstimate(
            flops=2 * rows * window * entries * channels,
            bytes_accessed=2 * MIB,
            transcendentals=rows * frames_out * channels,
        ),
        name="wave",
    )(numbers, codes, stay(table), stay(taps), stay(bias), before)


def expert_grid():
    chips = lax.axis_size("expert") // 2
    side = math.isqrt(chips)
    return side, chips // side


def swap_cores(array):
    return lax.ppermute(array, "expert", [(i, i ^ 1) for i in range(lax.axis_size("expert"))])


def move(array, stage, distance):
    nx, ny = expert_grid()
    route = []
    for x in range(nx):
        for y in range(ny):
            for core in range(2):
                if core == stage:
                    target = (x + distance) % nx * ny + y
                else:
                    target = x * ny + (y + distance) % ny
                route.append(((x * ny + y) * 2 + core, target * 2 + core))
    return lax.ppermute(array, "expert", route)


def along(array, distance):
    size = lax.axis_size("section")
    return lax.ppermute(array, "section", [(i, (i + distance) % size) for i in range(size)])


def shards(
    thinker_rows,
    codec_prev,
    w_text,
    attn_gain,
    w_q,
    key_value_weight,
    q_gain,
    k_gain,
    w_o,
    cache_k,
    value_cache,
    lengths,
    moe_gain,
    router,
    routes,
    w_gate_up,
    w_down,
    codes,
    counts,
    code_table,
    conv_weight,
    conv_bias,
):
    dialogs, steps, _ = thinker_rows.shape
    context = cache_k.shape[1]
    rows = dialogs * steps
    width = codec_prev.shape[2]
    handed = along(jnp.transpose(thinker_rows, (1, 0, 2)), 1)
    gu_a, down_a = w_gate_up[0], w_down[0]
    gu_b, down_b = swap_cores(gu_a), swap_cores(down_a)
    mine = lax.axis_index("expert").astype(jnp.int32)
    picks = jnp.transpose(routes, (2, 1, 0)).reshape(routes.shape[2], rows)
    live = (jnp.arange(context)[None, :] < lengths[:, None]).astype(F32)
    window = codes.shape[1]
    held = jnp.concatenate(
        [codes.T, counts[None], jnp.zeros((15 - window, dialogs), jnp.int32)], axis=0
    )
    held = jnp.concatenate([held, along(held, 1), along(held, -1), along(held, -2)], axis=1)
    held_far = along(held, 4)
    sections = lax.axis_size("section")
    place = lax.axis_index("section").astype(jnp.int32)
    wave_part = functools.partial(
        wave,
        table=code_table,
        taps=conv_weight,
        bias=conv_bias[None],
        total=sections,
        window=window,
        dialogs=dialogs,
    )
    numbers = [mine, mine + 1 - 2 * (mine % 2), jnp.int32(router.shape[1])]
    numbers += [(place + shift) % sections for shift in (0, 7, 1, 2, 4, 3, 5, 6)]
    numbers = jnp.stack(numbers)
    hidden, sent = dense(
        handed,
        picks,
        live.reshape(1, dialogs * context),
        (
            attn_gain[None],
            q_gain[None],
            k_gain[None],
            moe_gain[None],
            jnp.transpose(router),
            jnp.transpose(codec_prev, (1, 0, 2)),
        ),
        (w_text, w_q, key_value_weight, w_o),
        [c.reshape(dialogs * context, c.shape[2]) for c in (cache_k, value_cache)],
        (held, numbers),
    )
    sent_m, sent_p, sent_x = move(sent, 0, 1), move(sent, 0, -1), move(sent, 0, 2)
    expert_weights = stage((stay(gu_a), stay(down_a), gu_b, down_b), sent)
    upper = join((sent, sent_m), sent)
    upper_m, upper_p = move(upper, 1, 1), move(upper, 1, -1)
    lower = join((sent_p, sent_x), expert_weights[1])
    lower_m, lower_p = move(lower, 1, 1), move(lower, 1, -1)
    experts = functools.partial(run_experts, ids=numbers, weights=expert_weights)
    own_u, own_l = experts((upper, lower), after=lower, name="experts_own")
    upper_m, lower_p, own_u = lax.optimization_barrier((upper_m, lower_p, own_u))
    far_u, far_l = move(upper_m, 1, 1), move(lower_p, 1, -1)
    from_um, from_up, from_lm, from_lp = experts(
        (upper_m, upper_p, lower_m, lower_p), after=own_u, name="experts_near"
    )
    wave_feats, wave_done = wave_part(numbers, held, before=None, first=3)
    from_fu, from_fl = experts((far_u, far_l), after=wave_done, name="experts_far")
    back_up, back_lm = move(from_up, 1, 1), move(from_lm, 1, -1)
    back_fu, back_fl = move(from_fu, 1, -1), move(from_fl, 1, 1)
    from_um, from_lp = add_two(from_um, back_fu, from_lp, back_fl)
    back_um, back_lp = move(from_um, 1, -1), move(from_lp, 1, 1)
    wave_feats, wave_done = wave_part(numbers, held_far, before=wave_feats, first=7)
    kept, *sums = merge(
        hidden, (own_u, back_um, back_up), (own_l, back_lm, back_lp), wave_done
    )
    out = finish(kept, (move(sums[0], 0, -1), move(sums[1], 0, 1), move(sums[2], 0, 2)))
    return (jnp.transpose(out.reshape(steps, dialogs, width), (1, 0, 2)), wave_feats)


def solution(mesh):
    each = P(("expert", "section"), None, None)
    return jax.shard_map(
        shards,
        mesh=mesh,
        in_specs=(
            each,
            each,
            P(),
            P(),
            P(),
            P(),
            P(),
            P(),
            P(),
            each,
            each,
            P(("expert", "section")),
            P(),
            P(),
            each,
            P("expert", None, None),
            P("expert", None, None),
            P(("expert", "section"), None),
            P(("expert", "section")),
            P(None, "section"),
            P(None, "section"),
            P("section"),
        ),
        out_specs=(each, P("expert", None, "section")),
        check_vma=False,
    )
```

```python
import functools
import math

import jax
import jax.numpy as jnp
from jax import lax
from jax.experimental import pallas as pl
from jax.experimental.pallas import tpu as pltpu
from jax.sharding import PartitionSpec as P

epsilon = 1e-06
masked_score = -1e30
BF = jnp.bfloat16
F32 = jnp.float32
MIB = 1024 * 1024
GATE = 128


def vmem():
    return pl.BlockSpec(memory_space=pltpu.VMEM)


def smem():
    return pl.BlockSpec(memory_space=pltpu.SMEM)


def anywhere():
    return pl.BlockSpec(memory_space=pl.ANY)


def stay(array):
    return pltpu.with_memory_space_constraint(array, pltpu.HBM)


def pin(array):
    return pltpu.with_memory_space_constraint(array, pltpu.VMEM)


def dot_t(a, b):
    return lax.dot_general(a, b, (((1,), (1,)), ((), ())), preferred_element_type=F32)


def dot_n(a, b):
    return jnp.dot(a, b, preferred_element_type=F32)


def rms_norm(values, gain):
    mean_square = jnp.mean(values * values, axis=-1, keepdims=True)
    return values * lax.rsqrt(mean_square + epsilon) * gain


def dense_kernel(
    handed,
    picks,
    live,
    attn_gain_hbm,
    q_gain_hbm,
    k_gain_hbm,
    moe_gain_hbm,
    router_hbm,
    codec_hbm,
    w_text,
    w_q,
    w_kv,
    w_o,
    cache_k,
    cache_v,
    _after_a,
    _after_b,
    _after_c,
    _after_numbers,
    hidden_out,
    sent_out,
    attn_gain,
    q_gain,
    k_gain,
    moe_gain,
    router_t,
    codec,
    text_buf,
    q_buf,
    kv_buf,
    o_buf,
    ck_buf,
    cv_buf,
    att,
    sems,
):
    steps, dialogs, wide = handed.shape
    rows = steps * dialogs
    width = text_buf.shape[1]
    head = q_gain.shape[1]
    heads = q_buf.shape[1] // head
    kv_heads = kv_buf.shape[1] // (2 * head)
    group = heads // kv_heads
    context = cache_k.shape[0] // dialogs
    parts = 4
    span = wide // parts

    def text_copy(i):
        place = pl.ds(i * span, span)
        return pltpu.make_async_copy(w_text.at[place], text_buf.at[place], sems.at[i])

    def whole_copies(pairs, first):
        return [
            pltpu.make_async_copy(source, target, sems.at[first + i])
            for i, (source, target) in enumerate(pairs)
        ]

    copies = [text_copy(i) for i in range(parts)]
    copies += whole_copies(
        ((w_q, q_buf), (w_kv, kv_buf), (cache_k, ck_buf), (cache_v, cv_buf), (w_o, o_buf)), parts
    )
    small = whole_copies(
        (
            (codec_hbm, codec),
            (attn_gain_hbm, attn_gain),
            (q_gain_hbm, q_gain),
            (k_gain_hbm, k_gain),
            (moe_gain_hbm, moe_gain),
            (router_hbm, router_t),
        ),
        parts + 5,
    )
    copies[0].start()
    for copy in small:
        copy.start()
    for copy in copies[1:]:
        copy.start()
    for copy in small:
        copy.wait()
    inputs = codec[...].reshape(rows, width).astype(F32)
    for i in range(parts):
        copies[i].wait()
        block = handed[:, :, i * span : (i + 1) * span].reshape(rows, span)
        inputs = inputs + dot_n(block, text_buf[i * span : (i + 1) * span, :])
    normed = rms_norm(inputs, attn_gain[...]).astype(BF)
    copies[parts].wait()
    q_all = dot_n(normed, q_buf[...])
    copies[parts + 1].wait()
    kv = dot_n(normed, kv_buf[...])
    queries = [rms_norm(q_all[:, h * head : (h + 1) * head], q_gain[...]) for h in range(heads)]
    keys = [
        rms_norm(kv[:, n * head : (n + 1) * head], k_gain[...]).astype(BF) for n in range(kv_heads)
    ]
    values = [
        kv[:, (kv_heads + n) * head : (kv_heads + n + 1) * head].astype(BF)
        for n in range(kv_heads)
    ]
    copies[parts + 2].wait()
    copies[parts + 3].wait()

    bunch = 8
    q_rows = group * steps * bunch
    span_c = bunch * context
    row = lax.broadcasted_iota(jnp.int32, (q_rows, span_c), 0)
    col = lax.broadcasted_iota(jnp.int32, (q_rows, span_c), 1)
    same = (row % bunch) == (col // context)
    row_n = lax.broadcasted_iota(jnp.int32, (q_rows, rows), 0)
    col_n = lax.broadcasted_iota(jnp.int32, (q_rows, rows), 1)
    causal = (col_n // dialogs) <= ((row_n // bunch) % steps)
    scale = 1.0 / math.sqrt(head)
    pairs = [(g, n) for g in range(dialogs // bunch) for n in range(kv_heads)]
    scored = []
    for g, n in pairs:
        pieces = [
            queries[n * group + j][t * dialogs + g * bunch : t * dialogs + (g + 1) * bunch]
            for j in range(group)
            for t in range(steps)
        ]
        q = jnp.concatenate(pieces, axis=0).astype(BF)
        old_k = ck_buf[g * span_c : (g + 1) * span_c, n * head : (n + 1) * head]
        scored.append((dot_t(q, old_k) * scale, dot_t(q, keys[n]) * scale))
    weighted = []
    for (g, n), (s_c, s_n) in zip(pairs, scored):
        ok_c = same & (live[:, g * span_c : (g + 1) * span_c] > 0)
        ok_n = causal & ((col_n % dialogs) == (row_n % bunch + g * bunch))
        s_c = jnp.where(ok_c, s_c, masked_score)
        s_n = jnp.where(ok_n, s_n, masked_score)
        top = jnp.maximum(
            jnp.max(s_c, axis=-1, keepdims=True), jnp.max(s_n, axis=-1, keepdims=True)
        )
        e_c = jnp.where(ok_c, jnp.exp(s_c - top), 0.0)
        e_n = jnp.where(ok_n, jnp.exp(s_n - top), 0.0)
        total = jnp.sum(e_c, axis=-1, keepdims=True) + jnp.sum(e_n, axis=-1, keepdims=True)
        weighted.append(((e_c / total).astype(BF), (e_n / total).astype(BF)))
    for (g, n), (w_c, w_n) in zip(pairs, weighted):
        old_v = cv_buf[g * span_c : (g + 1) * span_c, n * head : (n + 1) * head]
        out = dot_n(w_c, old_v) + dot_n(w_n, values[n])
        for j in range(group):
            for t in range(steps):
                at = (j * steps + t) * bunch
                h = n * group + j
                att[
                    t * dialogs + g * bunch : t * dialogs + (g + 1) * bunch,
                    h * head : (h + 1) * head,
                ] = out[at : at + bunch]

    copies[parts + 4].wait()
    hidden = inputs + dot_n(att[...].astype(BF), o_buf[...])
    hidden_out[...] = hidden
    routed = rms_norm(hidden, moe_gain[...]).astype(BF)
    experts = router_t.shape[0]
    logits = dot_t(router_t[...], routed)
    expert_id = lax.broadcasted_iota(jnp.int32, (experts, rows), 0)
    chosen = expert_id == picks[0:1, :]
    for k in range(1, picks.shape[0]):
        chosen = chosen | (expert_id == picks[k : k + 1, :])
    logits = jnp.where(chosen, logits, masked_score)
    raised = jnp.where(chosen, jnp.exp(logits - jnp.max(logits, axis=0, keepdims=True)), 0.0)
    gate = raised / jnp.sum(raised, axis=0, keepdims=True)
    high = gate.astype(BF).astype(F32)
    low = gate - high
    flat = jnp.concatenate([high, low, jnp.zeros((GATE - 2 * experts, rows), F32)], axis=0)
    flat = jnp.concatenate([flat, jnp.zeros((GATE, GATE - rows), F32)], axis=1)
    columns = jnp.transpose(flat)[:rows].astype(BF)
    sent_out[:, :width] = routed
    sent_out[:, width:] = columns


def dense(handed, picks, live, small, weights, caches, after):
    steps, dialogs, _ = handed.shape
    rows = steps * dialogs
    w_text, _, _, w_o = weights
    width = w_text.shape[1]
    copied = [*small, *weights, *caches]
    return pl.pallas_call(
        dense_kernel,
        out_shape=(
            jax.ShapeDtypeStruct((rows, width), F32),
            jax.ShapeDtypeStruct((rows, width + GATE), BF),
        ),
        in_specs=[vmem()] * 3 + [anywhere()] * (len(copied) + len(after)),
        out_specs=(vmem(),) * 2,
        scratch_shapes=[pltpu.VMEM(c.shape, c.dtype) for c in copied]
        + [pltpu.VMEM((rows, w_o.shape[0]), F32), pltpu.SemaphoreType.DMA((15,))],
        compiler_params=pltpu.CompilerParams(vmem_limit_bytes=24 * MIB),
        cost_estimate=pl.CostEstimate(
            flops=10 * rows * width * width, bytes_accessed=11 * MIB, transcendentals=400000
        ),
        name="dense",
    )(handed, picks, live, *(stay(c) for c in copied), *after)


def silu(v):
    half = 0.5 * v
    return half + half * jnp.tanh(half)


def stage_kernel(count, pieces, *refs):
    sources, codes = refs[:count], refs[count : count + pieces]
    *targets, held, sems = refs[count + pieces + 1 :]
    copies = [pltpu.make_async_copy(sources[i], targets[i], sems.at[i]) for i in range(count)]
    for copy in copies:
        copy.start()
    held[...] = jnp.concatenate([part[...] for part in codes], axis=1)
    for copy in copies:
        copy.wait()


def stage(weights, codes, after):
    count = len(weights)
    return pl.pallas_call(
        functools.partial(stage_kernel, count, len(codes)),
        out_shape=tuple(pltpu.VMEM(w.shape, w.dtype) for w in weights)
        + (jax.ShapeDtypeStruct((codes[0].shape[0], len(codes) * codes[0].shape[1]), jnp.int32),),
        in_specs=[anywhere()] * count + [vmem()] * len(codes) + [anywhere()],
        out_specs=(vmem(),) * (count + 1),
        scratch_shapes=[pltpu.SemaphoreType.DMA((count,))],
        compiler_params=pltpu.CompilerParams(vmem_limit_bytes=8 * MIB),
        cost_estimate=pl.CostEstimate(flops=0, bytes_accessed=10 * MIB, transcendentals=0),
        name="stage",
    )(*weights, *codes, after)


def expert_kernel(count, ids, *refs):
    ins = refs[:count]
    weights = refs[count : count + 4]
    outs = refs[count + 5 :]
    inner, width = weights[1].shape
    x = jnp.concatenate([part[:, :width] for part in ins], axis=0)
    gates = jnp.concatenate([part[:, width:] for part in ins], axis=0).astype(F32)
    lane = lax.broadcasted_iota(jnp.int32, gates.shape, 1)
    acts = []
    for e in range(2):
        gu = dot_n(x, weights[2 * e][...])
        acts.append((silu(gu[:, :inner]) * gu[:, inner:]).astype(BF))
    total = None
    for e in range(2):
        mine = (lane == ids[e]) | (lane == ids[e] + ids[2])
        gate = jnp.sum(jnp.where(mine, gates, 0.0), axis=1, keepdims=True)
        out = dot_n(acts[e], weights[2 * e + 1][...]) * gate
        total = out if total is None else total + out
    total = total.astype(BF)
    place = 0
    for out in outs:
        out[...] = total[place : place + out.shape[0]]
        place += out.shape[0]


def run_experts(arrays, ids, weights, after, name):
    count = len(arrays)
    inner, width = weights[1].shape
    rows = sum(a.shape[0] for a in arrays)
    return pl.pallas_call(
        functools.partial(expert_kernel, count),
        out_shape=tuple(pltpu.VMEM((a.shape[0], width), BF) for a in arrays),
        in_specs=[smem()] + [vmem()] * (count + 4) + [anywhere()],
        out_specs=tuple(vmem() for _ in arrays),
        compiler_params=pltpu.CompilerParams(vmem_limit_bytes=24 * MIB),
        cost_estimate=pl.CostEstimate(
            flops=2 * rows * 6 * inner * width,
            bytes_accessed=4 * rows * width + 12 * inner * width,
            transcendentals=rows * 2 * inner,
        ),
        name=name,
    )(ids, *arrays, *(pin(w) for w in weights), after)


def join_kernel(*refs):
    *ins, _after, out = refs
    place = 0
    for part in ins:
        out[place : place + part.shape[0], :] = part[...]
        place += part.shape[0]


def join(arrays, after):
    rows = sum(a.shape[0] for a in arrays)
    return pl.pallas_call(
        join_kernel,
        out_shape=jax.ShapeDtypeStruct((rows, arrays[0].shape[1]), arrays[0].dtype),
        in_specs=[vmem()] * len(arrays) + [anywhere()],
        out_specs=vmem(),
        compiler_params=pltpu.CompilerParams(vmem_limit_bytes=16 * MIB),
        cost_estimate=pl.CostEstimate(flops=0, bytes_accessed=2 * MIB, transcendentals=0),
        name="join",
    )(*arrays, after)


def add_kernel(um, lm, far_u, up, lp, far_l, _after, m, p):
    half = um.shape[0]
    m[:half, :] = (um[...].astype(F32) + far_u[...].astype(F32)).astype(BF)
    m[half:, :] = lm[...]
    p[:half, :] = up[...]
    p[half:, :] = (lp[...].astype(F32) + far_l[...].astype(F32)).astype(BF)


def add_far(*parts):
    rows, width = parts[0].shape
    return pl.pallas_call(
        add_kernel,
        out_shape=(jax.ShapeDtypeStruct((2 * rows, width), BF),) * 2,
        in_specs=[vmem()] * 6 + [anywhere()],
        out_specs=(vmem(),) * 2,
        compiler_params=pltpu.CompilerParams(vmem_limit_bytes=16 * MIB),
        cost_estimate=pl.CostEstimate(flops=2**18, bytes_accessed=2 * MIB, transcendentals=0),
        name="add_far",
    )(*parts)


def merge_kernel(hidden, own_u, own_l, one, two, _after, kept, *outs):
    size = hidden.shape[0]
    for k in range(1 + len(outs)):
        own = (own_u, own_l)[k // 2]
        place = slice(k * size, (k + 1) * size)
        total = own[k % 2 * size : (k % 2 + 1) * size, :].astype(F32)
        total = total + one[place, :].astype(F32) + two[place, :].astype(F32)
        if k == 0:
            kept[...] = hidden[...] + total
        else:
            outs[k - 1][...] = total.astype(BF)


def merge(hidden, *parts):
    size, width = hidden.shape
    return pl.pallas_call(
        merge_kernel,
        out_shape=(jax.ShapeDtypeStruct(hidden.shape, F32),)
        + (jax.ShapeDtypeStruct((size, width), BF),) * 3,
        in_specs=[vmem()] * 5 + [anywhere()],
        out_specs=(vmem(),) * 4,
        compiler_params=pltpu.CompilerParams(vmem_limit_bytes=16 * MIB),
        cost_estimate=pl.CostEstimate(flops=2**20, bytes_accessed=4 * MIB, transcendentals=0),
        name="merge",
    )(hidden, *parts)


def finish_kernel(kept, *refs):
    *parts, out = refs
    total = kept[...]
    for part in parts:
        total = total + part[...].astype(F32)
    out[...] = total.astype(BF)


def finish(kept, parts):
    return pl.pallas_call(
        finish_kernel,
        out_shape=jax.ShapeDtypeStruct(kept.shape, BF),
        in_specs=[vmem()] * (1 + len(parts)),
        out_specs=vmem(),
        compiler_params=pltpu.CompilerParams(vmem_limit_bytes=16 * MIB),
        cost_estimate=pl.CostEstimate(flops=2**19, bytes_accessed=2 * MIB, transcendentals=0),
        name="finish",
    )(kept, *parts)


def wave_kernel(
    window, first, owners, near, far, table_hbm, taps_hbm, bias_hbm, _after, out, done, table, taps, bias, rows_of, laid, sems
):
    part, channels = table.shape[0], bias.shape[1]
    lanes = near.shape[1]
    tap_count = taps.shape[0]
    frames_out = window - tap_count + 1
    dialogs = laid.shape[0] // frames_out
    copies = [
        pltpu.make_async_copy(taps_hbm, taps, sems.at[0]),
        pltpu.make_async_copy(bias_hbm, bias, sems.at[1]),
    ]
    for q in range(2):
        copies.append(
            pltpu.make_async_copy(
                table_hbm.at[pl.ds(q * part, part)],
                table.at[:, pl.ds(q * channels, channels)],
                sems.at[2 + q],
            )
        )
    for copy in copies:
        copy.start()
    for q, codes in enumerate((near, far)):
        square = jnp.concatenate(
            [codes[...].astype(F32), jnp.zeros((lanes - codes.shape[0], lanes), F32)], axis=0
        )
        rows_of[q * lanes : (q + 1) * lanes, :] = jnp.transpose(square).astype(jnp.int32)
    for copy in copies:
        copy.wait()
    entry = lax.broadcasted_iota(jnp.int32, (dialogs, part), 1)

    def one_block(k, carry):
        block = rows_of[pl.ds(pl.multiple_of(k * dialogs, dialogs), dialogs), :]
        count = block[:, window : window + 1]
        hot, upper = [], []
        for p in range(window):
            code = block[:, p : p + 1]
            upper.append(code >= part)
            code = jnp.where(code >= part, code - part, code)
            code = jnp.where(p < count + tap_count - 1, code, -1)
            hot.append((entry == code).astype(F32).astype(BF))
        found = dot_n(jnp.concatenate(hot, axis=0), table[...])
        frames = []
        for p in range(window):
            rows = found[p * dialogs : (p + 1) * dialogs]
            frames.append(jnp.where(upper[p], rows[:, channels:], rows[:, :channels]))
        for t in range(frames_out):
            total = jnp.zeros((dialogs, channels), F32) + bias[...]
            for j in range(tap_count):
                total = total + taps[j : j + 1, :] * frames[t + j]
            laid[pl.ds(t, dialogs, stride=frames_out), :] = jnp.where(t < count, silu(total), 0.0)
        result = laid[...].astype(BF).reshape(dialogs, frames_out, channels)
        out[pl.ds(owners[first + k] * dialogs, dialogs)] = result
        return carry

    lax.fori_loop(0, rows_of.shape[0] // dialogs, one_block, 0)
    done[...] = jnp.zeros_like(done)


def wave(numbers, first, near, far, table, taps, bias, after, window, dialogs):
    lanes = near.shape[1]
    entries, channels = table.shape
    frames_out = window - taps.shape[0] + 1
    rows = 2 * lanes
    return pl.pallas_call(
        functools.partial(wave_kernel, window, first),
        out_shape=(
            jax.ShapeDtypeStruct((rows, frames_out, channels), BF),
            jax.ShapeDtypeStruct((8, 128), F32),
        ),
        in_specs=[smem()] + [vmem()] * 2 + [anywhere()] * 4,
        out_specs=(vmem(), vmem()),
        scratch_shapes=[
            pltpu.VMEM((entries // 2, 2 * channels), BF),
            pltpu.VMEM(taps.shape, F32),
            pltpu.VMEM(bias.shape, F32),
            pltpu.VMEM((rows, lanes), jnp.int32),
            pltpu.VMEM((dialogs * frames_out, channels), F32),
            pltpu.SemaphoreType.DMA((4,)),
        ],
        compiler_params=pltpu.CompilerParams(vmem_limit_bytes=16 * MIB),
        cost_estimate=pl.CostEstimate(
            flops=2 * rows * window * entries * channels,
            bytes_accessed=2 * MIB,
            transcendentals=rows * frames_out * channels,
        ),
        name="wave",
    )(numbers, near, far, stay(table), stay(taps), stay(bias), after)


def expert_grid():
    chips = lax.axis_size("expert") // 2
    side = math.isqrt(chips)
    return side, chips // side


def swap_cores(array):
    return lax.ppermute(array, "expert", [(i, i ^ 1) for i in range(lax.axis_size("expert"))])


def move(array, stage, distance):
    nx, ny = expert_grid()
    route = []
    for x in range(nx):
        for y in range(ny):
            for core in range(2):
                if core != stage:
                    target = (x + distance) % nx * ny + y
                else:
                    target = x * ny + (y + distance) % ny
                route.append(((x * ny + y) * 2 + core, target * 2 + core))
    return lax.ppermute(array, "expert", route)


def along(array, distance):
    size = lax.axis_size("section")
    return lax.ppermute(array, "section", [(i, (i + distance) % size) for i in range(size)])


def shards(
    thinker_rows,
    codec_prev,
    w_text,
    attn_gain,
    w_q,
    key_value_weight,
    q_gain,
    k_gain,
    w_o,
    cache_k,
    value_cache,
    lengths,
    moe_gain,
    router,
    routes,
    w_gate_up,
    w_down,
    codes,
    counts,
    code_table,
    conv_weight,
    conv_bias,
):
    dialogs, steps, _ = thinker_rows.shape
    context = cache_k.shape[1]
    rows = dialogs * steps
    width = codec_prev.shape[2]
    handed = along(jnp.transpose(thinker_rows, (1, 0, 2)), 1)
    gu_a, down_a = w_gate_up[0], w_down[0]
    gu_b, down_b = swap_cores(gu_a), swap_cores(down_a)
    mine = lax.axis_index("expert").astype(jnp.int32)
    picks = jnp.transpose(routes, (2, 1, 0)).reshape(routes.shape[2], rows)
    live = (jnp.arange(context)[None, :] < lengths[:, None]).astype(F32)
    window = codes.shape[1]
    held = jnp.concatenate(
        [codes.T, counts[None], jnp.zeros((15 - window, dialogs), jnp.int32)], axis=0
    )
    held = (held, along(held, 1), along(held, -1), along(held, -2))
    sections = lax.axis_size("section")
    place = lax.axis_index("section").astype(jnp.int32)
    numbers = [mine, mine + 1 - 2 * (mine % 2), jnp.int32(router.shape[1])]
    numbers += [(place + shift) % sections for shift in (0, 7, 1, 2, 4, 3, 5, 6)]
    numbers = jnp.stack(numbers)
    hidden, sent = dense(
        handed,
        picks,
        live.reshape(1, dialogs * context),
        (
            attn_gain[None],
            q_gain[None],
            k_gain[None],
            moe_gain[None],
            jnp.transpose(router),
            jnp.transpose(codec_prev, (1, 0, 2)),
        ),
        (w_text, w_q, key_value_weight, w_o),
        [c.reshape(dialogs * context, c.shape[2]) for c in (cache_k, value_cache)],
        (*held[1:], numbers),
    )
    sent_m, sent_p, sent_x = move(sent, 0, 1), move(sent, 0, -1), move(sent, 0, 2)
    *expert_weights, held = stage((stay(gu_a), stay(down_a), gu_b, down_b), held, sent)
    held_far = along(held, 4)
    upper = join((sent, sent_m), sent)
    upper_m, upper_p = move(upper, 1, 1), move(upper, 1, -1)
    lower = join((sent_p, sent_x), expert_weights[1])
    lower_m, lower_p = move(lower, 1, 1), move(lower, 1, -1)
    experts = functools.partial(run_experts, ids=numbers, weights=expert_weights)
    own_u, own_l = experts((upper, lower), after=lower, name="experts_own")
    upper_m, own_u = lax.optimization_barrier((upper_m, own_u))
    lower_p, own_l = lax.optimization_barrier((lower_p, own_l))
    far_u, far_l = move(upper_m, 1, 1), move(lower_p, 1, -1)
    from_um, from_up, from_lm, from_lp = experts(
        (upper_m, upper_p, lower_m, lower_p), after=own_u, name="experts_near"
    )
    from_fu, from_fl = experts((far_u, far_l), after=from_um, name="experts_far")
    back_fu, back_fl = move(from_fu, 1, -1), move(from_fl, 1, 1)
    from_m, from_p = add_far(from_um, from_lm, back_fu, from_up, from_lp, back_fl, held_far)
    back_m, back_p = move(from_m, 1, -1), move(from_p, 1, 1)
    wave_feats, wave_done = wave(
        numbers, 3, held, held_far, code_table, conv_weight, conv_bias[None], from_m, window, dialogs
    )
    kept, *sums = merge(hidden, own_u, own_l, back_m, back_p, wave_done)
    out = finish(kept, (move(sums[0], 0, -1), move(sums[1], 0, 1), move(sums[2], 0, 2)))
    return (jnp.transpose(out.reshape(steps, dialogs, width), (1, 0, 2)), wave_feats)


def solution(mesh):
    each = P(("expert", "section"), None, None)
    return jax.shard_map(
        shards,
        mesh=mesh,
        in_specs=(
            each,
            each,
            P(),
            P(),
            P(),
            P(),
            P(),
            P(),
            P(),
            each,
            each,
            P(("expert", "section")),
            P(),
            P(),
            each,
            P("expert", None, None),
            P("expert", None, None),
            P(("expert", "section"), None),
            P(("expert", "section")),
            P(None, "section"),
            P(None, "section"),
            P("section"),
        ),
        out_specs=(each, P("expert", None, "section")),
        check_vma=False,
    )
```

```python
import functools
import math

import jax
import jax.numpy as jnp
from jax import lax
from jax.experimental import pallas as pl
from jax.experimental.pallas import tpu as pltpu
from jax.sharding import PartitionSpec as P

epsilon = 1e-06
masked_score = -1e30
BF = jnp.bfloat16
F32 = jnp.float32
MIB = 1024 * 1024
GATE = 128


def vmem():
    return pl.BlockSpec(memory_space=pltpu.VMEM)


def smem():
    return pl.BlockSpec(memory_space=pltpu.SMEM)


def anywhere():
    return pl.BlockSpec(memory_space=pl.ANY)


def stay(array):
    return pltpu.with_memory_space_constraint(array, pltpu.HBM)


def pin(array):
    return pltpu.with_memory_space_constraint(array, pltpu.VMEM)


def dot_t(a, b):
    return lax.dot_general(a, b, (((1,), (1,)), ((), ())), preferred_element_type=F32)


def dot_n(a, b):
    return jnp.dot(a, b, preferred_element_type=F32)


def rms_norm(values, gain):
    mean_square = jnp.mean(values * values, axis=-1, keepdims=True)
    return values * lax.rsqrt(mean_square + epsilon) * gain


def dense_kernel(
    handed,
    picks,
    live,
    attn_gain_hbm,
    q_gain_hbm,
    k_gain_hbm,
    moe_gain_hbm,
    router_hbm,
    codec_hbm,
    w_text,
    w_q,
    w_kv,
    w_o,
    cache_k,
    cache_v,
    _after_codes,
    _after_numbers,
    hidden_out,
    sent_out,
    attn_gain,
    q_gain,
    k_gain,
    moe_gain,
    router_t,
    codec,
    text_buf,
    q_buf,
    kv_buf,
    o_buf,
    ck_buf,
    cv_buf,
    att,
    sems,
):
    steps, dialogs, wide = handed.shape
    rows = steps * dialogs
    width = text_buf.shape[1]
    head = q_gain.shape[1]
    heads = q_buf.shape[1] // head
    kv_heads = kv_buf.shape[1] // (2 * head)
    group = heads // kv_heads
    context = cache_k.shape[0] // dialogs
    parts = 4
    span = wide // parts

    def text_copy(i):
        place = pl.ds(i * span, span)
        return pltpu.make_async_copy(w_text.at[place], text_buf.at[place], sems.at[i])

    def whole_copies(pairs, first):
        return [
            pltpu.make_async_copy(source, target, sems.at[first + i])
            for i, (source, target) in enumerate(pairs)
        ]

    copies = [text_copy(i) for i in range(parts)]
    copies += whole_copies(
        ((w_q, q_buf), (w_kv, kv_buf), (cache_k, ck_buf), (cache_v, cv_buf), (w_o, o_buf)), parts
    )
    small = whole_copies(
        (
            (codec_hbm, codec),
            (attn_gain_hbm, attn_gain),
            (q_gain_hbm, q_gain),
            (k_gain_hbm, k_gain),
            (moe_gain_hbm, moe_gain),
            (router_hbm, router_t),
        ),
        parts + 5,
    )
    copies[0].start()
    for copy in small:
        copy.start()
    for copy in copies[1:]:
        copy.start()
    for copy in small:
        copy.wait()
    inputs = codec[...].reshape(rows, width).astype(F32)
    for i in range(parts):
        copies[i].wait()
        block = handed[:, :, i * span : (i + 1) * span].reshape(rows, span)
        inputs = inputs + dot_n(block, text_buf[i * span : (i + 1) * span, :])
    normed = rms_norm(inputs, attn_gain[...]).astype(BF)
    copies[parts].wait()
    q_all = dot_n(normed, q_buf[...])
    copies[parts + 1].wait()
    kv = dot_n(normed, kv_buf[...])
    queries = [rms_norm(q_all[:, h * head : (h + 1) * head], q_gain[...]) for h in range(heads)]
    keys = [
        rms_norm(kv[:, n * head : (n + 1) * head], k_gain[...]).astype(BF) for n in range(kv_heads)
    ]
    values = [
        kv[:, (kv_heads + n) * head : (kv_heads + n + 1) * head].astype(BF)
        for n in range(kv_heads)
    ]
    copies[parts + 2].wait()
    copies[parts + 3].wait()

    bunch = 8
    q_rows = group * steps * bunch
    span_c = bunch * context
    row = lax.broadcasted_iota(jnp.int32, (q_rows, span_c), 0)
    col = lax.broadcasted_iota(jnp.int32, (q_rows, span_c), 1)
    same = (row % bunch) == (col // context)
    row_n = lax.broadcasted_iota(jnp.int32, (q_rows, rows), 0)
    col_n = lax.broadcasted_iota(jnp.int32, (q_rows, rows), 1)
    causal = (col_n // dialogs) <= ((row_n // bunch) % steps)
    scale = 1.0 / math.sqrt(head)
    pairs = [(g, n) for g in range(dialogs // bunch) for n in range(kv_heads)]
    scored = []
    for g, n in pairs:
        pieces = [
            queries[n * group + j][t * dialogs + g * bunch : t * dialogs + (g + 1) * bunch]
            for j in range(group)
            for t in range(steps)
        ]
        q = jnp.concatenate(pieces, axis=0).astype(BF)
        old_k = ck_buf[g * span_c : (g + 1) * span_c, n * head : (n + 1) * head]
        scored.append((dot_t(q, old_k) * scale, dot_t(q, keys[n]) * scale))
    weighted = []
    for (g, n), (s_c, s_n) in zip(pairs, scored):
        ok_c = same & (live[:, g * span_c : (g + 1) * span_c] > 0)
        ok_n = causal & ((col_n % dialogs) == (row_n % bunch + g * bunch))
        s_c = jnp.where(ok_c, s_c, masked_score)
        s_n = jnp.where(ok_n, s_n, masked_score)
        top = jnp.maximum(
            jnp.max(s_c, axis=-1, keepdims=True), jnp.max(s_n, axis=-1, keepdims=True)
        )
        e_c = jnp.where(ok_c, jnp.exp(s_c - top), 0.0)
        e_n = jnp.where(ok_n, jnp.exp(s_n - top), 0.0)
        total = jnp.sum(e_c, axis=-1, keepdims=True) + jnp.sum(e_n, axis=-1, keepdims=True)
        weighted.append(((e_c / total).astype(BF), (e_n / total).astype(BF)))
    for (g, n), (w_c, w_n) in zip(pairs, weighted):
        old_v = cv_buf[g * span_c : (g + 1) * span_c, n * head : (n + 1) * head]
        out = dot_n(w_c, old_v) + dot_n(w_n, values[n])
        for j in range(group):
            for t in range(steps):
                at = (j * steps + t) * bunch
                h = n * group + j
                att[
                    t * dialogs + g * bunch : t * dialogs + (g + 1) * bunch,
                    h * head : (h + 1) * head,
                ] = out[at : at + bunch]

    copies[parts + 4].wait()
    hidden = inputs + dot_n(att[...].astype(BF), o_buf[...])
    hidden_out[...] = hidden
    routed = rms_norm(hidden, moe_gain[...]).astype(BF)
    experts = router_t.shape[0]
    logits = dot_t(router_t[...], routed)
    expert_id = lax.broadcasted_iota(jnp.int32, (experts, rows), 0)
    chosen = expert_id == picks[0:1, :]
    for k in range(1, picks.shape[0]):
        chosen = chosen | (expert_id == picks[k : k + 1, :])
    logits = jnp.where(chosen, logits, masked_score)
    raised = jnp.where(chosen, jnp.exp(logits - jnp.max(logits, axis=0, keepdims=True)), 0.0)
    gate = raised / jnp.sum(raised, axis=0, keepdims=True)
    high = gate.astype(BF).astype(F32)
    low = gate - high
    flat = jnp.concatenate([high, low, jnp.zeros((GATE - 2 * experts, rows), F32)], axis=0)
    flat = jnp.concatenate([flat, jnp.zeros((GATE, GATE - rows), F32)], axis=1)
    columns = jnp.transpose(flat)[:rows].astype(BF)
    sent_out[:, :width] = routed
    sent_out[:, width:] = columns


def dense(handed, picks, live, small, weights, caches, after):
    steps, dialogs, _ = handed.shape
    rows = steps * dialogs
    w_text, _, _, w_o = weights
    width = w_text.shape[1]
    copied = [*small, *weights, *caches]
    return pl.pallas_call(
        dense_kernel,
        out_shape=(
            jax.ShapeDtypeStruct((rows, width), F32),
            jax.ShapeDtypeStruct((rows, width + GATE), BF),
        ),
        in_specs=[vmem()] * 3 + [anywhere()] * (len(copied) + len(after)),
        out_specs=(vmem(),) * 2,
        scratch_shapes=[pltpu.VMEM(c.shape, c.dtype) for c in copied]
        + [pltpu.VMEM((rows, w_o.shape[0]), F32), pltpu.SemaphoreType.DMA((15,))],
        compiler_params=pltpu.CompilerParams(vmem_limit_bytes=24 * MIB),
        cost_estimate=pl.CostEstimate(
            flops=10 * rows * width * width, bytes_accessed=11 * MIB, transcendentals=400000
        ),
        name="dense",
    )(handed, picks, live, *(stay(c) for c in copied), *after)


def silu(v):
    half = 0.5 * v
    return half + half * jnp.tanh(half)


def stage_kernel(count, *refs):
    sources, targets, sems = refs[:count], refs[count + 1 : 2 * count + 1], refs[-1]
    copies = [pltpu.make_async_copy(sources[i], targets[i], sems.at[i]) for i in range(count)]
    for copy in copies:
        copy.start()
    for copy in copies:
        copy.wait()


def stage(weights, after):
    count = len(weights)
    return pl.pallas_call(
        functools.partial(stage_kernel, count),
        out_shape=tuple(pltpu.VMEM(w.shape, w.dtype) for w in weights),
        in_specs=[anywhere()] * (count + 1),
        out_specs=(vmem(),) * count,
        scratch_shapes=[pltpu.SemaphoreType.DMA((count,))],
        compiler_params=pltpu.CompilerParams(vmem_limit_bytes=8 * MIB),
        cost_estimate=pl.CostEstimate(flops=0, bytes_accessed=10 * MIB, transcendentals=0),
        name="stage",
    )(*weights, after)


def expert_kernel(count, ids, *refs):
    ins = refs[:count]
    weights = refs[count : count + 4]
    outs = refs[count + 5 :]
    inner, width = weights[1].shape
    x = jnp.concatenate([part[:, :width] for part in ins], axis=0)
    gates = jnp.concatenate([part[:, width:] for part in ins], axis=0).astype(F32)
    lane = lax.broadcasted_iota(jnp.int32, gates.shape, 1)
    acts = []
    for e in range(2):
        gu = dot_n(x, weights[2 * e][...])
        acts.append((silu(gu[:, :inner]) * gu[:, inner:]).astype(BF))
    total = None
    for e in range(2):
        mine = (lane == ids[e]) | (lane == ids[e] + ids[2])
        gate = jnp.sum(jnp.where(mine, gates, 0.0), axis=1, keepdims=True)
        out = dot_n(acts[e], weights[2 * e + 1][...]) * gate
        total = out if total is None else total + out
    total = total.astype(BF)
    place = 0
    for out in outs:
        out[...] = total[place : place + out.shape[0]]
        place += out.shape[0]


def run_experts(arrays, ids, weights, after, name):
    count = len(arrays)
    inner, width = weights[1].shape
    rows = sum(a.shape[0] for a in arrays)
    return pl.pallas_call(
        functools.partial(expert_kernel, count),
        out_shape=tuple(pltpu.VMEM((a.shape[0], width), BF) for a in arrays),
        in_specs=[smem()] + [vmem()] * (count + 4) + [anywhere()],
        out_specs=tuple(vmem() for _ in arrays),
        compiler_params=pltpu.CompilerParams(vmem_limit_bytes=24 * MIB),
        cost_estimate=pl.CostEstimate(
            flops=2 * rows * 6 * inner * width,
            bytes_accessed=4 * rows * width + 12 * inner * width,
            transcendentals=rows * 2 * inner,
        ),
        name=name,
    )(ids, *arrays, *(pin(w) for w in weights), after)


def join_kernel(*refs):
    *ins, _after, out = refs
    place = 0
    for part in ins:
        out[place : place + part.shape[0], :] = part[...]
        place += part.shape[0]


def join(arrays, after):
    rows = sum(a.shape[0] for a in arrays)
    return pl.pallas_call(
        join_kernel,
        out_shape=jax.ShapeDtypeStruct((rows, arrays[0].shape[1]), arrays[0].dtype),
        in_specs=[vmem()] * len(arrays) + [anywhere()],
        out_specs=vmem(),
        compiler_params=pltpu.CompilerParams(vmem_limit_bytes=16 * MIB),
        cost_estimate=pl.CostEstimate(flops=0, bytes_accessed=2 * MIB, transcendentals=0),
        name="join",
    )(*arrays, after)


def add_kernel(a, b, c, d, _after, first, second):
    first[...] = (a[...].astype(F32) + b[...].astype(F32)).astype(BF)
    second[...] = (c[...].astype(F32) + d[...].astype(F32)).astype(BF)


def add_two(a, b, c, d, after):
    shape = jax.ShapeDtypeStruct(a.shape, BF)
    return pl.pallas_call(
        add_kernel,
        out_shape=(shape,) * 2,
        in_specs=[vmem()] * 4 + [anywhere()],
        out_specs=(vmem(),) * 2,
        compiler_params=pltpu.CompilerParams(vmem_limit_bytes=16 * MIB),
        cost_estimate=pl.CostEstimate(flops=2**18, bytes_accessed=2 * MIB, transcendentals=0),
        name="add_far",
    )(a, b, c, d, after)


def merge_kernel(hidden, own_t, t1, t2, own_b, b1, b2, _after, kept, *outs):
    size = hidden.shape[0]
    for k in range(1 + len(outs)):
        group = (own_t, t1, t2) if k < 2 else (own_b, b1, b2)
        place = slice(k % 2 * size, (k % 2 + 1) * size)
        total = sum(part[place, :].astype(F32) for part in group)
        if k == 0:
            kept[...] = hidden[...] + total
        else:
            outs[k - 1][...] = total.astype(BF)


def merge(hidden, upper, lower, after):
    size, width = hidden.shape
    return pl.pallas_call(
        merge_kernel,
        out_shape=(jax.ShapeDtypeStruct(hidden.shape, F32),)
        + (jax.ShapeDtypeStruct((size, width), BF),) * 3,
        in_specs=[vmem()] * 7 + [anywhere()],
        out_specs=(vmem(),) * 4,
        compiler_params=pltpu.CompilerParams(vmem_limit_bytes=16 * MIB),
        cost_estimate=pl.CostEstimate(flops=2**20, bytes_accessed=4 * MIB, transcendentals=0),
        name="merge",
    )(hidden, *upper, *lower, after)


def finish_kernel(kept, *refs):
    *parts, out = refs
    total = kept[...]
    for part in parts:
        total = total + part[...].astype(F32)
    out[...] = total.astype(BF)


def finish(kept, parts):
    return pl.pallas_call(
        finish_kernel,
        out_shape=jax.ShapeDtypeStruct(kept.shape, BF),
        in_specs=[vmem()] * (1 + len(parts)),
        out_specs=vmem(),
        compiler_params=pltpu.CompilerParams(vmem_limit_bytes=16 * MIB),
        cost_estimate=pl.CostEstimate(flops=2**19, bytes_accessed=2 * MIB, transcendentals=0),
        name="finish",
    )(kept, *parts)


def wave_kernel(
    window, first, owners, near, far, table_hbm, taps_hbm, bias_hbm, _after, out, done, table, taps, bias, rows_of, laid, sems
):
    part, channels = table.shape[0], bias.shape[1]
    lanes = near.shape[1]
    tap_count = taps.shape[0]
    frames_out = window - tap_count + 1
    dialogs = laid.shape[0] // frames_out
    copies = [
        pltpu.make_async_copy(taps_hbm, taps, sems.at[0]),
        pltpu.make_async_copy(bias_hbm, bias, sems.at[1]),
    ]
    for q in range(2):
        copies.append(
            pltpu.make_async_copy(
                table_hbm.at[pl.ds(q * part, part)],
                table.at[:, pl.ds(q * channels, channels)],
                sems.at[2 + q],
            )
        )
    for copy in copies:
        copy.start()
    for q, codes in enumerate((near, far)):
        square = jnp.concatenate(
            [codes[...].astype(F32), jnp.zeros((lanes - codes.shape[0], lanes), F32)], axis=0
        )
        rows_of[q * lanes : (q + 1) * lanes, :] = jnp.transpose(square).astype(jnp.int32)
    for copy in copies:
        copy.wait()
    entry = lax.broadcasted_iota(jnp.int32, (dialogs, part), 1)

    def one_block(k, carry):
        block = rows_of[pl.ds(pl.multiple_of(k * dialogs, dialogs), dialogs), :]
        count = block[:, window : window + 1]
        hot, upper = [], []
        for p in range(window):
            code = block[:, p : p + 1]
            upper.append(code >= part)
            code = jnp.where(code >= part, code - part, code)
            code = jnp.where(p < count + tap_count - 1, code, -1)
            hot.append((entry == code).astype(F32).astype(BF))
        found = dot_n(jnp.concatenate(hot, axis=0), table[...])
        frames = []
        for p in range(window):
            rows = found[p * dialogs : (p + 1) * dialogs]
            frames.append(jnp.where(upper[p], rows[:, channels:], rows[:, :channels]))
        for t in range(frames_out):
            total = jnp.zeros((dialogs, channels), F32) + bias[...]
            for j in range(tap_count):
                total = total + taps[j : j + 1, :] * frames[t + j]
            laid[pl.ds(t, dialogs, stride=frames_out), :] = jnp.where(t < count, silu(total), 0.0)
        result = laid[...].astype(BF).reshape(dialogs, frames_out, channels)
        out[pl.ds(owners[first + k] * dialogs, dialogs)] = result
        return carry

    lax.fori_loop(0, rows_of.shape[0] // dialogs, one_block, 0)
    done[...] = jnp.zeros_like(done)


def wave(numbers, first, near, far, table, taps, bias, after, window, dialogs):
    lanes = near.shape[1]
    entries, channels = table.shape
    frames_out = window - taps.shape[0] + 1
    rows = 2 * lanes
    return pl.pallas_call(
        functools.partial(wave_kernel, window, first),
        out_shape=(
            jax.ShapeDtypeStruct((rows, frames_out, channels), BF),
            jax.ShapeDtypeStruct((8, 128), F32),
        ),
        in_specs=[smem()] + [vmem()] * 2 + [anywhere()] * 4,
        out_specs=(vmem(), vmem()),
        scratch_shapes=[
            pltpu.VMEM((entries // 2, 2 * channels), BF),
            pltpu.VMEM(taps.shape, F32),
            pltpu.VMEM(bias.shape, F32),
            pltpu.VMEM((rows, lanes), jnp.int32),
            pltpu.VMEM((dialogs * frames_out, channels), F32),
            pltpu.SemaphoreType.DMA((4,)),
        ],
        compiler_params=pltpu.CompilerParams(vmem_limit_bytes=16 * MIB),
        cost_estimate=pl.CostEstimate(
            flops=2 * rows * window * entries * channels,
            bytes_accessed=2 * MIB,
            transcendentals=rows * frames_out * channels,
        ),
        name="wave",
    )(numbers, near, far, stay(table), stay(taps), stay(bias), after)


def expert_grid():
    chips = lax.axis_size("expert") // 2
    side = math.isqrt(chips)
    return side, chips // side


def swap_cores(array):
    return lax.ppermute(array, "expert", [(i, i ^ 1) for i in range(lax.axis_size("expert"))])


def move(array, stage, distance):
    nx, ny = expert_grid()
    route = []
    for x in range(nx):
        for y in range(ny):
            for core in range(2):
                if core == stage:
                    target = (x + distance) % nx * ny + y
                else:
                    target = x * ny + (y + distance) % ny
                route.append(((x * ny + y) * 2 + core, target * 2 + core))
    return lax.ppermute(array, "expert", route)


def along(array, distance):
    size = lax.axis_size("section")
    return lax.ppermute(array, "section", [(i, (i + distance) % size) for i in range(size)])


def shards(
    thinker_rows,
    codec_prev,
    w_text,
    attn_gain,
    w_q,
    key_value_weight,
    q_gain,
    k_gain,
    w_o,
    cache_k,
    value_cache,
    lengths,
    moe_gain,
    router,
    routes,
    w_gate_up,
    w_down,
    codes,
    counts,
    code_table,
    conv_weight,
    conv_bias,
):
    dialogs, steps, _ = thinker_rows.shape
    context = cache_k.shape[1]
    rows = dialogs * steps
    width = codec_prev.shape[2]
    handed = along(jnp.transpose(thinker_rows, (1, 0, 2)), 1)
    gu_a, down_a = w_gate_up[0], w_down[0]
    gu_b, down_b = swap_cores(gu_a), swap_cores(down_a)
    mine = lax.axis_index("expert").astype(jnp.int32)
    picks = jnp.transpose(routes, (2, 1, 0)).reshape(routes.shape[2], rows)
    live = (jnp.arange(context)[None, :] < lengths[:, None]).astype(F32)
    window = codes.shape[1]
    held = jnp.concatenate(
        [codes.T, counts[None], jnp.zeros((15 - window, dialogs), jnp.int32)], axis=0
    )
    held = jnp.concatenate([held, along(held, 1), along(held, -1), along(held, -2)], axis=1)
    sections = lax.axis_size("section")
    place = lax.axis_index("section").astype(jnp.int32)
    numbers = [mine, mine + 1 - 2 * (mine % 2), jnp.int32(router.shape[1])]
    numbers += [(place + shift) % sections for shift in (0, 7, 1, 2, 4, 3, 5, 6)]
    numbers = jnp.stack(numbers)
    hidden, sent = dense(
        handed,
        picks,
        live.reshape(1, dialogs * context),
        (
            attn_gain[None],
            q_gain[None],
            k_gain[None],
            moe_gain[None],
            jnp.transpose(router),
            jnp.transpose(codec_prev, (1, 0, 2)),
        ),
        (w_text, w_q, key_value_weight, w_o),
        [c.reshape(dialogs * context, c.shape[2]) for c in (cache_k, value_cache)],
        (held, numbers),
    )
    sent_m, sent_p, sent_x = move(sent, 0, 1), move(sent, 0, -1), move(sent, 0, 2)
    expert_weights = stage((stay(gu_a), stay(down_a), gu_b, down_b), sent)
    upper = join((sent, sent_m), sent)
    upper_m, upper_p = move(upper, 1, 1), move(upper, 1, -1)
    lower = join((sent_p, sent_x), expert_weights[1])
    lower_m, lower_p = move(lower, 1, 1), move(lower, 1, -1)
    experts = functools.partial(run_experts, ids=numbers, weights=expert_weights)
    own_u, own_l = experts((upper, lower), after=lower, name="experts_own")
    upper_m, own_u = lax.optimization_barrier((upper_m, own_u))
    lower_p, own_l = lax.optimization_barrier((lower_p, own_l))
    far_u, far_l = move(upper_m, 1, 1), move(lower_p, 1, -1)
    from_um, from_up, from_lm, from_lp = experts(
        (upper_m, upper_p, lower_m, lower_p), after=own_u, name="experts_near"
    )
    from_fu, from_fl = experts((far_u, far_l), after=from_um, name="experts_far")
    back_up, back_lm = move(from_up, 1, 1), move(from_lm, 1, -1)
    back_fu, back_fl = move(from_fu, 1, -1), move(from_fl, 1, 1)
    held_far = along(held, 4)
    from_um, from_lp = add_two(from_um, back_fu, from_lp, back_fl, held_far)
    back_um, back_lp = move(from_um, 1, -1), move(from_lp, 1, 1)
    wave_feats, wave_done = wave(
        numbers, 3, held, held_far, code_table, conv_weight, conv_bias[None], from_um, window, dialogs
    )
    kept, *sums = merge(
        hidden, (own_u, back_um, back_up), (own_l, back_lm, back_lp), wave_done
    )
    out = finish(kept, (move(sums[0], 0, -1), move(sums[1], 0, 1), move(sums[2], 0, 2)))
    return (jnp.transpose(out.reshape(steps, dialogs, width), (1, 0, 2)), wave_feats)


def solution(mesh):
    each = P(("expert", "section"), None, None)
    return jax.shard_map(
        shards,
        mesh=mesh,
        in_specs=(
            each,
            each,
            P(),
            P(),
            P(),
            P(),
            P(),
            P(),
            P(),
            each,
            each,
            P(("expert", "section")),
            P(),
            P(),
            each,
            P("expert", None, None),
            P("expert", None, None),
            P(("expert", "section"), None),
            P(("expert", "section")),
            P(None, "section"),
            P(None, "section"),
            P("section"),
        ),
        out_specs=(each, P("expert", None, "section")),
        check_vma=False,
    )
```

```python
import functools
import math

import jax
import jax.numpy as jnp
from jax import lax
from jax.experimental import pallas as pl
from jax.experimental.pallas import tpu as pltpu
from jax.sharding import PartitionSpec as P

epsilon = 1e-06
masked_score = -1e30
BF = jnp.bfloat16
F32 = jnp.float32
MIB = 1024 * 1024
GATE = 128


def vmem():
    return pl.BlockSpec(memory_space=pltpu.VMEM)


def smem():
    return pl.BlockSpec(memory_space=pltpu.SMEM)


def anywhere():
    return pl.BlockSpec(memory_space=pl.ANY)


def stay(array):
    return pltpu.with_memory_space_constraint(array, pltpu.HBM)


def pin(array):
    return pltpu.with_memory_space_constraint(array, pltpu.VMEM)


def dot_t(a, b):
    return lax.dot_general(a, b, (((1,), (1,)), ((), ())), preferred_element_type=F32)


def dot_n(a, b):
    return jnp.dot(a, b, preferred_element_type=F32)


def rms_norm(values, gain):
    mean_square = jnp.mean(values * values, axis=-1, keepdims=True)
    return values * lax.rsqrt(mean_square + epsilon) * gain


def dense_kernel(
    handed,
    picks,
    live,
    text_buf,
    q_buf,
    kv_buf,
    o_buf,
    ck_buf,
    cv_buf,
    attn_gain_hbm,
    q_gain_hbm,
    k_gain_hbm,
    moe_gain_hbm,
    router_hbm,
    codec_hbm,
    hidden_out,
    sent_out,
    attn_gain,
    q_gain,
    k_gain,
    moe_gain,
    router_t,
    codec,
    att,
    sems,
):
    steps, dialogs, wide = handed.shape
    rows = steps * dialogs
    width = text_buf.shape[1]
    head = q_gain.shape[1]
    heads = q_buf.shape[1] // head
    kv_heads = kv_buf.shape[1] // (2 * head)
    group = heads // kv_heads
    context = ck_buf.shape[0] // dialogs
    small = [
        pltpu.make_async_copy(source, target, sems.at[i])
        for i, (source, target) in enumerate(
            (
                (codec_hbm, codec),
                (attn_gain_hbm, attn_gain),
                (q_gain_hbm, q_gain),
                (k_gain_hbm, k_gain),
                (moe_gain_hbm, moe_gain),
                (router_hbm, router_t),
            )
        )
    ]
    for copy in small:
        copy.start()
    product = dot_n(handed[...].reshape(rows, wide), text_buf[...])
    for copy in small:
        copy.wait()
    inputs = product + codec[...].reshape(rows, width).astype(F32)
    normed = rms_norm(inputs, attn_gain[...]).astype(BF)
    q_all = dot_n(normed, q_buf[...])
    kv = dot_n(normed, kv_buf[...])
    queries = [rms_norm(q_all[:, h * head : (h + 1) * head], q_gain[...]) for h in range(heads)]
    keys = [
        rms_norm(kv[:, n * head : (n + 1) * head], k_gain[...]).astype(BF) for n in range(kv_heads)
    ]
    values = [
        kv[:, (kv_heads + n) * head : (kv_heads + n + 1) * head].astype(BF)
        for n in range(kv_heads)
    ]

    bunch = 8
    q_rows = group * steps * bunch
    span_c = bunch * context
    row = lax.broadcasted_iota(jnp.int32, (q_rows, span_c), 0)
    col = lax.broadcasted_iota(jnp.int32, (q_rows, span_c), 1)
    same = (row % bunch) == (col // context)
    row_n = lax.broadcasted_iota(jnp.int32, (q_rows, rows), 0)
    col_n = lax.broadcasted_iota(jnp.int32, (q_rows, rows), 1)
    causal = (col_n // dialogs) <= ((row_n // bunch) % steps)
    scale = 1.0 / math.sqrt(head)
    pairs = [(g, n) for g in range(dialogs // bunch) for n in range(kv_heads)]
    scored = []
    for g, n in pairs:
        pieces = [
            queries[n * group + j][t * dialogs + g * bunch : t * dialogs + (g + 1) * bunch]
            for j in range(group)
            for t in range(steps)
        ]
        q = jnp.concatenate(pieces, axis=0).astype(BF)
        old_k = ck_buf[g * span_c : (g + 1) * span_c, n * head : (n + 1) * head]
        scored.append((dot_t(q, old_k) * scale, dot_t(q, keys[n]) * scale))
    weighted = []
    for (g, n), (s_c, s_n) in zip(pairs, scored):
        ok_c = same & (live[:, g * span_c : (g + 1) * span_c] > 0)
        ok_n = causal & ((col_n % dialogs) == (row_n % bunch + g * bunch))
        s_c = jnp.where(ok_c, s_c, masked_score)
        s_n = jnp.where(ok_n, s_n, masked_score)
        top = jnp.maximum(
            jnp.max(s_c, axis=-1, keepdims=True), jnp.max(s_n, axis=-1, keepdims=True)
        )
        e_c = jnp.where(ok_c, jnp.exp(s_c - top), 0.0)
        e_n = jnp.where(ok_n, jnp.exp(s_n - top), 0.0)
        total = jnp.sum(e_c, axis=-1, keepdims=True) + jnp.sum(e_n, axis=-1, keepdims=True)
        weighted.append(((e_c / total).astype(BF), (e_n / total).astype(BF)))
    for (g, n), (w_c, w_n) in zip(pairs, weighted):
        old_v = cv_buf[g * span_c : (g + 1) * span_c, n * head : (n + 1) * head]
        out = dot_n(w_c, old_v) + dot_n(w_n, values[n])
        for j in range(group):
            for t in range(steps):
                at = (j * steps + t) * bunch
                h = n * group + j
                att[
                    t * dialogs + g * bunch : t * dialogs + (g + 1) * bunch,
                    h * head : (h + 1) * head,
                ] = out[at : at + bunch]

    hidden = inputs + dot_n(att[...].astype(BF), o_buf[...])
    hidden_out[...] = hidden
    routed = rms_norm(hidden, moe_gain[...]).astype(BF)
    experts = router_t.shape[0]
    logits = dot_t(router_t[...], routed)
    expert_id = lax.broadcasted_iota(jnp.int32, (experts, rows), 0)
    chosen = expert_id == picks[0:1, :]
    for k in range(1, picks.shape[0]):
        chosen = chosen | (expert_id == picks[k : k + 1, :])
    logits = jnp.where(chosen, logits, masked_score)
    raised = jnp.where(chosen, jnp.exp(logits - jnp.max(logits, axis=0, keepdims=True)), 0.0)
    gate = raised / jnp.sum(raised, axis=0, keepdims=True)
    high = gate.astype(BF).astype(F32)
    low = gate - high
    flat = jnp.concatenate([high, low, jnp.zeros((GATE - 2 * experts, rows), F32)], axis=0)
    flat = jnp.concatenate([flat, jnp.zeros((GATE, GATE - rows), F32)], axis=1)
    columns = jnp.transpose(flat)[:rows].astype(BF)
    sent_out[:, :width] = routed
    sent_out[:, width:] = columns


def dense(handed, picks, live, staged, small):
    steps, dialogs, _ = handed.shape
    rows = steps * dialogs
    w_text, _, _, w_o = staged[:4]
    width = w_text.shape[1]
    return pl.pallas_call(
        dense_kernel,
        out_shape=(
            jax.ShapeDtypeStruct((rows, width), F32),
            jax.ShapeDtypeStruct((rows, width + GATE), BF),
        ),
        in_specs=[vmem()] * 9 + [anywhere()] * len(small),
        out_specs=(vmem(),) * 2,
        scratch_shapes=[pltpu.VMEM(c.shape, c.dtype) for c in small]
        + [pltpu.VMEM((rows, w_o.shape[0]), F32), pltpu.SemaphoreType.DMA((len(small),))],
        compiler_params=pltpu.CompilerParams(vmem_limit_bytes=16 * MIB),
        cost_estimate=pl.CostEstimate(
            flops=10 * rows * width * width, bytes_accessed=11 * MIB, transcendentals=400000
        ),
        name="dense",
    )(handed, picks, live, *(pin(w) for w in staged), *(stay(c) for c in small))


def silu(v):
    half = 0.5 * v
    return half + half * jnp.tanh(half)


def stage_kernel(count, pieces, *refs):
    sources, codes = refs[:count], refs[count : count + pieces]
    outs, sems = refs[-1 - count - bool(pieces) : -1], refs[-1]
    copies = [pltpu.make_async_copy(sources[i], outs[i], sems.at[i]) for i in range(count)]
    for copy in copies:
        copy.start()
    if pieces:
        outs[count][...] = jnp.concatenate([part[...] for part in codes], axis=1)
    for copy in copies:
        copy.wait()


def stage(weights, codes, after):
    count = len(weights)
    shapes = [pltpu.VMEM(w.shape, w.dtype) for w in weights]
    if codes:
        height, dialogs = codes[0].shape
        shapes.append(jax.ShapeDtypeStruct((height, len(codes) * dialogs), jnp.int32))
    return pl.pallas_call(
        functools.partial(stage_kernel, count, len(codes)),
        out_shape=tuple(shapes),
        in_specs=[anywhere()] * count + [vmem()] * len(codes) + [anywhere()] * len(after),
        out_specs=(vmem(),) * len(shapes),
        scratch_shapes=[pltpu.SemaphoreType.DMA((count,))],
        compiler_params=pltpu.CompilerParams(vmem_limit_bytes=8 * MIB),
        cost_estimate=pl.CostEstimate(flops=0, bytes_accessed=10 * MIB, transcendentals=0),
        name="stage",
    )(*weights, *codes, *after)


def expert_kernel(count, ids, *refs):
    ins = refs[:count]
    weights = refs[count : count + 4]
    outs = refs[count + 5 :]
    inner, width = weights[1].shape
    x = jnp.concatenate([part[:, :width] for part in ins], axis=0)
    gates = jnp.concatenate([part[:, width:] for part in ins], axis=0).astype(F32)
    lane = lax.broadcasted_iota(jnp.int32, gates.shape, 1)
    acts = []
    for e in range(2):
        gu = dot_n(x, weights[2 * e][...])
        acts.append((silu(gu[:, :inner]) * gu[:, inner:]).astype(BF))
    total = None
    for e in range(2):
        mine = (lane == ids[e]) | (lane == ids[e] + ids[2])
        gate = jnp.sum(jnp.where(mine, gates, 0.0), axis=1, keepdims=True)
        out = dot_n(acts[e], weights[2 * e + 1][...]) * gate
        total = out if total is None else total + out
    total = total.astype(BF)
    place = 0
    for out in outs:
        out[...] = total[place : place + out.shape[0]]
        place += out.shape[0]


def run_experts(arrays, ids, weights, after, name):
    count = len(arrays)
    inner, width = weights[1].shape
    rows = sum(a.shape[0] for a in arrays)
    return pl.pallas_call(
        functools.partial(expert_kernel, count),
        out_shape=tuple(pltpu.VMEM((a.shape[0], width), BF) for a in arrays),
        in_specs=[smem()] + [vmem()] * (count + 4) + [anywhere()],
        out_specs=tuple(vmem() for _ in arrays),
        compiler_params=pltpu.CompilerParams(vmem_limit_bytes=24 * MIB),
        cost_estimate=pl.CostEstimate(
            flops=2 * rows * 6 * inner * width,
            bytes_accessed=4 * rows * width + 12 * inner * width,
            transcendentals=rows * 2 * inner,
        ),
        name=name,
    )(ids, *arrays, *(pin(w) for w in weights), after)


def join_kernel(*refs):
    *ins, _after, out = refs
    place = 0
    for part in ins:
        out[place : place + part.shape[0], :] = part[...]
        place += part.shape[0]


def join(arrays, after):
    rows = sum(a.shape[0] for a in arrays)
    return pl.pallas_call(
        join_kernel,
        out_shape=jax.ShapeDtypeStruct((rows, arrays[0].shape[1]), arrays[0].dtype),
        in_specs=[vmem()] * len(arrays) + [anywhere()],
        out_specs=vmem(),
        compiler_params=pltpu.CompilerParams(vmem_limit_bytes=16 * MIB),
        cost_estimate=pl.CostEstimate(flops=0, bytes_accessed=2 * MIB, transcendentals=0),
        name="join",
    )(*arrays, after)


def add_kernel(a, b, c, d, _after, first, second):
    first[...] = (a[...].astype(F32) + b[...].astype(F32)).astype(BF)
    second[...] = (c[...].astype(F32) + d[...].astype(F32)).astype(BF)


def add_two(a, b, c, d, after):
    shape = jax.ShapeDtypeStruct(a.shape, BF)
    return pl.pallas_call(
        add_kernel,
        out_shape=(shape,) * 2,
        in_specs=[vmem()] * 4 + [anywhere()],
        out_specs=(vmem(),) * 2,
        compiler_params=pltpu.CompilerParams(vmem_limit_bytes=16 * MIB),
        cost_estimate=pl.CostEstimate(flops=2**18, bytes_accessed=2 * MIB, transcendentals=0),
        name="add_far",
    )(a, b, c, d, after)


def merge_kernel(hidden, own_t, t1, t2, own_b, b1, b2, _after, kept, *outs):
    size = hidden.shape[0]
    for k in range(1 + len(outs)):
        group = (own_t, t1, t2) if k < 2 else (own_b, b1, b2)
        place = slice(k % 2 * size, (k % 2 + 1) * size)
        total = sum(part[place, :].astype(F32) for part in group)
        if k == 0:
            kept[...] = hidden[...] + total
        else:
            outs[k - 1][...] = total.astype(BF)


def merge(hidden, upper, lower, after):
    size, width = hidden.shape
    return pl.pallas_call(
        merge_kernel,
        out_shape=(jax.ShapeDtypeStruct(hidden.shape, F32),)
        + (jax.ShapeDtypeStruct((size, width), BF),) * 3,
        in_specs=[vmem()] * 7 + [anywhere()],
        out_specs=(vmem(),) * 4,
        compiler_params=pltpu.CompilerParams(vmem_limit_bytes=16 * MIB),
        cost_estimate=pl.CostEstimate(flops=2**20, bytes_accessed=4 * MIB, transcendentals=0),
        name="merge",
    )(hidden, *upper, *lower, after)


def finish_kernel(kept, *refs):
    *parts, out = refs
    total = kept[...]
    for part in parts:
        total = total + part[...].astype(F32)
    out[...] = total.astype(BF)


def finish(kept, parts):
    return pl.pallas_call(
        finish_kernel,
        out_shape=jax.ShapeDtypeStruct(kept.shape, BF),
        in_specs=[vmem()] * (1 + len(parts)),
        out_specs=vmem(),
        compiler_params=pltpu.CompilerParams(vmem_limit_bytes=16 * MIB),
        cost_estimate=pl.CostEstimate(flops=2**19, bytes_accessed=2 * MIB, transcendentals=0),
        name="finish",
    )(kept, *parts)


def wave_kernel(
    window, first, owners, near, far, table_hbm, taps_hbm, bias_hbm, _after, out, done, table, taps, bias, rows_of, laid, sems
):
    part, channels = table.shape[0], bias.shape[1]
    lanes = near.shape[1]
    tap_count = taps.shape[0]
    frames_out = window - tap_count + 1
    dialogs = laid.shape[0] // frames_out
    copies = [
        pltpu.make_async_copy(taps_hbm, taps, sems.at[0]),
        pltpu.make_async_copy(bias_hbm, bias, sems.at[1]),
    ]
    for q in range(2):
        copies.append(
            pltpu.make_async_copy(
                table_hbm.at[pl.ds(q * part, part)],
                table.at[:, pl.ds(q * channels, channels)],
                sems.at[2 + q],
            )
        )
    for copy in copies:
        copy.start()
    for q, codes in enumerate((near, far)):
        square = jnp.concatenate(
            [codes[...].astype(F32), jnp.zeros((lanes - codes.shape[0], lanes), F32)], axis=0
        )
        rows_of[q * lanes : (q + 1) * lanes, :] = jnp.transpose(square).astype(jnp.int32)
    for copy in copies:
        copy.wait()
    entry = lax.broadcasted_iota(jnp.int32, (dialogs, part), 1)

    def one_block(k, carry):
        block = rows_of[pl.ds(pl.multiple_of(k * dialogs, dialogs), dialogs), :]
        count = block[:, window : window + 1]
        hot, upper = [], []
        for p in range(window):
            code = block[:, p : p + 1]
            upper.append(code >= part)
            code = jnp.where(code >= part, code - part, code)
            code = jnp.where(p < count + tap_count - 1, code, -1)
            hot.append((entry == code).astype(F32).astype(BF))
        found = dot_n(jnp.concatenate(hot, axis=0), table[...])
        frames = []
        for p in range(window):
            rows = found[p * dialogs : (p + 1) * dialogs]
            frames.append(jnp.where(upper[p], rows[:, channels:], rows[:, :channels]))
        for t in range(frames_out):
            total = jnp.zeros((dialogs, channels), F32) + bias[...]
            for j in range(tap_count):
                total = total + taps[j : j + 1, :] * frames[t + j]
            laid[pl.ds(t, dialogs, stride=frames_out), :] = jnp.where(t < count, silu(total), 0.0)
        result = laid[...].astype(BF).reshape(dialogs, frames_out, channels)
        out[pl.ds(owners[first + k] * dialogs, dialogs)] = result
        return carry

    lax.fori_loop(0, rows_of.shape[0] // dialogs, one_block, 0)
    done[...] = jnp.zeros_like(done)


def wave(numbers, first, near, far, table, taps, bias, after, window, dialogs):
    lanes = near.shape[1]
    entries, channels = table.shape
    frames_out = window - taps.shape[0] + 1
    rows = 2 * lanes
    return pl.pallas_call(
        functools.partial(wave_kernel, window, first),
        out_shape=(
            jax.ShapeDtypeStruct((rows, frames_out, channels), BF),
            jax.ShapeDtypeStruct((8, 128), F32),
        ),
        in_specs=[smem()] + [vmem()] * 2 + [anywhere()] * 4,
        out_specs=(vmem(), vmem()),
        scratch_shapes=[
            pltpu.VMEM((entries // 2, 2 * channels), BF),
            pltpu.VMEM(taps.shape, F32),
            pltpu.VMEM(bias.shape, F32),
            pltpu.VMEM((rows, lanes), jnp.int32),
            pltpu.VMEM((dialogs * frames_out, channels), F32),
            pltpu.SemaphoreType.DMA((4,)),
        ],
        compiler_params=pltpu.CompilerParams(vmem_limit_bytes=16 * MIB),
        cost_estimate=pl.CostEstimate(
            flops=2 * rows * window * entries * channels,
            bytes_accessed=2 * MIB,
            transcendentals=rows * frames_out * channels,
        ),
        name="wave",
    )(numbers, near, far, stay(table), stay(taps), stay(bias), after)


def expert_grid():
    chips = lax.axis_size("expert") // 2
    side = math.isqrt(chips)
    return side, chips // side


def swap_cores(array):
    return lax.ppermute(array, "expert", [(i, i ^ 1) for i in range(lax.axis_size("expert"))])


def move(array, stage, distance):
    nx, ny = expert_grid()
    route = []
    for x in range(nx):
        for y in range(ny):
            for core in range(2):
                if core == stage:
                    target = (x + distance) % nx * ny + y
                else:
                    target = x * ny + (y + distance) % ny
                route.append(((x * ny + y) * 2 + core, target * 2 + core))
    return lax.ppermute(array, "expert", route)


def along(array, distance):
    size = lax.axis_size("section")
    return lax.ppermute(array, "section", [(i, (i + distance) % size) for i in range(size)])


def shards(
    thinker_rows,
    codec_prev,
    w_text,
    attn_gain,
    w_q,
    key_value_weight,
    q_gain,
    k_gain,
    w_o,
    cache_k,
    value_cache,
    lengths,
    moe_gain,
    router,
    routes,
    w_gate_up,
    w_down,
    codes,
    counts,
    code_table,
    conv_weight,
    conv_bias,
):
    dialogs, steps, _ = thinker_rows.shape
    context = cache_k.shape[1]
    rows = dialogs * steps
    width = codec_prev.shape[2]
    handed = along(jnp.transpose(thinker_rows, (1, 0, 2)), 1)
    gu_a, down_a = w_gate_up[0], w_down[0]
    gu_b, down_b = swap_cores(gu_a), swap_cores(down_a)
    mine = lax.axis_index("expert").astype(jnp.int32)
    picks = jnp.transpose(routes, (2, 1, 0)).reshape(routes.shape[2], rows)
    live = (jnp.arange(context)[None, :] < lengths[:, None]).astype(F32)
    window = codes.shape[1]
    held = jnp.concatenate(
        [codes.T, counts[None], jnp.zeros((15 - window, dialogs), jnp.int32)], axis=0
    )
    held = (held, along(held, -1), along(held, -2), along(held, -3))
    sections = lax.axis_size("section")
    place = lax.axis_index("section").astype(jnp.int32)
    numbers = [mine, mine + 1 - 2 * (mine % 2), jnp.int32(router.shape[1])]
    numbers += [(place + shift) % sections for shift in range(sections)]
    numbers = jnp.stack(numbers)
    live = live.reshape(1, dialogs * context)
    staged = [w_text, w_q, key_value_weight, w_o]
    staged += [c.reshape(dialogs * context, c.shape[2]) for c in (cache_k, value_cache)]
    *staged, held = stage([stay(w) for w in staged], held, (numbers, picks, live))
    hidden, sent = dense(
        handed,
        picks,
        live,
        staged,
        (
            attn_gain[None],
            q_gain[None],
            k_gain[None],
            moe_gain[None],
            jnp.transpose(router),
            jnp.transpose(codec_prev, (1, 0, 2)),
        ),
    )
    sent_m, sent_p, sent_x = move(sent, 0, 1), move(sent, 0, -1), move(sent, 0, 2)
    expert_weights = stage((stay(gu_a), stay(down_a), gu_b, down_b), (), (sent,))
    upper = join((sent, sent_m), sent)
    upper_m, upper_p = move(upper, 1, 1), move(upper, 1, -1)
    lower = join((sent_p, sent_x), expert_weights[1])
    lower_m, lower_p = move(lower, 1, 1), move(lower, 1, -1)
    experts = functools.partial(run_experts, ids=numbers, weights=expert_weights)
    own_u, own_l = experts((upper, lower), after=lower, name="experts_own")
    upper_m, own_u = lax.optimization_barrier((upper_m, own_u))
    lower_p, own_l = lax.optimization_barrier((lower_p, own_l))
    far_u, far_l = move(upper_m, 1, 1), move(lower_p, 1, -1)
    from_um, from_up, from_lm, from_lp = experts(
        (upper_m, upper_p, lower_m, lower_p), after=own_u, name="experts_near"
    )
    from_fu, from_fl = experts((far_u, far_l), after=from_um, name="experts_far")
    back_up, back_lm = move(from_up, 1, 1), move(from_lm, 1, -1)
    back_fu, back_fl = move(from_fu, 1, -1), move(from_fl, 1, 1)
    held_far = along(held, sections // 2)
    from_um, from_lp = add_two(from_um, back_fu, from_lp, back_fl, held_far)
    back_um, back_lp = move(from_um, 1, -1), move(from_lp, 1, 1)
    wave_feats, wave_done = wave(
        numbers, 3, held, held_far, code_table, conv_weight, conv_bias[None], from_um, window, dialogs
    )
    kept, *sums = merge(
        hidden, (own_u, back_um, back_up), (own_l, back_lm, back_lp), wave_done
    )
    out = finish(kept, (move(sums[0], 0, -1), move(sums[1], 0, 1), move(sums[2], 0, 2)))
    return (jnp.transpose(out.reshape(steps, dialogs, width), (1, 0, 2)), wave_feats)


def solution(mesh):
    each = P(("expert", "section"), None, None)
    return jax.shard_map(
        shards,
        mesh=mesh,
        in_specs=(
            each,
            each,
            P(),
            P(),
            P(),
            P(),
            P(),
            P(),
            P(),
            each,
            each,
            P(("expert", "section")),
            P(),
            P(),
            each,
            P("expert", None, None),
            P("expert", None, None),
            P(("expert", "section"), None),
            P(("expert", "section")),
            P(None, "section"),
            P(None, "section"),
            P("section"),
        ),
        out_specs=(each, P("expert", None, "section")),
        check_vma=False,
    )
```

```python
import functools
import math

import jax
import jax.numpy as jnp
from jax import lax
from jax.experimental import pallas as pl
from jax.experimental.pallas import tpu as pltpu
from jax.sharding import PartitionSpec as P

epsilon = 1e-06
masked_score = -1e30
BF = jnp.bfloat16
F32 = jnp.float32
MIB = 1024 * 1024
GATE = 128


def vmem():
    return pl.BlockSpec(memory_space=pltpu.VMEM)


def smem():
    return pl.BlockSpec(memory_space=pltpu.SMEM)


def anywhere():
    return pl.BlockSpec(memory_space=pl.ANY)


def stay(array):
    return pltpu.with_memory_space_constraint(array, pltpu.HBM)


def pin(array):
    return pltpu.with_memory_space_constraint(array, pltpu.VMEM)


def dot_t(a, b):
    return lax.dot_general(a, b, (((1,), (1,)), ((), ())), preferred_element_type=F32)


def dot_n(a, b):
    return jnp.dot(a, b, preferred_element_type=F32)


def rms_norm(values, gain):
    mean_square = jnp.mean(values * values, axis=-1, keepdims=True)
    return values * lax.rsqrt(mean_square + epsilon) * gain


def dense_kernel(
    handed,
    picks,
    live,
    attn_gain_hbm,
    q_gain_hbm,
    k_gain_hbm,
    moe_gain_hbm,
    router_hbm,
    codec_hbm,
    w_text,
    w_q,
    w_kv,
    w_o,
    cache_k,
    cache_v,
    _after_codes,
    _after_numbers,
    hidden_out,
    sent_out,
    attn_gain,
    q_gain,
    k_gain,
    moe_gain,
    router_t,
    codec,
    text_buf,
    q_buf,
    kv_buf,
    o_buf,
    ck_buf,
    cv_buf,
    att,
    sems,
):
    steps, dialogs, wide = handed.shape
    rows = steps * dialogs
    width = text_buf.shape[1]
    head = q_gain.shape[1]
    heads = q_buf.shape[1] // head
    kv_heads = kv_buf.shape[1] // (2 * head)
    group = heads // kv_heads
    context = cache_k.shape[0] // dialogs
    parts = 4
    span = wide // parts

    def text_copy(i):
        place = pl.ds(i * span, span)
        return pltpu.make_async_copy(w_text.at[place], text_buf.at[place], sems.at[i])

    def whole_copies(pairs, first):
        return [
            pltpu.make_async_copy(source, target, sems.at[first + i])
            for i, (source, target) in enumerate(pairs)
        ]

    copies = [text_copy(i) for i in range(parts)]
    copies += whole_copies(
        ((w_q, q_buf), (w_kv, kv_buf), (cache_k, ck_buf), (cache_v, cv_buf), (w_o, o_buf)), parts
    )
    small = whole_copies(
        (
            (codec_hbm, codec),
            (attn_gain_hbm, attn_gain),
            (q_gain_hbm, q_gain),
            (k_gain_hbm, k_gain),
            (moe_gain_hbm, moe_gain),
            (router_hbm, router_t),
        ),
        parts + 5,
    )
    copies[0].start()
    for copy in small:
        copy.start()
    for copy in copies[1:]:
        copy.start()
    for copy in small:
        copy.wait()
    inputs = codec[...].reshape(rows, width).astype(F32)
    for i in range(parts):
        copies[i].wait()
        block = handed[:, :, i * span : (i + 1) * span].reshape(rows, span)
        inputs = inputs + dot_n(block, text_buf[i * span : (i + 1) * span, :])
    normed = rms_norm(inputs, attn_gain[...]).astype(BF)
    copies[parts].wait()
    q_all = dot_n(normed, q_buf[...])
    copies[parts + 1].wait()
    kv = dot_n(normed, kv_buf[...])
    queries = [rms_norm(q_all[:, h * head : (h + 1) * head], q_gain[...]) for h in range(heads)]
    keys = [
        rms_norm(kv[:, n * head : (n + 1) * head], k_gain[...]).astype(BF) for n in range(kv_heads)
    ]
    values = [
        kv[:, (kv_heads + n) * head : (kv_heads + n + 1) * head].astype(BF)
        for n in range(kv_heads)
    ]
    copies[parts + 2].wait()
    copies[parts + 3].wait()

    bunch = 8
    q_rows = group * steps * bunch
    span_c = bunch * context
    row = lax.broadcasted_iota(jnp.int32, (q_rows, span_c), 0)
    col = lax.broadcasted_iota(jnp.int32, (q_rows, span_c), 1)
    same = (row % bunch) == (col // context)
    row_n = lax.broadcasted_iota(jnp.int32, (q_rows, rows), 0)
    col_n = lax.broadcasted_iota(jnp.int32, (q_rows, rows), 1)
    causal = (col_n // dialogs) <= ((row_n // bunch) % steps)
    scale = 1.0 / math.sqrt(head)
    pairs = [(g, n) for g in range(dialogs // bunch) for n in range(kv_heads)]
    scored = []
    for g, n in pairs:
        pieces = [
            queries[n * group + j][t * dialogs + g * bunch : t * dialogs + (g + 1) * bunch]
            for j in range(group)
            for t in range(steps)
        ]
        q = jnp.concatenate(pieces, axis=0).astype(BF)
        old_k = ck_buf[g * span_c : (g + 1) * span_c, n * head : (n + 1) * head]
        scored.append((dot_t(q, old_k) * scale, dot_t(q, keys[n]) * scale))
    weighted = []
    for (g, n), (s_c, s_n) in zip(pairs, scored):
        ok_c = same & (live[:, g * span_c : (g + 1) * span_c] > 0)
        ok_n = causal & ((col_n % dialogs) == (row_n % bunch + g * bunch))
        s_c = jnp.where(ok_c, s_c, masked_score)
        s_n = jnp.where(ok_n, s_n, masked_score)
        top = jnp.maximum(
            jnp.max(s_c, axis=-1, keepdims=True), jnp.max(s_n, axis=-1, keepdims=True)
        )
        e_c = jnp.where(ok_c, jnp.exp(s_c - top), 0.0)
        e_n = jnp.where(ok_n, jnp.exp(s_n - top), 0.0)
        total = jnp.sum(e_c, axis=-1, keepdims=True) + jnp.sum(e_n, axis=-1, keepdims=True)
        weighted.append(((e_c / total).astype(BF), (e_n / total).astype(BF)))
    for (g, n), (w_c, w_n) in zip(pairs, weighted):
        old_v = cv_buf[g * span_c : (g + 1) * span_c, n * head : (n + 1) * head]
        out = dot_n(w_c, old_v) + dot_n(w_n, values[n])
        for j in range(group):
            for t in range(steps):
                at = (j * steps + t) * bunch
                h = n * group + j
                att[
                    t * dialogs + g * bunch : t * dialogs + (g + 1) * bunch,
                    h * head : (h + 1) * head,
                ] = out[at : at + bunch]

    copies[parts + 4].wait()
    hidden = inputs + dot_n(att[...].astype(BF), o_buf[...])
    hidden_out[...] = hidden
    routed = rms_norm(hidden, moe_gain[...]).astype(BF)
    experts = router_t.shape[0]
    logits = dot_t(router_t[...], routed)
    expert_id = lax.broadcasted_iota(jnp.int32, (experts, rows), 0)
    chosen = expert_id == picks[0:1, :]
    for k in range(1, picks.shape[0]):
        chosen = chosen | (expert_id == picks[k : k + 1, :])
    logits = jnp.where(chosen, logits, masked_score)
    raised = jnp.where(chosen, jnp.exp(logits - jnp.max(logits, axis=0, keepdims=True)), 0.0)
    gate = raised / jnp.sum(raised, axis=0, keepdims=True)
    high = gate.astype(BF).astype(F32)
    low = gate - high
    flat = jnp.concatenate([high, low, jnp.zeros((GATE - 2 * experts, rows), F32)], axis=0)
    flat = jnp.concatenate([flat, jnp.zeros((GATE, GATE - rows), F32)], axis=1)
    columns = jnp.transpose(flat)[:rows].astype(BF)
    sent_out[:, :width] = routed
    sent_out[:, width:] = columns


def dense(handed, picks, live, small, weights, caches, after):
    steps, dialogs, _ = handed.shape
    rows = steps * dialogs
    w_text, _, _, w_o = weights
    width = w_text.shape[1]
    copied = [*small, *weights, *caches]
    return pl.pallas_call(
        dense_kernel,
        out_shape=(
            jax.ShapeDtypeStruct((rows, width), F32),
            jax.ShapeDtypeStruct((rows, width + GATE), BF),
        ),
        in_specs=[vmem()] * 3 + [anywhere()] * (len(copied) + len(after)),
        out_specs=(vmem(),) * 2,
        scratch_shapes=[pltpu.VMEM(c.shape, c.dtype) for c in copied]
        + [pltpu.VMEM((rows, w_o.shape[0]), F32), pltpu.SemaphoreType.DMA((15,))],
        compiler_params=pltpu.CompilerParams(vmem_limit_bytes=24 * MIB),
        cost_estimate=pl.CostEstimate(
            flops=10 * rows * width * width, bytes_accessed=11 * MIB, transcendentals=400000
        ),
        name="dense",
    )(handed, picks, live, *(stay(c) for c in copied), *after)


def silu(v):
    half = 0.5 * v
    return half + half * jnp.tanh(half)


def stage_kernel(count, *refs):
    sources, targets, sems = refs[:count], refs[count + 1 : 2 * count + 1], refs[-1]
    copies = [pltpu.make_async_copy(sources[i], targets[i], sems.at[i]) for i in range(count)]
    for copy in copies:
        copy.start()
    for copy in copies:
        copy.wait()


def stage(weights, after):
    count = len(weights)
    return pl.pallas_call(
        functools.partial(stage_kernel, count),
        out_shape=tuple(pltpu.VMEM(w.shape, w.dtype) for w in weights),
        in_specs=[anywhere()] * (count + 1),
        out_specs=(vmem(),) * count,
        scratch_shapes=[pltpu.SemaphoreType.DMA((count,))],
        compiler_params=pltpu.CompilerParams(vmem_limit_bytes=8 * MIB),
        cost_estimate=pl.CostEstimate(flops=0, bytes_accessed=10 * MIB, transcendentals=0),
        name="stage",
    )(*weights, after)


def expert_kernel(count, ids, *refs):
    ins = refs[:count]
    weights = refs[count : count + 4]
    outs = refs[count + 5 :]
    inner, width = weights[1].shape
    x = jnp.concatenate([part[:, :width] for part in ins], axis=0)
    gates = jnp.concatenate([part[:, width:] for part in ins], axis=0).astype(F32)
    lane = lax.broadcasted_iota(jnp.int32, gates.shape, 1)
    acts = []
    for e in range(2):
        gu = dot_n(x, weights[2 * e][...])
        acts.append((silu(gu[:, :inner]) * gu[:, inner:]).astype(BF))
    total = None
    for e in range(2):
        mine = (lane == ids[e]) | (lane == ids[e] + ids[2])
        gate = jnp.sum(jnp.where(mine, gates, 0.0), axis=1, keepdims=True)
        out = dot_n(acts[e], weights[2 * e + 1][...]) * gate
        total = out if total is None else total + out
    total = total.astype(BF)
    place = 0
    for out in outs:
        out[...] = total[place : place + out.shape[0]]
        place += out.shape[0]


def run_experts(arrays, ids, weights, after, name):
    count = len(arrays)
    inner, width = weights[1].shape
    rows = sum(a.shape[0] for a in arrays)
    return pl.pallas_call(
        functools.partial(expert_kernel, count),
        out_shape=tuple(pltpu.VMEM((a.shape[0], width), BF) for a in arrays),
        in_specs=[smem()] + [vmem()] * (count + 4) + [anywhere()],
        out_specs=tuple(vmem() for _ in arrays),
        compiler_params=pltpu.CompilerParams(vmem_limit_bytes=24 * MIB),
        cost_estimate=pl.CostEstimate(
            flops=2 * rows * 6 * inner * width,
            bytes_accessed=4 * rows * width + 12 * inner * width,
            transcendentals=rows * 2 * inner,
        ),
        name=name,
    )(ids, *arrays, *(pin(w) for w in weights), after)


def join_kernel(*refs):
    *ins, _after, out = refs
    place = 0
    for part in ins:
        out[place : place + part.shape[0], :] = part[...]
        place += part.shape[0]


def join(arrays, after):
    rows = sum(a.shape[0] for a in arrays)
    return pl.pallas_call(
        join_kernel,
        out_shape=jax.ShapeDtypeStruct((rows, arrays[0].shape[1]), arrays[0].dtype),
        in_specs=[vmem()] * len(arrays) + [anywhere()],
        out_specs=vmem(),
        compiler_params=pltpu.CompilerParams(vmem_limit_bytes=16 * MIB),
        cost_estimate=pl.CostEstimate(flops=0, bytes_accessed=2 * MIB, transcendentals=0),
        name="join",
    )(*arrays, after)


def add_kernel(a, b, c, d, _after, first, second):
    first[...] = (a[...].astype(F32) + b[...].astype(F32)).astype(BF)
    second[...] = (c[...].astype(F32) + d[...].astype(F32)).astype(BF)


def add_two(a, b, c, d, after):
    shape = jax.ShapeDtypeStruct(a.shape, BF)
    return pl.pallas_call(
        add_kernel,
        out_shape=(shape,) * 2,
        in_specs=[vmem()] * 4 + [anywhere()],
        out_specs=(vmem(),) * 2,
        compiler_params=pltpu.CompilerParams(vmem_limit_bytes=16 * MIB),
        cost_estimate=pl.CostEstimate(flops=2**18, bytes_accessed=2 * MIB, transcendentals=0),
        name="add_far",
    )(a, b, c, d, after)


def merge_kernel(hidden, own_t, t1, t2, own_b, b1, b2, _after, kept, *outs):
    size = hidden.shape[0]
    for k in range(1 + len(outs)):
        group = (own_t, t1, t2) if k < 2 else (own_b, b1, b2)
        place = slice(k % 2 * size, (k % 2 + 1) * size)
        total = sum(part[place, :].astype(F32) for part in group)
        if k == 0:
            kept[...] = hidden[...] + total
        else:
            outs[k - 1][...] = total.astype(BF)


def merge(hidden, upper, lower, after):
    size, width = hidden.shape
    return pl.pallas_call(
        merge_kernel,
        out_shape=(jax.ShapeDtypeStruct(hidden.shape, F32),)
        + (jax.ShapeDtypeStruct((size, width), BF),) * 3,
        in_specs=[vmem()] * 7 + [anywhere()],
        out_specs=(vmem(),) * 4,
        compiler_params=pltpu.CompilerParams(vmem_limit_bytes=16 * MIB),
        cost_estimate=pl.CostEstimate(flops=2**20, bytes_accessed=4 * MIB, transcendentals=0),
        name="merge",
    )(hidden, *upper, *lower, after)


def finish_kernel(kept, *refs):
    *parts, out = refs
    total = kept[...]
    for part in parts:
        total = total + part[...].astype(F32)
    out[...] = total.astype(BF)


def finish(kept, parts):
    return pl.pallas_call(
        finish_kernel,
        out_shape=jax.ShapeDtypeStruct(kept.shape, BF),
        in_specs=[vmem()] * (1 + len(parts)),
        out_specs=vmem(),
        compiler_params=pltpu.CompilerParams(vmem_limit_bytes=16 * MIB),
        cost_estimate=pl.CostEstimate(flops=2**19, bytes_accessed=2 * MIB, transcendentals=0),
        name="finish",
    )(kept, *parts)


def wave_kernel(
    window, first, owners, near, far, table_hbm, taps_hbm, bias_hbm, _after, out, done, table, taps, bias, rows_of, laid, sems
):
    part, channels = table.shape[0], bias.shape[1]
    lanes = near.shape[1]
    tap_count = taps.shape[0]
    frames_out = window - tap_count + 1
    dialogs = laid.shape[0] // frames_out
    copies = [
        pltpu.make_async_copy(taps_hbm, taps, sems.at[0]),
        pltpu.make_async_copy(bias_hbm, bias, sems.at[1]),
    ]
    for q in range(2):
        copies.append(
            pltpu.make_async_copy(
                table_hbm.at[pl.ds(q * part, part)],
                table.at[:, pl.ds(q * channels, channels)],
                sems.at[2 + q],
            )
        )
    for copy in copies:
        copy.start()
    for q, codes in enumerate((near, far)):
        square = jnp.concatenate(
            [codes[...].astype(F32), jnp.zeros((lanes - codes.shape[0], lanes), F32)], axis=0
        )
        rows_of[q * lanes : (q + 1) * lanes, :] = jnp.transpose(square).astype(jnp.int32)
    for copy in copies:
        copy.wait()
    entry = lax.broadcasted_iota(jnp.int32, (dialogs, part), 1)

    def one_block(k, carry):
        block = rows_of[pl.ds(pl.multiple_of(k * dialogs, dialogs), dialogs), :]
        count = block[:, window : window + 1]
        hot, upper = [], []
        for p in range(window):
            code = block[:, p : p + 1]
            upper.append(code >= part)
            code = jnp.where(code >= part, code - part, code)
            code = jnp.where(p < count + tap_count - 1, code, -1)
            hot.append((entry == code).astype(F32).astype(BF))
        found = dot_n(jnp.concatenate(hot, axis=0), table[...])
        frames = []
        for p in range(window):
            rows = found[p * dialogs : (p + 1) * dialogs]
            frames.append(jnp.where(upper[p], rows[:, channels:], rows[:, :channels]))
        for t in range(frames_out):
            total = jnp.zeros((dialogs, channels), F32) + bias[...]
            for j in range(tap_count):
                total = total + taps[j : j + 1, :] * frames[t + j]
            laid[pl.ds(t, dialogs, stride=frames_out), :] = jnp.where(t < count, silu(total), 0.0)
        result = laid[...].astype(BF).reshape(dialogs, frames_out, channels)
        out[pl.ds(owners[first + k] * dialogs, dialogs)] = result
        return carry

    lax.fori_loop(0, rows_of.shape[0] // dialogs, one_block, 0)
    done[...] = jnp.zeros_like(done)


def wave(numbers, first, near, far, table, taps, bias, after, window, dialogs):
    lanes = near.shape[1]
    entries, channels = table.shape
    frames_out = window - taps.shape[0] + 1
    rows = 2 * lanes
    return pl.pallas_call(
        functools.partial(wave_kernel, window, first),
        out_shape=(
            jax.ShapeDtypeStruct((rows, frames_out, channels), BF),
            jax.ShapeDtypeStruct((8, 128), F32),
        ),
        in_specs=[smem()] + [vmem()] * 2 + [anywhere()] * 4,
        out_specs=(vmem(), vmem()),
        scratch_shapes=[
            pltpu.VMEM((entries // 2, 2 * channels), BF),
            pltpu.VMEM(taps.shape, F32),
            pltpu.VMEM(bias.shape, F32),
            pltpu.VMEM((rows, lanes), jnp.int32),
            pltpu.VMEM((dialogs * frames_out, channels), F32),
            pltpu.SemaphoreType.DMA((4,)),
        ],
        compiler_params=pltpu.CompilerParams(vmem_limit_bytes=16 * MIB),
        cost_estimate=pl.CostEstimate(
            flops=2 * rows * window * entries * channels,
            bytes_accessed=2 * MIB,
            transcendentals=rows * frames_out * channels,
        ),
        name="wave",
    )(numbers, near, far, stay(table), stay(taps), stay(bias), after)


def expert_grid():
    chips = lax.axis_size("expert") // 2
    side = math.isqrt(chips)
    return side, chips // side


def swap_cores(array):
    return lax.ppermute(array, "expert", [(i, i ^ 1) for i in range(lax.axis_size("expert"))])


def move(array, stage, distance):
    nx, ny = expert_grid()
    route = []
    for x in range(nx):
        for y in range(ny):
            for core in range(2):
                if core == stage:
                    target = (x + distance) % nx * ny + y
                else:
                    target = x * ny + (y + distance) % ny
                route.append(((x * ny + y) * 2 + core, target * 2 + core))
    return lax.ppermute(array, "expert", route)


def along(array, distance):
    size = lax.axis_size("section")
    return lax.ppermute(array, "section", [(i, (i + distance) % size) for i in range(size)])


def shards(
    thinker_rows,
    codec_prev,
    w_text,
    attn_gain,
    w_q,
    key_value_weight,
    q_gain,
    k_gain,
    w_o,
    cache_k,
    value_cache,
    lengths,
    moe_gain,
    router,
    routes,
    w_gate_up,
    w_down,
    codes,
    counts,
    code_table,
    conv_weight,
    conv_bias,
):
    dialogs, steps, _ = thinker_rows.shape
    context = cache_k.shape[1]
    rows = dialogs * steps
    width = codec_prev.shape[2]
    handed = along(jnp.transpose(thinker_rows, (1, 0, 2)), 1)
    gu_a, down_a = w_gate_up[0], w_down[0]
    gu_b, down_b = swap_cores(gu_a), swap_cores(down_a)
    mine = lax.axis_index("expert").astype(jnp.int32)
    picks = jnp.transpose(routes, (2, 1, 0)).reshape(routes.shape[2], rows)
    live = (jnp.arange(context)[None, :] < lengths[:, None]).astype(F32)
    window = codes.shape[1]
    held = jnp.concatenate(
        [codes.T, counts[None], jnp.zeros((15 - window, dialogs), jnp.int32)], axis=0
    )
    held = jnp.concatenate([held, along(held, 1), along(held, -1), along(held, -2)], axis=1)
    sections = lax.axis_size("section")
    place = lax.axis_index("section").astype(jnp.int32)
    numbers = [mine, mine + 1 - 2 * (mine % 2), jnp.int32(router.shape[1])]
    numbers += [(place + shift) % sections for shift in (0, 7, 1, 2, 4, 3, 5, 6)]
    numbers = jnp.stack(numbers)
    hidden, sent = dense(
        handed,
        picks,
        live.reshape(1, dialogs * context),
        (
            attn_gain[None],
            q_gain[None],
            k_gain[None],
            moe_gain[None],
            jnp.transpose(router),
            jnp.transpose(codec_prev, (1, 0, 2)),
        ),
        (w_text, w_q, key_value_weight, w_o),
        [c.reshape(dialogs * context, c.shape[2]) for c in (cache_k, value_cache)],
        (held, numbers),
    )
    sent_m, sent_x, sent_p = move(sent, 0, 1), move(sent, 0, 2), move(sent, 0, -1)
    expert_weights = stage((stay(gu_a), stay(down_a), gu_b, down_b), sent)
    upper = join((sent, sent_m), sent)
    upper_m, upper_p = move(upper, 1, 1), move(upper, 1, -1)
    lower = join((sent_x, sent_p), expert_weights[1])
    lower_m, lower_p = move(lower, 1, 1), move(lower, 1, -1)
    experts = functools.partial(run_experts, ids=numbers, weights=expert_weights)
    own_u, own_l = experts((upper, lower), after=lower, name="experts_own")
    upper_m, own_u = lax.optimization_barrier((upper_m, own_u))
    lower_p, own_l = lax.optimization_barrier((lower_p, own_l))
    far_u, far_l = move(upper_m, 1, 1), move(lower_p, 1, -1)
    from_um, from_up, from_lm, from_lp = experts(
        (upper_m, upper_p, lower_m, lower_p), after=own_u, name="experts_near"
    )
    from_fu, from_fl = experts((far_u, far_l), after=from_um, name="experts_far")
    back_up, back_lm = move(from_up, 1, 1), move(from_lm, 1, -1)
    back_fu, back_fl = move(from_fu, 1, -1), move(from_fl, 1, 1)
    held_far = along(held, 4)
    from_um, from_lp = add_two(from_um, back_fu, from_lp, back_fl, held_far)
    back_um, back_lp = move(from_um, 1, -1), move(from_lp, 1, 1)
    wave_feats, wave_done = wave(
        numbers, 3, held, held_far, code_table, conv_weight, conv_bias[None], from_um, window, dialogs
    )
    kept, *sums = merge(
        hidden, (own_u, back_um, back_up), (own_l, back_lm, back_lp), wave_done
    )
    out = finish(kept, (move(sums[1], 0, 2), move(sums[0], 0, -1), move(sums[2], 0, 1)))
    return (jnp.transpose(out.reshape(steps, dialogs, width), (1, 0, 2)), wave_feats)


def solution(mesh):
    each = P(("expert", "section"), None, None)
    return jax.shard_map(
        shards,
        mesh=mesh,
        in_specs=(
            each,
            each,
            P(),
            P(),
            P(),
            P(),
            P(),
            P(),
            P(),
            each,
            each,
            P(("expert", "section")),
            P(),
            P(),
            each,
            P("expert", None, None),
            P("expert", None, None),
            P(("expert", "section"), None),
            P(("expert", "section")),
            P(None, "section"),
            P(None, "section"),
            P("section"),
        ),
        out_specs=(each, P("expert", None, "section")),
        check_vma=False,
    )
```

```python
import functools
import math

import jax
import jax.numpy as jnp
from jax import lax
from jax.experimental import pallas as pl
from jax.experimental.pallas import tpu as pltpu
from jax.sharding import PartitionSpec as P

epsilon = 1e-06
masked_score = -1e30
BF = jnp.bfloat16
F32 = jnp.float32
MIB = 1024 * 1024
GATE = 128


def vmem():
    return pl.BlockSpec(memory_space=pltpu.VMEM)


def smem():
    return pl.BlockSpec(memory_space=pltpu.SMEM)


def anywhere():
    return pl.BlockSpec(memory_space=pl.ANY)


def stay(array):
    return pltpu.with_memory_space_constraint(array, pltpu.HBM)


def pin(array):
    return pltpu.with_memory_space_constraint(array, pltpu.VMEM)


def dot_t(a, b):
    return lax.dot_general(a, b, (((1,), (1,)), ((), ())), preferred_element_type=F32)


def dot_n(a, b):
    return jnp.dot(a, b, preferred_element_type=F32)


def rms_norm(values, gain):
    mean_square = jnp.mean(values * values, axis=-1, keepdims=True)
    return values * lax.rsqrt(mean_square + epsilon) * gain


def dense_kernel(
    handed,
    picks,
    live,
    attn_gain_hbm,
    q_gain_hbm,
    k_gain_hbm,
    moe_gain_hbm,
    router_hbm,
    codec_hbm,
    w_text,
    w_q,
    w_kv,
    w_o,
    cache_k,
    cache_v,
    _after_a,
    _after_b,
    _after_c,
    _after_numbers,
    hidden_out,
    sent_out,
    attn_gain,
    q_gain,
    k_gain,
    moe_gain,
    router_t,
    codec,
    text_buf,
    q_buf,
    kv_buf,
    o_buf,
    ck_buf,
    cv_buf,
    att,
    sems,
):
    steps, dialogs, wide = handed.shape
    rows = steps * dialogs
    width = text_buf.shape[1]
    head = q_gain.shape[1]
    heads = q_buf.shape[1] // head
    kv_heads = kv_buf.shape[1] // (2 * head)
    group = heads // kv_heads
    context = cache_k.shape[0] // dialogs
    parts = 4
    span = wide // parts

    def text_copy(i):
        place = pl.ds(i * span, span)
        return pltpu.make_async_copy(w_text.at[place], text_buf.at[place], sems.at[i])

    def whole_copies(pairs, first):
        return [
            pltpu.make_async_copy(source, target, sems.at[first + i])
            for i, (source, target) in enumerate(pairs)
        ]

    copies = [text_copy(i) for i in range(parts)]
    copies += whole_copies(
        ((w_q, q_buf), (w_kv, kv_buf), (cache_k, ck_buf), (cache_v, cv_buf), (w_o, o_buf)), parts
    )
    small = whole_copies(
        (
            (codec_hbm, codec),
            (attn_gain_hbm, attn_gain),
            (q_gain_hbm, q_gain),
            (k_gain_hbm, k_gain),
            (moe_gain_hbm, moe_gain),
            (router_hbm, router_t),
        ),
        parts + 5,
    )
    copies[0].start()
    for copy in small:
        copy.start()
    for copy in copies[1:]:
        copy.start()
    for copy in small:
        copy.wait()
    inputs = codec[...].reshape(rows, width).astype(F32)
    for i in range(parts):
        copies[i].wait()
        block = handed[:, :, i * span : (i + 1) * span].reshape(rows, span)
        inputs = inputs + dot_n(block, text_buf[i * span : (i + 1) * span, :])
    normed = rms_norm(inputs, attn_gain[...]).astype(BF)
    copies[parts].wait()
    q_all = dot_n(normed, q_buf[...])
    copies[parts + 1].wait()
    kv = dot_n(normed, kv_buf[...])
    queries = [rms_norm(q_all[:, h * head : (h + 1) * head], q_gain[...]) for h in range(heads)]
    keys = [
        rms_norm(kv[:, n * head : (n + 1) * head], k_gain[...]).astype(BF) for n in range(kv_heads)
    ]
    values = [
        kv[:, (kv_heads + n) * head : (kv_heads + n + 1) * head].astype(BF)
        for n in range(kv_heads)
    ]
    copies[parts + 2].wait()
    copies[parts + 3].wait()

    bunch = 8
    q_rows = group * steps * bunch
    span_c = bunch * context
    row = lax.broadcasted_iota(jnp.int32, (q_rows, span_c), 0)
    col = lax.broadcasted_iota(jnp.int32, (q_rows, span_c), 1)
    same = (row % bunch) == (col // context)
    row_n = lax.broadcasted_iota(jnp.int32, (q_rows, rows), 0)
    col_n = lax.broadcasted_iota(jnp.int32, (q_rows, rows), 1)
    causal = (col_n // dialogs) <= ((row_n // bunch) % steps)
    scale = 1.0 / math.sqrt(head)
    pairs = [(g, n) for g in range(dialogs // bunch) for n in range(kv_heads)]
    scored = []
    for g, n in pairs:
        pieces = [
            queries[n * group + j][t * dialogs + g * bunch : t * dialogs + (g + 1) * bunch]
            for j in range(group)
            for t in range(steps)
        ]
        q = jnp.concatenate(pieces, axis=0).astype(BF)
        old_k = ck_buf[g * span_c : (g + 1) * span_c, n * head : (n + 1) * head]
        scored.append((dot_t(q, old_k) * scale, dot_t(q, keys[n]) * scale))
    weighted = []
    for (g, n), (s_c, s_n) in zip(pairs, scored):
        ok_c = same & (live[:, g * span_c : (g + 1) * span_c] > 0)
        ok_n = causal & ((col_n % dialogs) == (row_n % bunch + g * bunch))
        s_c = jnp.where(ok_c, s_c, masked_score)
        s_n = jnp.where(ok_n, s_n, masked_score)
        top = jnp.maximum(
            jnp.max(s_c, axis=-1, keepdims=True), jnp.max(s_n, axis=-1, keepdims=True)
        )
        e_c = jnp.where(ok_c, jnp.exp(s_c - top), 0.0)
        e_n = jnp.where(ok_n, jnp.exp(s_n - top), 0.0)
        total = jnp.sum(e_c, axis=-1, keepdims=True) + jnp.sum(e_n, axis=-1, keepdims=True)
        weighted.append(((e_c / total).astype(BF), (e_n / total).astype(BF)))
    for (g, n), (w_c, w_n) in zip(pairs, weighted):
        old_v = cv_buf[g * span_c : (g + 1) * span_c, n * head : (n + 1) * head]
        out = dot_n(w_c, old_v) + dot_n(w_n, values[n])
        for j in range(group):
            for t in range(steps):
                at = (j * steps + t) * bunch
                h = n * group + j
                att[
                    t * dialogs + g * bunch : t * dialogs + (g + 1) * bunch,
                    h * head : (h + 1) * head,
                ] = out[at : at + bunch]

    copies[parts + 4].wait()
    hidden = inputs + dot_n(att[...].astype(BF), o_buf[...])
    hidden_out[...] = hidden
    routed = rms_norm(hidden, moe_gain[...]).astype(BF)
    experts = router_t.shape[0]
    logits = dot_t(router_t[...], routed)
    expert_id = lax.broadcasted_iota(jnp.int32, (experts, rows), 0)
    chosen = expert_id == picks[0:1, :]
    for k in range(1, picks.shape[0]):
        chosen = chosen | (expert_id == picks[k : k + 1, :])
    logits = jnp.where(chosen, logits, masked_score)
    raised = jnp.where(chosen, jnp.exp(logits - jnp.max(logits, axis=0, keepdims=True)), 0.0)
    gate = raised / jnp.sum(raised, axis=0, keepdims=True)
    high = gate.astype(BF).astype(F32)
    low = gate - high
    flat = jnp.concatenate([high, low, jnp.zeros((GATE - 2 * experts, rows), F32)], axis=0)
    flat = jnp.concatenate([flat, jnp.zeros((GATE, GATE - rows), F32)], axis=1)
    columns = jnp.transpose(flat)[:rows].astype(BF)
    sent_out[:, :width] = routed
    sent_out[:, width:] = columns


def dense(handed, picks, live, small, weights, caches, after):
    steps, dialogs, _ = handed.shape
    rows = steps * dialogs
    w_text, _, _, w_o = weights
    width = w_text.shape[1]
    copied = [*small, *weights, *caches]
    return pl.pallas_call(
        dense_kernel,
        out_shape=(
            jax.ShapeDtypeStruct((rows, width), F32),
            jax.ShapeDtypeStruct((rows, width + GATE), BF),
        ),
        in_specs=[vmem()] * 3 + [anywhere()] * (len(copied) + len(after)),
        out_specs=(vmem(),) * 2,
        scratch_shapes=[pltpu.VMEM(c.shape, c.dtype) for c in copied]
        + [pltpu.VMEM((rows, w_o.shape[0]), F32), pltpu.SemaphoreType.DMA((15,))],
        compiler_params=pltpu.CompilerParams(vmem_limit_bytes=24 * MIB),
        cost_estimate=pl.CostEstimate(
            flops=10 * rows * width * width, bytes_accessed=11 * MIB, transcendentals=400000
        ),
        name="dense",
    )(handed, picks, live, *(stay(c) for c in copied), *after)


def silu(v):
    half = 0.5 * v
    return half + half * jnp.tanh(half)


def stage_kernel(count, pieces, *refs):
    sources, codes = refs[:count], refs[count : count + pieces]
    outs, sems = refs[-1 - count - bool(pieces) : -1], refs[-1]
    copies = [pltpu.make_async_copy(sources[i], outs[i], sems.at[i]) for i in range(count)]
    for copy in copies:
        copy.start()
    if pieces:
        outs[count][...] = jnp.concatenate([part[...] for part in codes], axis=1)
    for copy in copies:
        copy.wait()


def stage(weights, codes, after):
    count = len(weights)
    shapes = [pltpu.VMEM(w.shape, w.dtype) for w in weights]
    if codes:
        height, dialogs = codes[0].shape
        shapes.append(jax.ShapeDtypeStruct((height, len(codes) * dialogs), jnp.int32))
    return pl.pallas_call(
        functools.partial(stage_kernel, count, len(codes)),
        out_shape=tuple(shapes),
        in_specs=[anywhere()] * count + [vmem()] * len(codes) + [anywhere()] * len(after),
        out_specs=(vmem(),) * len(shapes),
        scratch_shapes=[pltpu.SemaphoreType.DMA((count,))],
        compiler_params=pltpu.CompilerParams(vmem_limit_bytes=8 * MIB),
        cost_estimate=pl.CostEstimate(flops=0, bytes_accessed=10 * MIB, transcendentals=0),
        name="stage",
    )(*weights, *codes, *after)


def expert_kernel(count, ids, *refs):
    ins = refs[:count]
    weights = refs[count : count + 4]
    outs = refs[count + 5 :]
    inner, width = weights[1].shape
    x = jnp.concatenate([part[:, :width] for part in ins], axis=0)
    gates = jnp.concatenate([part[:, width:] for part in ins], axis=0).astype(F32)
    lane = lax.broadcasted_iota(jnp.int32, gates.shape, 1)
    acts = []
    for e in range(2):
        gu = dot_n(x, weights[2 * e][...])
        acts.append((silu(gu[:, :inner]) * gu[:, inner:]).astype(BF))
    total = None
    for e in range(2):
        mine = (lane == ids[e]) | (lane == ids[e] + ids[2])
        gate = jnp.sum(jnp.where(mine, gates, 0.0), axis=1, keepdims=True)
        out = dot_n(acts[e], weights[2 * e + 1][...]) * gate
        total = out if total is None else total + out
    total = total.astype(BF)
    place = 0
    for out in outs:
        out[...] = total[place : place + out.shape[0]]
        place += out.shape[0]


def run_experts(arrays, ids, weights, after, name):
    count = len(arrays)
    inner, width = weights[1].shape
    rows = sum(a.shape[0] for a in arrays)
    return pl.pallas_call(
        functools.partial(expert_kernel, count),
        out_shape=tuple(pltpu.VMEM((a.shape[0], width), BF) for a in arrays),
        in_specs=[smem()] + [vmem()] * (count + 4) + [anywhere()],
        out_specs=tuple(vmem() for _ in arrays),
        compiler_params=pltpu.CompilerParams(vmem_limit_bytes=24 * MIB),
        cost_estimate=pl.CostEstimate(
            flops=2 * rows * 6 * inner * width,
            bytes_accessed=4 * rows * width + 12 * inner * width,
            transcendentals=rows * 2 * inner,
        ),
        name=name,
    )(ids, *arrays, *(pin(w) for w in weights), after)


def join_kernel(*refs):
    *ins, _after, out = refs
    place = 0
    for part in ins:
        out[place : place + part.shape[0], :] = part[...]
        place += part.shape[0]


def join(arrays, after):
    rows = sum(a.shape[0] for a in arrays)
    return pl.pallas_call(
        join_kernel,
        out_shape=jax.ShapeDtypeStruct((rows, arrays[0].shape[1]), arrays[0].dtype),
        in_specs=[vmem()] * len(arrays) + [anywhere()],
        out_specs=vmem(),
        compiler_params=pltpu.CompilerParams(vmem_limit_bytes=16 * MIB),
        cost_estimate=pl.CostEstimate(flops=0, bytes_accessed=2 * MIB, transcendentals=0),
        name="join",
    )(*arrays, after)


def add_kernel(a, b, c, d, _after, first, second):
    first[...] = (a[...].astype(F32) + b[...].astype(F32)).astype(BF)
    second[...] = (c[...].astype(F32) + d[...].astype(F32)).astype(BF)


def add_two(a, b, c, d, after):
    shape = jax.ShapeDtypeStruct(a.shape, BF)
    return pl.pallas_call(
        add_kernel,
        out_shape=(shape,) * 2,
        in_specs=[vmem()] * 4 + [anywhere()],
        out_specs=(vmem(),) * 2,
        compiler_params=pltpu.CompilerParams(vmem_limit_bytes=16 * MIB),
        cost_estimate=pl.CostEstimate(flops=2**18, bytes_accessed=2 * MIB, transcendentals=0),
        name="add_far",
    )(a, b, c, d, after)


def merge_kernel(hidden, own_t, t1, t2, own_b, b1, b2, _after, kept, *outs):
    size = hidden.shape[0]
    for k in range(1 + len(outs)):
        group = (own_t, t1, t2) if k < 2 else (own_b, b1, b2)
        place = slice(k % 2 * size, (k % 2 + 1) * size)
        total = sum(part[place, :].astype(F32) for part in group)
        if k == 0:
            kept[...] = hidden[...] + total
        else:
            outs[k - 1][...] = total.astype(BF)


def merge(hidden, upper, lower, after):
    size, width = hidden.shape
    return pl.pallas_call(
        merge_kernel,
        out_shape=(jax.ShapeDtypeStruct(hidden.shape, F32),)
        + (jax.ShapeDtypeStruct((size, width), BF),) * 3,
        in_specs=[vmem()] * 7 + [anywhere()],
        out_specs=(vmem(),) * 4,
        compiler_params=pltpu.CompilerParams(vmem_limit_bytes=16 * MIB),
        cost_estimate=pl.CostEstimate(flops=2**20, bytes_accessed=4 * MIB, transcendentals=0),
        name="merge",
    )(hidden, *upper, *lower, after)


def finish_kernel(kept, *refs):
    *parts, out = refs
    total = kept[...]
    for part in parts:
        total = total + part[...].astype(F32)
    out[...] = total.astype(BF)


def finish(kept, parts):
    return pl.pallas_call(
        finish_kernel,
        out_shape=jax.ShapeDtypeStruct(kept.shape, BF),
        in_specs=[vmem()] * (1 + len(parts)),
        out_specs=vmem(),
        compiler_params=pltpu.CompilerParams(vmem_limit_bytes=16 * MIB),
        cost_estimate=pl.CostEstimate(flops=2**19, bytes_accessed=2 * MIB, transcendentals=0),
        name="finish",
    )(kept, *parts)


def wave_kernel(
    window, first, owners, near, far, table_hbm, taps_hbm, bias_hbm, _after, out, done, table, taps, bias, rows_of, laid, sems
):
    part, channels = table.shape[0], bias.shape[1]
    lanes = near.shape[1]
    tap_count = taps.shape[0]
    frames_out = window - tap_count + 1
    dialogs = laid.shape[0] // frames_out
    copies = [
        pltpu.make_async_copy(taps_hbm, taps, sems.at[0]),
        pltpu.make_async_copy(bias_hbm, bias, sems.at[1]),
    ]
    for q in range(2):
        copies.append(
            pltpu.make_async_copy(
                table_hbm.at[pl.ds(q * part, part)],
                table.at[:, pl.ds(q * channels, channels)],
                sems.at[2 + q],
            )
        )
    for copy in copies:
        copy.start()
    for q, codes in enumerate((near, far)):
        square = jnp.concatenate(
            [codes[...].astype(F32), jnp.zeros((lanes - codes.shape[0], lanes), F32)], axis=0
        )
        rows_of[q * lanes : (q + 1) * lanes, :] = jnp.transpose(square).astype(jnp.int32)
    for copy in copies:
        copy.wait()
    entry = lax.broadcasted_iota(jnp.int32, (dialogs, part), 1)

    def one_block(k, carry):
        block = rows_of[pl.ds(pl.multiple_of(k * dialogs, dialogs), dialogs), :]
        count = block[:, window : window + 1]
        hot, upper = [], []
        for p in range(window):
            code = block[:, p : p + 1]
            upper.append(code >= part)
            code = jnp.where(code >= part, code - part, code)
            code = jnp.where(p < count + tap_count - 1, code, -1)
            hot.append((entry == code).astype(F32).astype(BF))
        found = dot_n(jnp.concatenate(hot, axis=0), table[...])
        frames = []
        for p in range(window):
            rows = found[p * dialogs : (p + 1) * dialogs]
            frames.append(jnp.where(upper[p], rows[:, channels:], rows[:, :channels]))
        for t in range(frames_out):
            total = jnp.zeros((dialogs, channels), F32) + bias[...]
            for j in range(tap_count):
                total = total + taps[j : j + 1, :] * frames[t + j]
            laid[pl.ds(t, dialogs, stride=frames_out), :] = jnp.where(t < count, silu(total), 0.0)
        result = laid[...].astype(BF).reshape(dialogs, frames_out, channels)
        out[pl.ds(owners[first + k] * dialogs, dialogs)] = result
        return carry

    lax.fori_loop(0, rows_of.shape[0] // dialogs, one_block, 0)
    done[...] = jnp.zeros_like(done)


def wave(numbers, first, near, far, table, taps, bias, after, window, dialogs):
    lanes = near.shape[1]
    entries, channels = table.shape
    frames_out = window - taps.shape[0] + 1
    rows = 2 * lanes
    return pl.pallas_call(
        functools.partial(wave_kernel, window, first),
        out_shape=(
            jax.ShapeDtypeStruct((rows, frames_out, channels), BF),
            jax.ShapeDtypeStruct((8, 128), F32),
        ),
        in_specs=[smem()] + [vmem()] * 2 + [anywhere()] * 4,
        out_specs=(vmem(), vmem()),
        scratch_shapes=[
            pltpu.VMEM((entries // 2, 2 * channels), BF),
            pltpu.VMEM(taps.shape, F32),
            pltpu.VMEM(bias.shape, F32),
            pltpu.VMEM((rows, lanes), jnp.int32),
            pltpu.VMEM((dialogs * frames_out, channels), F32),
            pltpu.SemaphoreType.DMA((4,)),
        ],
        compiler_params=pltpu.CompilerParams(vmem_limit_bytes=16 * MIB),
        cost_estimate=pl.CostEstimate(
            flops=2 * rows * window * entries * channels,
            bytes_accessed=2 * MIB,
            transcendentals=rows * frames_out * channels,
        ),
        name="wave",
    )(numbers, near, far, stay(table), stay(taps), stay(bias), after)


def expert_grid():
    chips = lax.axis_size("expert") // 2
    side = math.isqrt(chips)
    return side, chips // side


def swap_cores(array):
    return lax.ppermute(array, "expert", [(i, i ^ 1) for i in range(lax.axis_size("expert"))])


def move(array, stage, distance):
    nx, ny = expert_grid()
    route = []
    for x in range(nx):
        for y in range(ny):
            for core in range(2):
                if core == stage:
                    target = (x + distance) % nx * ny + y
                else:
                    target = x * ny + (y + distance) % ny
                route.append(((x * ny + y) * 2 + core, target * 2 + core))
    return lax.ppermute(array, "expert", route)


def along(array, distance):
    size = lax.axis_size("section")
    return lax.ppermute(array, "section", [(i, (i + distance) % size) for i in range(size)])


def shards(
    thinker_rows,
    codec_prev,
    w_text,
    attn_gain,
    w_q,
    key_value_weight,
    q_gain,
    k_gain,
    w_o,
    cache_k,
    value_cache,
    lengths,
    moe_gain,
    router,
    routes,
    w_gate_up,
    w_down,
    codes,
    counts,
    code_table,
    conv_weight,
    conv_bias,
):
    dialogs, steps, _ = thinker_rows.shape
    context = cache_k.shape[1]
    rows = dialogs * steps
    width = codec_prev.shape[2]
    handed = along(jnp.transpose(thinker_rows, (1, 0, 2)), 1)
    gu_a, down_a = w_gate_up[0], w_down[0]
    gu_b, down_b = swap_cores(gu_a), swap_cores(down_a)
    mine = lax.axis_index("expert").astype(jnp.int32)
    picks = jnp.transpose(routes, (2, 1, 0)).reshape(routes.shape[2], rows)
    live = (jnp.arange(context)[None, :] < lengths[:, None]).astype(F32)
    window = codes.shape[1]
    held = jnp.concatenate(
        [codes.T, counts[None], jnp.zeros((15 - window, dialogs), jnp.int32)], axis=0
    )
    held = (held, along(held, 1), along(held, -1), along(held, -2))
    sections = lax.axis_size("section")
    place = lax.axis_index("section").astype(jnp.int32)
    numbers = [mine, mine + 1 - 2 * (mine % 2), jnp.int32(router.shape[1])]
    numbers += [(place + shift) % sections for shift in (0, 7, 1, 2, 4, 3, 5, 6)]
    numbers = jnp.stack(numbers)
    hidden, sent = dense(
        handed,
        picks,
        live.reshape(1, dialogs * context),
        (
            attn_gain[None],
            q_gain[None],
            k_gain[None],
            moe_gain[None],
            jnp.transpose(router),
            jnp.transpose(codec_prev, (1, 0, 2)),
        ),
        (w_text, w_q, key_value_weight, w_o),
        [c.reshape(dialogs * context, c.shape[2]) for c in (cache_k, value_cache)],
        (held[3], held[2], held[1], numbers),
    )
    sent_m, sent_x, sent_p = move(sent, 0, 1), move(sent, 0, 2), move(sent, 0, -1)
    *expert_weights, held = stage((stay(gu_a), stay(down_a), gu_b, down_b), held, (sent,))
    upper = join((sent, sent_m), sent)
    upper_m, upper_p = move(upper, 1, 1), move(upper, 1, -1)
    lower = join((sent_x, sent_p), expert_weights[1])
    lower_m, lower_p = move(lower, 1, 1), move(lower, 1, -1)
    experts = functools.partial(run_experts, ids=numbers, weights=expert_weights)
    own_u, own_l = experts((upper, lower), after=lower, name="experts_own")
    upper_m, own_u = lax.optimization_barrier((upper_m, own_u))
    lower_p, own_l = lax.optimization_barrier((lower_p, own_l))
    far_u, far_l = move(upper_m, 1, 1), move(lower_p, 1, -1)
    from_um, from_up, from_lm, from_lp = experts(
        (upper_m, upper_p, lower_m, lower_p), after=own_u, name="experts_near"
    )
    from_fu, from_fl = experts((far_u, far_l), after=from_um, name="experts_far")
    back_up, back_lm = move(from_up, 1, 1), move(from_lm, 1, -1)
    back_fu, back_fl = move(from_fu, 1, -1), move(from_fl, 1, 1)
    held_far = along(held, 4)
    from_um, from_lp = add_two(from_um, back_fu, from_lp, back_fl, held_far)
    back_um, back_lp = move(from_um, 1, -1), move(from_lp, 1, 1)
    wave_feats, wave_done = wave(
        numbers, 3, held, held_far, code_table, conv_weight, conv_bias[None], from_um, window, dialogs
    )
    kept, *sums = merge(
        hidden, (own_u, back_um, back_up), (own_l, back_lm, back_lp), wave_done
    )
    out = finish(kept, (move(sums[1], 0, 2), move(sums[0], 0, -1), move(sums[2], 0, 1)))
    return (jnp.transpose(out.reshape(steps, dialogs, width), (1, 0, 2)), wave_feats)


def solution(mesh):
    each = P(("expert", "section"), None, None)
    return jax.shard_map(
        shards,
        mesh=mesh,
        in_specs=(
            each,
            each,
            P(),
            P(),
            P(),
            P(),
            P(),
            P(),
            P(),
            each,
            each,
            P(("expert", "section")),
            P(),
            P(),
            each,
            P("expert", None, None),
            P("expert", None, None),
            P(("expert", "section"), None),
            P(("expert", "section")),
            P(None, "section"),
            P(None, "section"),
            P("section"),
        ),
        out_specs=(each, P("expert", None, "section")),
        check_vma=False,
    )
```
